32 devices in a mesh: dp: 8 (over z, x), fsdp: 4 (over y, core).
Axes of the slice: x: 2, y: 2, z: 4, core: 2. Of those that a mesh axis runs over, the one named last changes fastest.
Arguments:
- tokens: bfloat16 [16384, 1024], P(('dp', 'fsdp')), may hold values from -6 to 6
- segment: int32 [32, 512], P(('dp', 'fsdp')), may hold values from -1 to 5, as said below
- cotangent: bfloat16 [16384, 1024], P(('dp', 'fsdp')), may hold values from -6 to 6
- query_w: float32 [1024, 1024], P(('dp', 'fsdp')), may hold values from -0.1875 to 0.1875
- key_w: float32 [1024, 1024], P(('dp', 'fsdp')), may hold values from -0.1875 to 0.1875
- value_w: float32 [1024, 1024], P(('dp', 'fsdp')), may hold values from -0.1875 to 0.1875
- attn_out_w: float32 [1024, 1024], P(('dp', 'fsdp')), may hold values from -0.75 to 0.75
- up_w: float32 [1024, 4096], P(('dp', 'fsdp')), may hold values from -0.1875 to 0.1875
- down_w: float32 [4096, 1024], P(None, ('dp', 'fsdp')), may hold values from -0.09375 to 0.09375
- query_bias: float32 [1024], P(('dp', 'fsdp')), may hold values from -3 to 3
- value_bias: float32 [1024], P(('dp', 'fsdp')), may hold values from -2 to 2
- attn_out_bias: float32 [1024], P(('dp', 'fsdp')), may hold values from -2 to 2
- up_bias: float32 [4096], P(('dp', 'fsdp')), may hold values from -2 to 2
- down_bias: float32 [1024], P(('dp', 'fsdp')), may hold values from -2 to 2
- norm1_gain: float32 [1024], P(('dp', 'fsdp')), may hold values from 0.5 to 1.5
- norm1_shift: float32 [1024], P(('dp', 'fsdp')), may hold values from -2 to 2
- norm2_gain: float32 [1024], P(('dp', 'fsdp')), may hold values from 0.5 to 1.5
- norm2_shift: float32 [1024], P(('dp', 'fsdp')), may hold values from -2 to 2
Outputs:
- outputs: bfloat16 [16384, 1024], P(('dp', 'fsdp'))
- d_tokens: float32 [16384, 1024], P(('dp', 'fsdp'))
- d_query_w: float32 [1024, 1024], P(('dp', 'fsdp'))
- d_key_w: float32 [1024, 1024], P(('dp', 'fsdp'))
- d_value_w: float32 [1024, 1024], P(('dp', 'fsdp'))
- d_attn_out_w: float32 [1024, 1024], P(('dp', 'fsdp'))
- d_up_w: float32 [1024, 4096], P(('dp', 'fsdp'))
- d_down_w: float32 [4096, 1024], P(None, ('dp', 'fsdp'))
- d_query_bias: float32 [1024], P(('dp', 'fsdp'))
- d_value_bias: float32 [1024], P(('dp', 'fsdp'))
- d_attn_out_bias: float32 [1024], P(('dp', 'fsdp'))
- d_up_bias: float32 [4096], P(('dp', 'fsdp'))
- d_down_bias: float32 [1024], P(('dp', 'fsdp'))
- d_norm1_gain: float32 [1024], P(('dp', 'fsdp'))
- d_norm1_shift: float32 [1024], P(('dp', 'fsdp'))
- d_norm2_gain: float32 [1024], P(('dp', 'fsdp'))
- d_norm2_shift: float32 [1024], P(('dp', 'fsdp'))
The draws below stay inside these ranges and needn't reach their ends.
Inputs may be any that keep to these rules, and one draw needn't show every extreme that they name: `segment`: within each row, ids start at 0 and never fall over its real tokens; padding tokens hold -1 and stand only at a row's end; every row has real tokens.
All inputs are finite; a program needn't handle non-finite values.
Results may differ from the reference program's by a relative error of at most 0.02.
Values may be sent and summed in bfloat16 or wider, within the bound.
A program may use at most 192 MiB of HBM per device.

```python
import jax
import jax.numpy as jnp
from jax import lax

D = 1024
HEADS = 16
HEAD = 64
FF = 4096
LEN = 512
ROWS_DEV = 1
ROWS = 32
TOKENS = 16384


most_cuts = 5


def draw_segment(key, part):
    key = jax.random.fold_in(key, 7)
    cut_key, count_key, pad_key = jax.random.split(key, 3)
    orders = jax.vmap(lambda row_key: jax.random.permutation(row_key, LEN - 1))(jax.random.split(cut_key, ROWS))
    cut_points = orders[:, :most_cuts] + 1
    cut_count = jax.random.randint(count_key, (ROWS, 1), 1, most_cuts + 1)
    first_row = jnp.arange(ROWS)[:, None] == 0
    cut_count = jnp.where(first_row, most_cuts, cut_count)
    ranks = jnp.arange(most_cuts)[None, :]
    cut_points = jnp.where(ranks < cut_count, cut_points, LEN)
    places = jnp.arange(LEN)
    segment_ids = jnp.sum((places[None, :, None] >= cut_points[:, None, :]).astype(jnp.int32), axis=-1)
    padding = jax.random.randint(pad_key, (ROWS, 1), 0, LEN // 8)
    padding = jnp.where(first_row, 0, padding)
    return jnp.where(places[None, :] >= LEN - padding, -1, segment_ids).astype(jnp.int32)


def spiked(values, key, source, target, parts, factor):
    owner, partner = [(jnp.arange(values.shape[axis_at]) // (values.shape[axis_at] // parts)).reshape([-1 if axis == axis_at else 1 for axis in range(values.ndim)]) for axis_at in (source, target)]
    chosen = jax.random.permutation(key, parts)[partner]
    strong = (owner == chosen) | (owner == (partner + parts // 2) % parts)
    return jnp.where(strong, factor * values, values)


def block_levels(key, shape, cuts, least, high):
    def one(dim, parts):
        draws = jax.random.uniform(jax.random.fold_in(jax.random.fold_in(key, 6), dim), (parts,), jnp.float32, least / len(cuts), high / len(cuts))
        return jnp.repeat(jnp.exp(draws), shape[dim] // parts).reshape((-1,) + (1,) * (len(shape) - dim - 1))

    gain = one(*cuts[0])
    for cut in cuts[1:]:
        gain = gain * one(*cut)
    return gain


def normal_values(rng, extent, width, reach, shards=(), dtype=jnp.bfloat16):
    loudness = block_levels(rng, extent, shards, -0.22, 0.18) if shards else 1.0
    values = jax.random.normal(rng, extent, jnp.float32) * width * loudness
    return jnp.minimum(jnp.maximum(values, -reach), reach).astype(dtype)


def bell_draw_with(key, shape, scale, limit, cuts, heavy, held_as=jnp.bfloat16):
    array = scale * jax.random.normal(key, shape, jnp.float32)
    if cuts:
        array = array * block_levels(key, shape, cuts, -0.22, 0.18)
    return jnp.clip(spiked(array, jax.random.fold_in(key, 3), *heavy), -limit, limit).astype(held_as)


def setup_inputs(seed: int = 0) -> dict:
    key_of = jax.random.split(jax.random.key(seed), 19)
    return {
        "tokens": bell_draw_with(key_of[0], (TOKENS, D), 1.0, 6.0, ((0, 32),), (0, 1, 32, 2.75)),
        "segment": draw_segment(jax.random.fold_in(key_of[18], 71), 0),
        "cotangent": bell_draw_with(key_of[2], (TOKENS, D), 1.0, 6.0, ((0, 32),), (0, 1, 32, 2.75)),
        "query_w": normal_values(key_of[3], (D, D), D ** -0.5, 0.1875, ((0, 32),), jnp.float32),
        "key_w": normal_values(key_of[4], (D, D), D ** -0.5, 0.1875, ((0, 32),), jnp.float32),
        "value_w": normal_values(key_of[5], (D, D), D ** -0.5, 0.1875, ((0, 32),), jnp.float32),
        "attn_out_w": normal_values(key_of[6], (D, D), (D // 16) ** -0.5, 0.75, ((0, 32),), jnp.float32),
        "up_w": normal_values(key_of[7], (D, FF), D ** -0.5, 0.1875, ((0, 32),), jnp.float32),
        "down_w": normal_values(key_of[8], (FF, D), FF ** -0.5, 0.09375, ((1, 32),), jnp.float32),
        "query_bias": normal_values(key_of[9], (D,), 0.5, 3.0, ((0, 32),), jnp.float32),
        "value_bias": normal_values(key_of[10], (D,), 0.3, 2.0, ((0, 32),), jnp.float32),
        "attn_out_bias": normal_values(key_of[11], (D,), 0.3, 2.0, ((0, 32),), jnp.float32),
        "up_bias": normal_values(key_of[12], (FF,), 0.3, 2.0, ((0, 32),), jnp.float32),
        "down_bias": normal_values(key_of[13], (D,), 0.3, 2.0, ((0, 32),), jnp.float32),
        "norm1_gain": jnp.clip(1.0 + 0.1 * jax.random.normal(key_of[14], (D,), jnp.float32), 0.5, 1.5),
        "norm1_shift": normal_values(key_of[15], (D,), 0.3, 2.0, ((0, 32),), jnp.float32),
        "norm2_gain": jnp.clip(1.0 + 0.1 * jax.random.normal(key_of[16], (D,), jnp.float32), 0.5, 1.5),
        "norm2_shift": normal_values(key_of[17], (D,), 0.3, 2.0, ((0, 32),), jnp.float32),
    }


@jax.custom_vjp
def low(v):
    return lax.optimization_barrier(v.astype(jnp.bfloat16)).astype(jnp.float32)

@jax.custom_vjp
def low_back(v):
    return v

def low_keep(v):
    return (low(v), None)

def low_pass(kept, grad):
    return (grad,)

def back_keep(v):
    return (v, None)

def back_low(kept, grad):
    return (low(grad),)
low.defvjp(low_keep, low_pass)
low_back.defvjp(back_keep, back_low)
norm_epsilon = 1e-12
masked_score = -1000000000.0

def matmul(left, right):
    return jnp.dot(left, right, precision=lax.Precision.HIGHEST, preferred_element_type=jnp.float32)

def normalize(values, gain_vec, shift_vec):
    center = values - lax.optimization_barrier(jnp.mean(values, axis=-1, keepdims=True))
    spread = lax.optimization_barrier(jnp.mean(jnp.square(center), axis=-1, keepdims=True))
    return center * lax.rsqrt(spread + norm_epsilon) * gain_vec + shift_vec

def gelu_exact(values):
    return jax.nn.gelu(values, approximate=False)

def attend_row(pieces):
    queries, key_rows, value_rows, labels = pieces
    scores = jnp.einsum('qhe,khe->hqk', queries, key_rows, precision=lax.Precision.HIGHEST) * 0.125
    allowed = labels[:, None] == labels[None, :]
    scores = low_back(jnp.where(allowed[None], scores, masked_score))
    row_max = lax.optimization_barrier(jnp.max(scores, axis=-1, keepdims=True))
    row_exp = jnp.exp(scores - row_max)
    attn_probs = low(row_exp / lax.optimization_barrier(jnp.sum(row_exp, axis=-1, keepdims=True)))
    return jnp.einsum('hqk,khe->qhe', attn_probs, value_rows, precision=lax.Precision.HIGHEST)

def forward(params, inputs, labels):
    rounded = [low(param) for param in params]
    wq_full, wk_full, wv_full, wo_full, w_up, w_down, bias_q, bias_v, bias_o, bias_up, bias_down, gain_one, shift_one, gain_two, shift_two = rounded
    queries = low(low_back(matmul(inputs, wq_full) + bias_q))
    key_rows = low(low_back(matmul(inputs, wk_full)))
    value_rows = low(low_back(matmul(inputs, wv_full) + bias_v))
    head_shape = (ROWS_DEV, LEN, HEADS, HEAD)
    context = lax.map(jax.checkpoint(attend_row), (queries.reshape(head_shape), key_rows.reshape(head_shape), value_rows.reshape(head_shape), labels))
    context = low(low_back(context.reshape(-1, D)))
    attended = low_back(matmul(context, wo_full) + bias_o)
    norm_mid = low(normalize(inputs + attended, gain_one, shift_one))
    pre_act = low_back(matmul(norm_mid, w_up) + bias_up)
    act_out = low(gelu_exact(pre_act))
    ffn_out = low_back(matmul(act_out, w_down) + bias_down)
    return normalize(norm_mid + ffn_out, gain_two, shift_two)

def reference(tokens, segment, cotangent, query_w, key_w, value_w, attn_out_w, up_w, down_w, query_bias, value_bias, attn_out_bias, up_bias, down_bias, norm1_gain, norm1_shift, norm2_gain, norm2_shift):
    params = (query_w, key_w, value_w, attn_out_w, up_w, down_w, query_bias, value_bias, attn_out_bias, up_bias, down_bias, norm1_gain, norm1_shift, norm2_gain, norm2_shift)
    block_rows = ROWS_DEV * LEN
    block_count = tokens.shape[0] // block_rows
    inputs = tokens.astype(jnp.float32).reshape(block_count, block_rows, D)
    labels = segment.reshape(block_count, ROWS_DEV, LEN)
    upstream = cotangent.astype(jnp.float32).reshape(block_count, block_rows, D)

    def step(totals, item):
        block_in, block_labels, block_cot = item
        valid = (block_labels.reshape(-1) >= 0).astype(jnp.float32)[:, None]
        result, pull = jax.vjp(lambda p, v: forward(p, v, block_labels), params, block_in)
        grad_params, grad_in = pull(block_cot * valid)
        totals = tuple((total + grad for total, grad in zip(totals, grad_params)))
        return (totals, (result.astype(jnp.bfloat16), grad_in))
    zeros = tuple((jnp.zeros(param.shape, jnp.float32) for param in params))
    totals, (results, grads_in) = lax.scan(step, zeros, (inputs, labels, upstream))
    return (results.reshape(-1, D), grads_in.reshape(-1, D), totals[0], totals[1], totals[2], totals[3], totals[4], totals[5], totals[6], totals[7], totals[8], totals[9], totals[10], totals[11], totals[12], totals[13], totals[14])
```

```python
import functools

import jax
import jax.numpy as jnp
from jax import lax
from jax.experimental import pallas as pl
from jax.experimental.pallas import tpu as pltpu
from jax.sharding import PartitionSpec as P

MESH = pl.DeviceIdType.MESH
BLOCKS = 12


def place():
    dp = lax.axis_index("dp")
    fs = lax.axis_index("fsdp")
    return dp // 2, dp % 2, fs // 2, fs % 2


def device(z, x, y, c):
    return (z * 2 + x, y * 2 + c)


def greet(depth):
    z, x, y, c = place()
    peers = [device(z, x, y, 1 - c), device(z, 1 - x, y, c), device(z, x, 1 - y, c)]
    peers += [device((z + k) % depth, x, y, c) for k in range(1, depth)]
    bar = pltpu.get_barrier_semaphore()
    for peer in peers:
        pl.semaphore_signal(bar, inc=1, device_id=peer, device_id_type=MESH)
    pl.semaphore_wait(bar, len(peers))


def send(src, dst, ssem, rsem, peer):
    return pltpu.make_async_remote_copy(
        src_ref=src, dst_ref=dst, send_sem=ssem, recv_sem=rsem, device_id=peer, device_id_type=MESH
    )


class GatherBlock:
    def __init__(self, full, mine, ss, rs, depth):
        self.full, self.ss, self.rs, self.depth = full, ss, rs, depth
        self.mine = mine
        z, x, y, c = self.at = place()
        self.xn, self.yn, self.cn = device(z, 1 - x, y, c), device(z, x, 1 - y, c), device(z, x, y, 1 - c)
        half = depth // 2
        self.low, self.high = pl.ds(0, half), pl.ds(half, depth - half)

    def moves(self):
        z, x, y, c = self.at
        full, ss, rs = self.full, self.ss, self.rs
        every = pl.ds(0, self.depth)
        out = {}
        own = full.at[z, x, y, c]
        for k in range(1, self.depth):
            out["col", k] = send(own, own, ss.at[k - 1], rs.at[k - 1], device((z + k) % self.depth, x, y, c))
        base = self.depth - 1
        column = full.at[every, x, y, c]
        out["x"] = send(column, column, ss.at[base], rs.at[base], self.xn)
        out["y"] = send(column, column, ss.at[base + 1], rs.at[base + 1], self.yn)
        out["c0"] = send(column, column, ss.at[base + 2], rs.at[base + 2], self.cn)
        xcol = full.at[every, 1 - x, y, c]
        ycol = full.at[every, x, 1 - y, c]
        out["c1"] = send(xcol, xcol, ss.at[base + 3], rs.at[base + 3], self.cn)
        out["c2"] = send(ycol, ycol, ss.at[base + 4], rs.at[base + 4], self.cn)
        xlow = full.at[self.low, 1 - x, y, c]
        yhigh = full.at[self.high, x, 1 - y, c]
        out["dy"] = send(xlow, xlow, ss.at[base + 5], rs.at[base + 5], self.yn)
        out["dx"] = send(yhigh, yhigh, ss.at[base + 6], rs.at[base + 6], self.xn)
        dcol = full.at[every, 1 - x, 1 - y, c]
        out["c3"] = send(dcol, dcol, ss.at[base + 7], rs.at[base + 7], self.cn)
        return out

    def arrivals(self):
        z, x, y, c = self.at
        full, ss, rs = self.full, self.ss, self.rs
        every = pl.ds(0, self.depth)
        out = {}

        def got(ref, i):
            return send(ref, ref, ss.at[i], rs.at[i], self.cn)

        for k in range(1, self.depth):
            out["col", k] = got(full.at[(z + self.depth - k) % self.depth, x, y, c], k - 1)
        base = self.depth - 1
        out["x"] = got(full.at[every, 1 - x, y, c], base)
        out["y"] = got(full.at[every, x, 1 - y, c], base + 1)
        out["c0"] = got(full.at[every, x, y, 1 - c], base + 2)
        out["c1"] = got(full.at[every, 1 - x, y, 1 - c], base + 3)
        out["c2"] = got(full.at[every, x, 1 - y, 1 - c], base + 4)
        out["dy"] = got(full.at[self.low, 1 - x, 1 - y, c], base + 5)
        out["dx"] = got(full.at[self.high, 1 - x, 1 - y, c], base + 6)
        out["c3"] = got(full.at[every, 1 - x, 1 - y, 1 - c], base + 7)
        return out

    def stage(self, s):
        moves, arrivals = self.moves(), self.arrivals()
        if s == 0:
            z, x, y, c = self.at
            self.full[z, x, y, c] = self.mine[...]
            for k in range(1, self.depth):
                moves["col", k].start()
        if s == 1:
            for k in range(1, self.depth):
                arrivals["col", k].wait_recv()
            for name in ("x", "y", "c0"):
                moves[name].start()
        if s == 2:
            arrivals["x"].wait_recv()
            moves["dy"].start()
            moves["c1"].start()
            arrivals["y"].wait_recv()
            moves["dx"].start()
            moves["c2"].start()
        if s == 3:
            arrivals["dy"].wait_recv()
            arrivals["dx"].wait_recv()
            moves["c3"].start()
        if s == 4:
            for name in ("c0", "c1", "c2", "c3"):
                arrivals[name].wait_recv()
            for move in moves.values():
                move.wait_send()


def gather_kernel(depth, shard_ref, vec_ref, wout_ref, vout_ref, full, vfull, ss, rs, osem):
    greet(depth)

    def block(b):
        return GatherBlock(full.at[b], shard_ref.at[b], ss.at[b], rs.at[b], depth)

    vec = GatherBlock(vfull, vec_ref, ss.at[BLOCKS], rs.at[BLOCKS], depth)
    for t in range(BLOCKS + 4):
        for s in range(5):
            b = t - s
            if 0 <= b < BLOCKS:
                block(b).stage(s)
                if s == 4:
                    pltpu.make_async_copy(full.at[b], wout_ref.at[b], osem.at[b]).start()
            if b == 1:
                vec.stage(s)
    vout_ref[...] = vfull[...]
    for b in range(BLOCKS):
        pltpu.make_async_copy(full.at[b], wout_ref.at[b], osem.at[b]).wait()


def gather_call(shard, vec, depth):
    rows, cols = shard.shape[1:]
    dims = (depth, 2, 2, 2)
    n = depth + 7
    return pl.pallas_call(
        functools.partial(gather_kernel, depth),
        out_shape=(
            jax.ShapeDtypeStruct((BLOCKS,) + dims + (rows, cols), jnp.bfloat16),
            jax.ShapeDtypeStruct(dims + vec.shape, jnp.bfloat16),
        ),
        in_specs=[pl.BlockSpec(memory_space=pltpu.VMEM)] * 2,
        out_specs=(pl.BlockSpec(memory_space=pl.ANY), pl.BlockSpec(memory_space=pltpu.VMEM)),
        scratch_shapes=[
            pltpu.VMEM((BLOCKS,) + dims + (rows, cols), jnp.bfloat16),
            pltpu.VMEM(dims + vec.shape, jnp.bfloat16),
            pltpu.SemaphoreType.DMA((BLOCKS + 1, n)),
            pltpu.SemaphoreType.DMA((BLOCKS + 1, n)),
            pltpu.SemaphoreType.DMA((BLOCKS,)),
        ],
        compiler_params=pltpu.CompilerParams(
            collective_id=0, has_side_effects=True, vmem_limit_bytes=56 * 2**20
        ),
        name="gather",
    )(shard, vec)


class SumBlock:
    def __init__(self, grad, r0, r1x, r1y, r2x, r2y, r3, ss, rs, depth):
        self.grad, self.r0, self.r1x, self.r1y, self.r2x, self.r2y, self.r3 = grad, r0, r1x, r1y, r2x, r2y, r3
        self.ss, self.rs, self.depth = ss, rs, depth
        self.at = place()

    def moves(self):
        z, x, y, c = self.at
        xn, yn, cn = device(z, 1 - x, y, c), device(z, x, 1 - y, c), device(z, x, y, 1 - c)
        g, ss, rs, depth = self.grad, self.ss, self.rs, self.depth
        half = depth // 2
        low, high, every = pl.ds(0, half), pl.ds(half, depth - half), pl.ds(0, depth)
        out = {}
        out["c"] = send(g.at[every, pl.ds(0, 2), pl.ds(0, 2), 1 - c], self.r0, ss.at[0], rs.at[0], cn)
        out["dx"] = send(g.at[low, 1 - x, 1 - y, c], self.r1x, ss.at[1], rs.at[1], xn)
        out["dy"] = send(g.at[high, 1 - x, 1 - y, c], self.r1y, ss.at[2], rs.at[2], yn)
        out["x"] = send(g.at[every, 1 - x, y, c], self.r2x, ss.at[3], rs.at[3], xn)
        out["y"] = send(g.at[every, x, 1 - y, c], self.r2y, ss.at[4], rs.at[4], yn)
        for k in range(1, depth):
            out["z", k] = send(
                g.at[(z + k) % depth, x, y, c], self.r3.at[k - 1], ss.at[4 + k], rs.at[4 + k],
                device((z + k) % depth, x, y, c),
            )
        return out

    def stage(self, s, out=None):
        m = self.moves()
        z, x, y, c = self.at
        g, depth = self.grad, self.depth
        half = depth // 2
        if s == 0:
            m["c"].start()
        if s == 1:
            m["c"].wait_recv()
            for xx, yy in ((1 - x, 1 - y), (1 - x, y), (x, 1 - y), (x, y)):
                for zz in range(depth):
                    g[zz, xx, yy, c] = g[zz, xx, yy, c] + self.r0[zz, xx, yy]
                if xx is not x and yy is not y:
                    m["dx"].start()
                    m["dy"].start()
        if s == 2:
            m["dx"].wait_recv()
            for zz in range(half):
                g[zz, x, 1 - y, c] = g[zz, x, 1 - y, c] + self.r1x[zz]
            m["y"].start()
            m["dy"].wait_recv()
            for zz in range(half, depth):
                g[zz, 1 - x, y, c] = g[zz, 1 - x, y, c] + self.r1y[zz - half]
            m["x"].start()
        if s == 3:
            m["x"].wait_recv()
            m["y"].wait_recv()
            for k in list(range(1, depth)) + [0]:
                zz = (z + k) % depth
                total = (
                    g[zz, x, y, c].astype(jnp.float32)
                    + self.r2x[zz].astype(jnp.float32)
                    + self.r2y[zz].astype(jnp.float32)
                )
                g[zz, x, y, c] = total.astype(jnp.bfloat16)
                if k:
                    m["z", k].start()
        if s == 4:
            total = g[z, x, y, c].astype(jnp.float32)
            for k in range(1, depth):
                m["z", k].wait_recv()
                total = total + self.r3[k - 1].astype(jnp.float32)
            out[...] = total
            for move in m.values():
                move.wait_send()


SLOTS = 6


def sum_scratch(depth, rows, cols, slots, n_sems):
    bf = jnp.bfloat16
    half = depth // 2
    return [
        pltpu.VMEM((slots, depth, 2, 2, 2, rows, cols), bf),
        pltpu.VMEM((slots, depth, 2, 2, rows, cols), bf),
        pltpu.VMEM((slots, half, rows, cols), bf),
        pltpu.VMEM((slots, depth - half, rows, cols), bf),
        pltpu.VMEM((slots, depth, rows, cols), bf),
        pltpu.VMEM((slots, depth, rows, cols), bf),
        pltpu.VMEM((slots, depth - 1, rows, cols), bf),
        pltpu.SemaphoreType.DMA((n_sems, depth + 4)),
        pltpu.SemaphoreType.DMA((n_sems, depth + 4)),
    ]


def sum_kernel(depth, grads_ref, vgrad_ref, out_ref, vout_ref, *scratch):
    big, vec, lsem = scratch[:9], scratch[9:18], scratch[18]
    greet(depth)

    def block(b):
        slot = b % SLOTS
        return SumBlock(*[r.at[slot] for r in big[:7]], big[7].at[b], big[8].at[b], depth)

    vblock = SumBlock(*[r.at[0] for r in vec[:7]], vec[7].at[0], vec[8].at[0], depth)

    def fetch(b):
        return pltpu.make_async_copy(grads_ref.at[b], big[0].at[b % SLOTS], lsem.at[b])

    vec[0][0] = vgrad_ref[...]
    fetch(0).start()
    for t in range(BLOCKS + 4):
        if t < BLOCKS:
            if t + 1 < BLOCKS:
                fetch(t + 1).start()
            fetch(t).wait()
        for s in range(5):
            b = t - s
            if 0 <= b < BLOCKS:
                block(b).stage(s, out_ref.at[b])
            if b == 1:
                vblock.stage(s, vout_ref)


def sum_call(grads, vgrad, depth):
    rows, cols = grads.shape[-2:]
    vrows, vcols = vgrad.shape[-2:]
    return pl.pallas_call(
        functools.partial(sum_kernel, depth),
        out_shape=(
            jax.ShapeDtypeStruct((BLOCKS, rows, cols), jnp.float32),
            jax.ShapeDtypeStruct((vrows, vcols), jnp.float32),
        ),
        in_specs=[pl.BlockSpec(memory_space=pl.ANY), pl.BlockSpec(memory_space=pltpu.VMEM)],
        out_specs=(pl.BlockSpec(memory_space=pltpu.VMEM),) * 2,
        scratch_shapes=sum_scratch(depth, rows, cols, SLOTS, BLOCKS)
        + sum_scratch(depth, vrows, vcols, 1, 1)
        + [pltpu.SemaphoreType.DMA((BLOCKS,))],
        compiler_params=pltpu.CompilerParams(
            collective_id=1, has_side_effects=True, vmem_limit_bytes=56 * 2**20
        ),
        name="sum_grads",
    )(grads, vgrad)


HEAD = 64


norm_epsilon = 1e-12
masked_score = -1000000000.0


def to_half(array):
    return array.astype(jnp.bfloat16)


def matmul(left, right):
    return jnp.dot(left, right, preferred_element_type=jnp.float32)


def matmul_nt(left, right):
    return lax.dot_general(
        left, right, (((1,), (1,)), ((), ())), preferred_element_type=jnp.float32
    )


def contract_rows(left, right):
    return lax.dot_general(
        left, right, (((0,), (0,)), ((), ())), preferred_element_type=jnp.float32
    )


def column_sums(array):
    return jnp.sum(array.astype(jnp.float32), axis=0)


def normalize(values, gain_vec, shift_vec):
    center = values - jnp.mean(values, axis=-1, keepdims=True)
    spread = jnp.mean(center * center, axis=-1, keepdims=True)
    return center * lax.rsqrt(spread + norm_epsilon) * gain_vec + shift_vec


def gelu_exact(values):
    return jax.nn.gelu(values, approximate=False)


def split_heads(block):
    return block.reshape(block.shape[0], -1, HEAD)


def row_scores(queries, key_rows, labels):
    scores = (
        jnp.einsum("qhe,khe->hqk", queries, key_rows, preferred_element_type=jnp.float32) * 0.125
    )
    allowed = labels[:, None] == labels[None, :]
    return jnp.where(allowed[None], scores, masked_score)


def attend_row(pieces):
    queries, key_rows, value_rows, labels = pieces
    scores = row_scores(split_heads(queries), split_heads(key_rows), labels)
    row_max = jnp.max(scores, axis=-1, keepdims=True)
    row_exp = jnp.exp(scores - row_max)
    row_total = jnp.sum(row_exp, axis=-1, keepdims=True)
    probs_half = to_half(row_exp / row_total)
    context = jnp.einsum(
        "hqk,khe->qhe", probs_half, split_heads(value_rows), preferred_element_type=jnp.float32
    )
    return (to_half(context.reshape(queries.shape)), (row_max + jnp.log(row_total))[..., 0])


def attend_back(pieces):
    queries, key_rows, value_rows, labels, log_total, d_context = pieces
    query_heads = split_heads(queries)
    key_heads = split_heads(key_rows)
    context_heads = split_heads(d_context)
    scores = row_scores(query_heads, key_heads, labels)
    attn_probs = jnp.exp(scores - log_total[..., None])
    d_probs = jnp.einsum(
        "qhe,khe->hqk", context_heads, split_heads(value_rows), preferred_element_type=jnp.float32
    )
    row_delta = jnp.sum(attn_probs * d_probs, axis=-1, keepdims=True)
    d_scores = to_half(attn_probs * (d_probs - row_delta))
    d_queries = (
        jnp.einsum("hqk,khe->qhe", d_scores, key_heads, preferred_element_type=jnp.float32) * 0.125
    )
    d_keys = (
        jnp.einsum("hqk,qhe->khe", d_scores, query_heads, preferred_element_type=jnp.float32)
        * 0.125
    )
    d_values = jnp.einsum(
        "hqk,qhe->khe", to_half(attn_probs), context_heads, preferred_element_type=jnp.float32
    )
    return (
        to_half(d_queries.reshape(queries.shape)),
        to_half(d_keys.reshape(queries.shape)),
        to_half(d_values.reshape(queries.shape)),
    )


def plain_device(
    tokens,
    segment,
    cotangent,
    query_w,
    key_w,
    value_w,
    attn_out_w,
    up_w,
    down_w,
    query_bias,
    value_bias,
    attn_out_bias,
    up_bias,
    down_bias,
    norm1_gain,
    norm1_shift,
    norm2_gain,
    norm2_shift,
):
    row_count = segment.shape[0]
    row_length = segment.shape[1]
    model_width = tokens.shape[1]

    def by_rows(array):
        return array.reshape(row_count, row_length, -1)

    attn_set = (
        lax.all_gather(to_half(query_w), ("dp", "fsdp"), axis=0, tiled=True),
        lax.all_gather(to_half(key_w), ("dp", "fsdp"), axis=0, tiled=True),
        lax.all_gather(to_half(value_w), ("dp", "fsdp"), axis=0, tiled=True),
        lax.all_gather(to_half(attn_out_w), ("dp", "fsdp"), axis=0, tiled=True),
        lax.all_gather(to_half(query_bias), ("dp", "fsdp"), axis=0, tiled=True),
        lax.all_gather(to_half(value_bias), ("dp", "fsdp"), axis=0, tiled=True),
        lax.all_gather(to_half(attn_out_bias), ("dp", "fsdp"), axis=0, tiled=True),
        lax.all_gather(to_half(norm1_gain), ("dp", "fsdp"), axis=0, tiled=True),
        lax.all_gather(to_half(norm1_shift), ("dp", "fsdp"), axis=0, tiled=True),
    )
    wq_full, wk_full, wv_full, wo_full, bias_q, bias_v, bias_o, gain_one, shift_one = attn_set
    ffn_set = (
        lax.all_gather(to_half(up_w), ("dp", "fsdp"), axis=0, tiled=True),
        lax.all_gather(to_half(down_w), ("dp", "fsdp"), axis=1, tiled=True),
        lax.all_gather(to_half(up_bias), ("dp", "fsdp"), axis=0, tiled=True),
        lax.all_gather(to_half(down_bias), ("dp", "fsdp"), axis=0, tiled=True),
        lax.all_gather(to_half(norm2_gain), ("dp", "fsdp"), axis=0, tiled=True),
        lax.all_gather(to_half(norm2_shift), ("dp", "fsdp"), axis=0, tiled=True),
    )
    w_up, w_down, bias_up, bias_down, gain_two, shift_two = ffn_set
    queries = to_half(matmul(tokens, wq_full) + bias_q.astype(jnp.float32))
    key_rows = to_half(matmul(tokens, wk_full))
    value_rows = to_half(matmul(tokens, wv_full) + bias_v.astype(jnp.float32))
    context, log_total = lax.map(
        attend_row, (by_rows(queries), by_rows(key_rows), by_rows(value_rows), segment)
    )
    context = context.reshape(-1, model_width)
    attended = matmul(context, wo_full) + bias_o.astype(jnp.float32)
    first_sum = tokens.astype(jnp.float32) + attended
    norm_mid, pull_one = jax.vjp(
        normalize, first_sum, gain_one.astype(jnp.float32), shift_one.astype(jnp.float32)
    )
    mid_half = to_half(norm_mid)
    pre_act = matmul(mid_half, w_up) + bias_up.astype(jnp.float32)
    act_out, pull_act = jax.vjp(gelu_exact, pre_act)
    act_half = to_half(act_out)
    ffn_out = matmul(act_half, w_down) + bias_down.astype(jnp.float32)
    second_sum = mid_half.astype(jnp.float32) + ffn_out
    final, pull_two = jax.vjp(
        normalize, second_sum, gain_two.astype(jnp.float32), shift_two.astype(jnp.float32)
    )
    outputs = to_half(final)
    valid = (segment.reshape(-1) >= 0).astype(jnp.float32)[:, None]
    d_out = cotangent.astype(jnp.float32) * valid
    d_second, d_gain_two, d_shift_two = pull_two(d_out)
    up_back, down_back = (
        lax.all_gather(to_half(up_w), ("dp", "fsdp"), axis=0, tiled=True),
        lax.all_gather(to_half(down_w), ("dp", "fsdp"), axis=1, tiled=True),
    )
    d_ffn = to_half(d_second)
    d_down_turned = contract_rows(d_ffn, act_half)
    d_down_bias = column_sums(d_ffn)
    (d_pre,) = pull_act(matmul_nt(d_ffn, down_back))
    d_pre_half = to_half(d_pre)
    d_up_w = contract_rows(mid_half, d_pre_half)
    d_up_bias = column_sums(d_pre_half)
    d_mid = d_second + matmul_nt(d_pre_half, up_back)
    d_first, d_gain_one, d_shift_one = pull_one(d_mid)
    wq_back, wk_back, wv_back, wo_back = (
        lax.all_gather(to_half(query_w), ("dp", "fsdp"), axis=0, tiled=True),
        lax.all_gather(to_half(key_w), ("dp", "fsdp"), axis=0, tiled=True),
        lax.all_gather(to_half(value_w), ("dp", "fsdp"), axis=0, tiled=True),
        lax.all_gather(to_half(attn_out_w), ("dp", "fsdp"), axis=0, tiled=True),
    )
    d_att = to_half(d_first)
    d_attn_out_w = contract_rows(context, d_att)
    d_attn_out_bias = column_sums(d_att)
    d_context = to_half(matmul_nt(d_att, wo_back))
    d_queries, d_keys, d_values = lax.map(
        attend_back,
        (
            by_rows(queries),
            by_rows(key_rows),
            by_rows(value_rows),
            segment,
            log_total,
            by_rows(d_context),
        ),
    )
    d_queries = d_queries.reshape(-1, model_width)
    d_keys = d_keys.reshape(-1, model_width)
    d_values = d_values.reshape(-1, model_width)
    d_query_w = contract_rows(tokens, d_queries)
    d_key_w = contract_rows(tokens, d_keys)
    d_value_w = contract_rows(tokens, d_values)
    d_query_bias = column_sums(d_queries)
    d_value_bias = column_sums(d_values)
    d_tokens = (
        d_first
        + matmul_nt(d_queries, wq_back)
        + matmul_nt(d_keys, wk_back)
        + matmul_nt(d_values, wv_back)
    )
    members = (
        d_query_w,
        d_key_w,
        d_value_w,
        d_attn_out_w,
        d_up_w,
        d_down_turned,
        d_query_bias,
        d_value_bias,
        d_attn_out_bias,
        d_up_bias,
        d_down_bias,
        d_gain_one,
        d_shift_one,
        d_gain_two,
        d_shift_two,
    )
    block_sums = (
        lax.psum_scatter(
            members[0].astype(jnp.bfloat16), "dp", scatter_dimension=0, tiled=True
        ).astype(jnp.float32),
        lax.psum_scatter(
            members[1].astype(jnp.bfloat16), "dp", scatter_dimension=0, tiled=True
        ).astype(jnp.float32),
        lax.psum_scatter(
            members[2].astype(jnp.bfloat16), "dp", scatter_dimension=0, tiled=True
        ).astype(jnp.float32),
        lax.psum_scatter(
            members[3].astype(jnp.bfloat16), "dp", scatter_dimension=0, tiled=True
        ).astype(jnp.float32),
        lax.psum_scatter(
            members[4].astype(jnp.bfloat16), "dp", scatter_dimension=0, tiled=True
        ).astype(jnp.float32),
        lax.psum_scatter(
            members[5].astype(jnp.bfloat16), "dp", scatter_dimension=0, tiled=True
        ).astype(jnp.float32),
        lax.psum_scatter(
            members[6].astype(jnp.bfloat16), "dp", scatter_dimension=0, tiled=True
        ).astype(jnp.float32),
        lax.psum_scatter(
            members[7].astype(jnp.bfloat16), "dp", scatter_dimension=0, tiled=True
        ).astype(jnp.float32),
        lax.psum_scatter(
            members[8].astype(jnp.bfloat16), "dp", scatter_dimension=0, tiled=True
        ).astype(jnp.float32),
        lax.psum_scatter(
            members[9].astype(jnp.bfloat16), "dp", scatter_dimension=0, tiled=True
        ).astype(jnp.float32),
        lax.psum_scatter(
            members[10].astype(jnp.bfloat16), "dp", scatter_dimension=0, tiled=True
        ).astype(jnp.float32),
        lax.psum_scatter(
            members[11].astype(jnp.bfloat16), "dp", scatter_dimension=0, tiled=True
        ).astype(jnp.float32),
        lax.psum_scatter(
            members[12].astype(jnp.bfloat16), "dp", scatter_dimension=0, tiled=True
        ).astype(jnp.float32),
        lax.psum_scatter(
            members[13].astype(jnp.bfloat16), "dp", scatter_dimension=0, tiled=True
        ).astype(jnp.float32),
        lax.psum_scatter(
            members[14].astype(jnp.bfloat16), "dp", scatter_dimension=0, tiled=True
        ).astype(jnp.float32),
    )
    every_shard = (
        lax.psum_scatter(
            block_sums[0].astype(jnp.bfloat16), "fsdp", scatter_dimension=0, tiled=True
        ).astype(jnp.float32),
        lax.psum_scatter(
            block_sums[1].astype(jnp.bfloat16), "fsdp", scatter_dimension=0, tiled=True
        ).astype(jnp.float32),
        lax.psum_scatter(
            block_sums[2].astype(jnp.bfloat16), "fsdp", scatter_dimension=0, tiled=True
        ).astype(jnp.float32),
        lax.psum_scatter(
            block_sums[3].astype(jnp.bfloat16), "fsdp", scatter_dimension=0, tiled=True
        ).astype(jnp.float32),
        lax.psum_scatter(
            block_sums[4].astype(jnp.bfloat16), "fsdp", scatter_dimension=0, tiled=True
        ).astype(jnp.float32),
        lax.psum_scatter(
            block_sums[5].astype(jnp.bfloat16), "fsdp", scatter_dimension=0, tiled=True
        ).astype(jnp.float32),
        lax.psum_scatter(
            block_sums[6].astype(jnp.bfloat16), "fsdp", scatter_dimension=0, tiled=True
        ).astype(jnp.float32),
        lax.psum_scatter(
            block_sums[7].astype(jnp.bfloat16), "fsdp", scatter_dimension=0, tiled=True
        ).astype(jnp.float32),
        lax.psum_scatter(
            block_sums[8].astype(jnp.bfloat16), "fsdp", scatter_dimension=0, tiled=True
        ).astype(jnp.float32),
        lax.psum_scatter(
            block_sums[9].astype(jnp.bfloat16), "fsdp", scatter_dimension=0, tiled=True
        ).astype(jnp.float32),
        lax.psum_scatter(
            block_sums[10].astype(jnp.bfloat16), "fsdp", scatter_dimension=0, tiled=True
        ).astype(jnp.float32),
        lax.psum_scatter(
            block_sums[11].astype(jnp.bfloat16), "fsdp", scatter_dimension=0, tiled=True
        ).astype(jnp.float32),
        lax.psum_scatter(
            block_sums[12].astype(jnp.bfloat16), "fsdp", scatter_dimension=0, tiled=True
        ).astype(jnp.float32),
        lax.psum_scatter(
            block_sums[13].astype(jnp.bfloat16), "fsdp", scatter_dimension=0, tiled=True
        ).astype(jnp.float32),
        lax.psum_scatter(
            block_sums[14].astype(jnp.bfloat16), "fsdp", scatter_dimension=0, tiled=True
        ).astype(jnp.float32),
    )
    (
        shard_qw,
        shard_kw,
        shard_vw,
        shard_ow,
        shard_uw,
        shard_turned,
        shard_qb,
        shard_vb,
        shard_ob,
        shard_ub,
        shard_db,
        shard_g1,
        shard_s1,
        shard_g2,
        shard_s2,
    ) = every_shard
    shard_dw = jnp.transpose(shard_turned)
    return (
        outputs,
        d_tokens,
        shard_qw,
        shard_kw,
        shard_vw,
        shard_ow,
        shard_uw,
        shard_dw,
        shard_qb,
        shard_vb,
        shard_ob,
        shard_ub,
        shard_db,
        shard_g1,
        shard_s1,
        shard_g2,
        shard_s2,
    )


def kernel_device(
    tokens, segment, cotangent, query_w, key_w, value_w, attn_out_w, up_w, down_w, query_bias, value_bias,
    attn_out_bias, up_bias, down_bias, norm1_gain, norm1_shift, norm2_gain, norm2_shift,
):
    row_count, row_length = segment.shape
    model_width = tokens.shape[1]
    depth = lax.axis_size("dp") // 2
    fs = lax.axis_index("fsdp")
    rows = query_w.shape[0]
    quarters = up_w.shape[1] // model_width

    def by_rows(array):
        return array.reshape(row_count, row_length, -1)

    def quarter(array):
        return [array[:, i * model_width : (i + 1) * model_width] for i in range(quarters)]

    down_turned = jnp.transpose(to_half(down_w))
    shard = jnp.stack(
        [to_half(w) for w in (query_w, key_w, value_w, attn_out_w)] + quarter(to_half(up_w)) + quarter(down_turned)
    )
    short = jnp.stack(
        [query_bias, value_bias, attn_out_bias, down_bias, norm1_gain, norm1_shift, norm2_gain, norm2_shift]
    )
    at_lane = jnp.arange(128)[None, :] // rows == fs
    short = jnp.where(at_lane, jnp.tile(short, (1, 128 // rows)), 0.0)
    at_row = jnp.arange(8)[:, None] == fs
    tile = to_half(jnp.concatenate([short, jnp.where(at_row, up_bias[None], 0.0)]))

    full, vectors = gather_call(shard, tile, depth)
    full = full.reshape(BLOCKS, model_width, model_width)
    vectors = vectors.reshape(2 * depth, 4, 16, 128).astype(jnp.float32).sum(axis=1)
    short_full = jnp.moveaxis(vectors[:, :8], 0, 1).reshape(8, model_width)
    bias_q, bias_v, bias_o, bias_down, gain_one, shift_one, gain_two, shift_two = short_full
    bias_up = vectors[:, 8:12].reshape(-1)
    wq_full, wk_full, wv_full, wo_full = [full[i] for i in range(4)]
    ups, downs = full[4:8], full[8:12]

    queries = to_half(matmul(tokens, wq_full) + bias_q)
    key_rows = to_half(matmul(tokens, wk_full))
    value_rows = to_half(matmul(tokens, wv_full) + bias_v)
    context, log_total = lax.map(
        attend_row, (by_rows(queries), by_rows(key_rows), by_rows(value_rows), segment)
    )
    context = context.reshape(-1, model_width)
    attended = matmul(context, wo_full) + bias_o
    first_sum = tokens.astype(jnp.float32) + attended
    norm_mid, pull_one = jax.vjp(normalize, first_sum, gain_one, shift_one)
    mid_half = to_half(norm_mid)
    pre_act = jnp.concatenate([matmul(mid_half, w) for w in ups], axis=1) + bias_up
    act_out, pull_act = jax.vjp(gelu_exact, pre_act)
    act_half = to_half(act_out)
    ffn_out = sum(matmul_nt(a, w) for a, w in zip(quarter(act_half), downs)) + bias_down
    second_sum = mid_half.astype(jnp.float32) + ffn_out
    final, pull_two = jax.vjp(normalize, second_sum, gain_two, shift_two)
    outputs = to_half(final)
    valid = (segment.reshape(-1) >= 0).astype(jnp.float32)[:, None]
    d_out = cotangent.astype(jnp.float32) * valid
    d_second, d_gain_two, d_shift_two = pull_two(d_out)
    d_ffn = to_half(d_second)
    d_down_turned = [contract_rows(d_ffn, a) for a in quarter(act_half)]
    d_down_bias = column_sums(d_ffn)
    (d_pre,) = pull_act(jnp.concatenate([matmul(d_ffn, w) for w in downs], axis=1))
    d_pre_half = to_half(d_pre)
    d_up_w = [contract_rows(mid_half, d) for d in quarter(d_pre_half)]
    d_up_bias = column_sums(d_pre_half)
    d_mid = d_second + sum(matmul_nt(d, w) for d, w in zip(quarter(d_pre_half), ups))
    d_first, d_gain_one, d_shift_one = pull_one(d_mid)
    d_att = to_half(d_first)
    d_attn_out_w = contract_rows(context, d_att)
    d_attn_out_bias = column_sums(d_att)
    d_context = to_half(matmul_nt(d_att, wo_full))
    d_queries, d_keys, d_values = lax.map(
        attend_back,
        (by_rows(queries), by_rows(key_rows), by_rows(value_rows), segment, log_total, by_rows(d_context)),
    )
    d_queries = d_queries.reshape(-1, model_width)
    d_keys = d_keys.reshape(-1, model_width)
    d_values = d_values.reshape(-1, model_width)
    d_query_w = contract_rows(tokens, d_queries)
    d_key_w = contract_rows(tokens, d_keys)
    d_value_w = contract_rows(tokens, d_values)
    d_tokens = (
        d_first + matmul_nt(d_queries, wq_full) + matmul_nt(d_keys, wk_full) + matmul_nt(d_values, wv_full)
    )
    grads = [to_half(g) for g in d_down_turned + d_up_w + [d_attn_out_w, d_value_w, d_key_w, d_query_w]]
    grads = jnp.stack(grads).reshape(BLOCKS, depth, 2, 2, 2, rows, model_width)
    short_grads = jnp.stack(
        [
            column_sums(d_queries), column_sums(d_values), d_attn_out_bias, d_down_bias,
            d_gain_one, d_shift_one, d_gain_two, d_shift_two,
        ]
    )
    short_grads = jnp.moveaxis(short_grads.reshape(8, 2 * depth, 1, 128), 0, 2)
    short_grads = jnp.broadcast_to(short_grads, (2 * depth, 4, 8, 128))
    up_grads = d_up_bias.reshape(2 * depth, 4, 1, 128)
    up_grads = jnp.broadcast_to(up_grads, (2 * depth, 4, 8, 128))
    tiles = to_half(jnp.concatenate([short_grads, up_grads], axis=2)).reshape(depth, 2, 2, 2, 16, 128)
    sums, tile_sum = sum_call(grads, tiles, depth)
    short_sum = lax.dynamic_slice(tile_sum, (0, fs * rows), (8, rows))
    qb, vb, ob, db, g1, s1, g2, s2 = short_sum
    ub = tile_sum[8]
    dw = jnp.transpose(jnp.concatenate(list(sums[:4]), axis=1))
    uw = jnp.concatenate(list(sums[4:8]), axis=1)
    return (
        outputs, d_tokens, sums[11], sums[10], sums[9], sums[8], uw, dw, qb, vb, ob, ub, db, g1, s1, g2, s2,
    )


def solution(mesh):
    fits = mesh.shape["fsdp"] == 4 and mesh.shape["dp"] % 2 == 0 and 1024 // mesh.size == 32
    body = kernel_device if fits else plain_device
    in_specs = (
        P(("dp", "fsdp"), None),
        P(("dp", "fsdp"), None),
        P(("dp", "fsdp"), None),
        P(("dp", "fsdp"), None),
        P(("dp", "fsdp"), None),
        P(("dp", "fsdp"), None),
        P(("dp", "fsdp"), None),
        P(("dp", "fsdp"), None),
        P(None, ("dp", "fsdp")),
        P(("dp", "fsdp")),
        P(("dp", "fsdp")),
        P(("dp", "fsdp")),
        P(("dp", "fsdp")),
        P(("dp", "fsdp")),
        P(("dp", "fsdp")),
        P(("dp", "fsdp")),
        P(("dp", "fsdp")),
        P(("dp", "fsdp")),
    )
    out_specs = (
        P(("dp", "fsdp"), None),
        P(("dp", "fsdp"), None),
        P(("dp", "fsdp"), None),
        P(("dp", "fsdp"), None),
        P(("dp", "fsdp"), None),
        P(("dp", "fsdp"), None),
        P(("dp", "fsdp"), None),
        P(None, ("dp", "fsdp")),
        P(("dp", "fsdp")),
        P(("dp", "fsdp")),
        P(("dp", "fsdp")),
        P(("dp", "fsdp")),
        P(("dp", "fsdp")),
        P(("dp", "fsdp")),
        P(("dp", "fsdp")),
        P(("dp", "fsdp")),
        P(("dp", "fsdp")),
    )
    return jax.shard_map(
        body, mesh=mesh, in_specs=in_specs, out_specs=out_specs, check_vma=False
    )
```

```python
import functools

import jax
import jax.numpy as jnp
from jax import lax
from jax.experimental import pallas as pl
from jax.experimental.pallas import tpu as pltpu
from jax.sharding import PartitionSpec as P

MESH = pl.DeviceIdType.MESH
BLOCKS = 12


def place():
    dp = lax.axis_index("dp")
    fs = lax.axis_index("fsdp")
    return dp // 2, dp % 2, fs // 2, fs % 2


def device(z, x, y, c):
    return (z * 2 + x, y * 2 + c)


def greet(depth):
    z, x, y, c = place()
    peers = [device(z, x, y, 1 - c), device(z, 1 - x, y, c), device(z, x, 1 - y, c)]
    peers += [device((z + k) % depth, x, y, c) for k in range(1, depth)]
    bar = pltpu.get_barrier_semaphore()
    for peer in peers:
        pl.semaphore_signal(bar, inc=1, device_id=peer, device_id_type=MESH)
    pl.semaphore_wait(bar, len(peers))


def send(src, dst, ssem, rsem, peer):
    return pltpu.make_async_remote_copy(
        src_ref=src, dst_ref=dst, send_sem=ssem, recv_sem=rsem, device_id=peer, device_id_type=MESH
    )


class GatherBlock:
    def __init__(self, full, mine, ss, rs, depth):
        self.full, self.ss, self.rs, self.depth = full, ss, rs, depth
        self.mine = mine
        z, x, y, c = self.at = place()
        self.xn, self.yn, self.cn = device(z, 1 - x, y, c), device(z, x, 1 - y, c), device(z, x, y, 1 - c)
        half = depth // 2
        self.low, self.high = pl.ds(0, half), pl.ds(half, depth - half)

    def moves(self):
        z, x, y, c = self.at
        full, ss, rs = self.full, self.ss, self.rs
        every = pl.ds(0, self.depth)
        out = {}
        own = full.at[z, x, y, c]
        for k in range(1, self.depth):
            out["col", k] = send(own, own, ss.at[k - 1], rs.at[k - 1], device((z + k) % self.depth, x, y, c))
        base = self.depth - 1
        column = full.at[every, x, y, c]
        out["x"] = send(column, column, ss.at[base], rs.at[base], self.xn)
        out["y"] = send(column, column, ss.at[base + 1], rs.at[base + 1], self.yn)
        out["c0"] = send(column, column, ss.at[base + 2], rs.at[base + 2], self.cn)
        xcol = full.at[every, 1 - x, y, c]
        ycol = full.at[every, x, 1 - y, c]
        out["c1"] = send(xcol, xcol, ss.at[base + 3], rs.at[base + 3], self.cn)
        out["c2"] = send(ycol, ycol, ss.at[base + 4], rs.at[base + 4], self.cn)
        xlow = full.at[self.low, 1 - x, y, c]
        yhigh = full.at[self.high, x, 1 - y, c]
        out["dy"] = send(xlow, xlow, ss.at[base + 5], rs.at[base + 5], self.yn)
        out["dx"] = send(yhigh, yhigh, ss.at[base + 6], rs.at[base + 6], self.xn)
        dcol = full.at[every, 1 - x, 1 - y, c]
        out["c3"] = send(dcol, dcol, ss.at[base + 7], rs.at[base + 7], self.cn)
        return out

    def arrivals(self):
        z, x, y, c = self.at
        full, ss, rs = self.full, self.ss, self.rs
        every = pl.ds(0, self.depth)
        out = {}

        def got(ref, i):
            return send(ref, ref, ss.at[i], rs.at[i], self.cn)

        for k in range(1, self.depth):
            out["col", k] = got(full.at[(z + self.depth - k) % self.depth, x, y, c], k - 1)
        base = self.depth - 1
        out["x"] = got(full.at[every, 1 - x, y, c], base)
        out["y"] = got(full.at[every, x, 1 - y, c], base + 1)
        out["c0"] = got(full.at[every, x, y, 1 - c], base + 2)
        out["c1"] = got(full.at[every, 1 - x, y, 1 - c], base + 3)
        out["c2"] = got(full.at[every, x, 1 - y, 1 - c], base + 4)
        out["dy"] = got(full.at[self.low, 1 - x, 1 - y, c], base + 5)
        out["dx"] = got(full.at[self.high, 1 - x, 1 - y, c], base + 6)
        out["c3"] = got(full.at[every, 1 - x, 1 - y, 1 - c], base + 7)
        return out

    def stage(self, s):
        moves, arrivals = self.moves(), self.arrivals()
        if s == 0:
            z, x, y, c = self.at
            self.full[z, x, y, c] = self.mine()
            for k in range(1, self.depth):
                moves["col", k].start()
        if s == 1:
            for k in range(1, self.depth):
                arrivals["col", k].wait_recv()
            for name in ("x", "y", "c0"):
                moves[name].start()
        if s == 2:
            arrivals["x"].wait_recv()
            moves["dy"].start()
            moves["c1"].start()
            arrivals["y"].wait_recv()
            moves["dx"].start()
            moves["c2"].start()
        if s == 3:
            arrivals["dy"].wait_recv()
            arrivals["dx"].wait_recv()
            moves["c3"].start()
        if s == 4:
            for name in ("c0", "c1", "c2", "c3"):
                arrivals[name].wait_recv()
            for move in moves.values():
                move.wait_send()


HEAD = 64


norm_epsilon = 1e-12
masked_score = -1000000000.0


def to_half(array):
    return array.astype(jnp.bfloat16)


def matmul(left, right):
    return jnp.dot(left, right, preferred_element_type=jnp.float32)


def matmul_nt(left, right):
    return lax.dot_general(
        left, right, (((1,), (1,)), ((), ())), preferred_element_type=jnp.float32
    )


def contract_rows(left, right):
    return lax.dot_general(
        left, right, (((0,), (0,)), ((), ())), preferred_element_type=jnp.float32
    )


def column_sums(array):
    return jnp.sum(array.astype(jnp.float32), axis=0)


def normalize(values, gain_vec, shift_vec):
    center = values - jnp.mean(values, axis=-1, keepdims=True)
    spread = jnp.mean(center * center, axis=-1, keepdims=True)
    return center * lax.rsqrt(spread + norm_epsilon) * gain_vec + shift_vec


def gelu_exact(values):
    return jax.nn.gelu(values, approximate=False)


def split_heads(block):
    return block.reshape(block.shape[0], -1, HEAD)


def row_scores(queries, key_rows, labels):
    scores = (
        jnp.einsum("qhe,khe->hqk", queries, key_rows, preferred_element_type=jnp.float32) * 0.125
    )
    allowed = labels[:, None] == labels[None, :]
    return jnp.where(allowed[None], scores, masked_score)


def attend_row(pieces):
    queries, key_rows, value_rows, labels = pieces
    scores = row_scores(split_heads(queries), split_heads(key_rows), labels)
    row_max = jnp.max(scores, axis=-1, keepdims=True)
    row_exp = jnp.exp(scores - row_max)
    row_total = jnp.sum(row_exp, axis=-1, keepdims=True)
    probs_half = to_half(row_exp / row_total)
    context = jnp.einsum(
        "hqk,khe->qhe", probs_half, split_heads(value_rows), preferred_element_type=jnp.float32
    )
    return (to_half(context.reshape(queries.shape)), (row_max + jnp.log(row_total))[..., 0])


def attend_back(pieces):
    queries, key_rows, value_rows, labels, log_total, d_context = pieces
    query_heads = split_heads(queries)
    key_heads = split_heads(key_rows)
    context_heads = split_heads(d_context)
    scores = row_scores(query_heads, key_heads, labels)
    attn_probs = jnp.exp(scores - log_total[..., None])
    d_probs = jnp.einsum(
        "qhe,khe->hqk", context_heads, split_heads(value_rows), preferred_element_type=jnp.float32
    )
    row_delta = jnp.sum(attn_probs * d_probs, axis=-1, keepdims=True)
    d_scores = to_half(attn_probs * (d_probs - row_delta))
    d_queries = (
        jnp.einsum("hqk,khe->qhe", d_scores, key_heads, preferred_element_type=jnp.float32) * 0.125
    )
    d_keys = (
        jnp.einsum("hqk,qhe->khe", d_scores, query_heads, preferred_element_type=jnp.float32)
        * 0.125
    )
    d_values = jnp.einsum(
        "hqk,qhe->khe", to_half(attn_probs), context_heads, preferred_element_type=jnp.float32
    )
    return (
        to_half(d_queries.reshape(queries.shape)),
        to_half(d_keys.reshape(queries.shape)),
        to_half(d_values.reshape(queries.shape)),
    )


def plain_device(
    tokens,
    segment,
    cotangent,
    query_w,
    key_w,
    value_w,
    attn_out_w,
    up_w,
    down_w,
    query_bias,
    value_bias,
    attn_out_bias,
    up_bias,
    down_bias,
    norm1_gain,
    norm1_shift,
    norm2_gain,
    norm2_shift,
):
    row_count = segment.shape[0]
    row_length = segment.shape[1]
    model_width = tokens.shape[1]

    def by_rows(array):
        return array.reshape(row_count, row_length, -1)

    attn_set = (
        lax.all_gather(to_half(query_w), ("dp", "fsdp"), axis=0, tiled=True),
        lax.all_gather(to_half(key_w), ("dp", "fsdp"), axis=0, tiled=True),
        lax.all_gather(to_half(value_w), ("dp", "fsdp"), axis=0, tiled=True),
        lax.all_gather(to_half(attn_out_w), ("dp", "fsdp"), axis=0, tiled=True),
        lax.all_gather(to_half(query_bias), ("dp", "fsdp"), axis=0, tiled=True),
        lax.all_gather(to_half(value_bias), ("dp", "fsdp"), axis=0, tiled=True),
        lax.all_gather(to_half(attn_out_bias), ("dp", "fsdp"), axis=0, tiled=True),
        lax.all_gather(to_half(norm1_gain), ("dp", "fsdp"), axis=0, tiled=True),
        lax.all_gather(to_half(norm1_shift), ("dp", "fsdp"), axis=0, tiled=True),
    )
    wq_full, wk_full, wv_full, wo_full, bias_q, bias_v, bias_o, gain_one, shift_one = attn_set
    ffn_set = (
        lax.all_gather(to_half(up_w), ("dp", "fsdp"), axis=0, tiled=True),
        lax.all_gather(to_half(down_w), ("dp", "fsdp"), axis=1, tiled=True),
        lax.all_gather(to_half(up_bias), ("dp", "fsdp"), axis=0, tiled=True),
        lax.all_gather(to_half(down_bias), ("dp", "fsdp"), axis=0, tiled=True),
        lax.all_gather(to_half(norm2_gain), ("dp", "fsdp"), axis=0, tiled=True),
        lax.all_gather(to_half(norm2_shift), ("dp", "fsdp"), axis=0, tiled=True),
    )
    w_up, w_down, bias_up, bias_down, gain_two, shift_two = ffn_set
    queries = to_half(matmul(tokens, wq_full) + bias_q.astype(jnp.float32))
    key_rows = to_half(matmul(tokens, wk_full))
    value_rows = to_half(matmul(tokens, wv_full) + bias_v.astype(jnp.float32))
    context, log_total = lax.map(
        attend_row, (by_rows(queries), by_rows(key_rows), by_rows(value_rows), segment)
    )
    context = context.reshape(-1, model_width)
    attended = matmul(context, wo_full) + bias_o.astype(jnp.float32)
    first_sum = tokens.astype(jnp.float32) + attended
    norm_mid, pull_one = jax.vjp(
        normalize, first_sum, gain_one.astype(jnp.float32), shift_one.astype(jnp.float32)
    )
    mid_half = to_half(norm_mid)
    pre_act = matmul(mid_half, w_up) + bias_up.astype(jnp.float32)
    act_out, pull_act = jax.vjp(gelu_exact, pre_act)
    act_half = to_half(act_out)
    ffn_out = matmul(act_half, w_down) + bias_down.astype(jnp.float32)
    second_sum = mid_half.astype(jnp.float32) + ffn_out
    final, pull_two = jax.vjp(
        normalize, second_sum, gain_two.astype(jnp.float32), shift_two.astype(jnp.float32)
    )
    outputs = to_half(final)
    valid = (segment.reshape(-1) >= 0).astype(jnp.float32)[:, None]
    d_out = cotangent.astype(jnp.float32) * valid
    d_second, d_gain_two, d_shift_two = pull_two(d_out)
    up_back, down_back = (
        lax.all_gather(to_half(up_w), ("dp", "fsdp"), axis=0, tiled=True),
        lax.all_gather(to_half(down_w), ("dp", "fsdp"), axis=1, tiled=True),
    )
    d_ffn = to_half(d_second)
    d_down_turned = contract_rows(d_ffn, act_half)
    d_down_bias = column_sums(d_ffn)
    (d_pre,) = pull_act(matmul_nt(d_ffn, down_back))
    d_pre_half = to_half(d_pre)
    d_up_w = contract_rows(mid_half, d_pre_half)
    d_up_bias = column_sums(d_pre_half)
    d_mid = d_second + matmul_nt(d_pre_half, up_back)
    d_first, d_gain_one, d_shift_one = pull_one(d_mid)
    wq_back, wk_back, wv_back, wo_back = (
        lax.all_gather(to_half(query_w), ("dp", "fsdp"), axis=0, tiled=True),
        lax.all_gather(to_half(key_w), ("dp", "fsdp"), axis=0, tiled=True),
        lax.all_gather(to_half(value_w), ("dp", "fsdp"), axis=0, tiled=True),
        lax.all_gather(to_half(attn_out_w), ("dp", "fsdp"), axis=0, tiled=True),
    )
    d_att = to_half(d_first)
    d_attn_out_w = contract_rows(context, d_att)
    d_attn_out_bias = column_sums(d_att)
    d_context = to_half(matmul_nt(d_att, wo_back))
    d_queries, d_keys, d_values = lax.map(
        attend_back,
        (
            by_rows(queries),
            by_rows(key_rows),
            by_rows(value_rows),
            segment,
            log_total,
            by_rows(d_context),
        ),
    )
    d_queries = d_queries.reshape(-1, model_width)
    d_keys = d_keys.reshape(-1, model_width)
    d_values = d_values.reshape(-1, model_width)
    d_query_w = contract_rows(tokens, d_queries)
    d_key_w = contract_rows(tokens, d_keys)
    d_value_w = contract_rows(tokens, d_values)
    d_query_bias = column_sums(d_queries)
    d_value_bias = column_sums(d_values)
    d_tokens = (
        d_first
        + matmul_nt(d_queries, wq_back)
        + matmul_nt(d_keys, wk_back)
        + matmul_nt(d_values, wv_back)
    )
    members = (
        d_query_w,
        d_key_w,
        d_value_w,
        d_attn_out_w,
        d_up_w,
        d_down_turned,
        d_query_bias,
        d_value_bias,
        d_attn_out_bias,
        d_up_bias,
        d_down_bias,
        d_gain_one,
        d_shift_one,
        d_gain_two,
        d_shift_two,
    )
    block_sums = (
        lax.psum_scatter(
            members[0].astype(jnp.bfloat16), "dp", scatter_dimension=0, tiled=True
        ).astype(jnp.float32),
        lax.psum_scatter(
            members[1].astype(jnp.bfloat16), "dp", scatter_dimension=0, tiled=True
        ).astype(jnp.float32),
        lax.psum_scatter(
            members[2].astype(jnp.bfloat16), "dp", scatter_dimension=0, tiled=True
        ).astype(jnp.float32),
        lax.psum_scatter(
            members[3].astype(jnp.bfloat16), "dp", scatter_dimension=0, tiled=True
        ).astype(jnp.float32),
        lax.psum_scatter(
            members[4].astype(jnp.bfloat16), "dp", scatter_dimension=0, tiled=True
        ).astype(jnp.float32),
        lax.psum_scatter(
            members[5].astype(jnp.bfloat16), "dp", scatter_dimension=0, tiled=True
        ).astype(jnp.float32),
        lax.psum_scatter(
            members[6].astype(jnp.bfloat16), "dp", scatter_dimension=0, tiled=True
        ).astype(jnp.float32),
        lax.psum_scatter(
            members[7].astype(jnp.bfloat16), "dp", scatter_dimension=0, tiled=True
        ).astype(jnp.float32),
        lax.psum_scatter(
            members[8].astype(jnp.bfloat16), "dp", scatter_dimension=0, tiled=True
        ).astype(jnp.float32),
        lax.psum_scatter(
            members[9].astype(jnp.bfloat16), "dp", scatter_dimension=0, tiled=True
        ).astype(jnp.float32),
        lax.psum_scatter(
            members[10].astype(jnp.bfloat16), "dp", scatter_dimension=0, tiled=True
        ).astype(jnp.float32),
        lax.psum_scatter(
            members[11].astype(jnp.bfloat16), "dp", scatter_dimension=0, tiled=True
        ).astype(jnp.float32),
        lax.psum_scatter(
            members[12].astype(jnp.bfloat16), "dp", scatter_dimension=0, tiled=True
        ).astype(jnp.float32),
        lax.psum_scatter(
            members[13].astype(jnp.bfloat16), "dp", scatter_dimension=0, tiled=True
        ).astype(jnp.float32),
        lax.psum_scatter(
            members[14].astype(jnp.bfloat16), "dp", scatter_dimension=0, tiled=True
        ).astype(jnp.float32),
    )
    every_shard = (
        lax.psum_scatter(
            block_sums[0].astype(jnp.bfloat16), "fsdp", scatter_dimension=0, tiled=True
        ).astype(jnp.float32),
        lax.psum_scatter(
            block_sums[1].astype(jnp.bfloat16), "fsdp", scatter_dimension=0, tiled=True
        ).astype(jnp.float32),
        lax.psum_scatter(
            block_sums[2].astype(jnp.bfloat16), "fsdp", scatter_dimension=0, tiled=True
        ).astype(jnp.float32),
        lax.psum_scatter(
            block_sums[3].astype(jnp.bfloat16), "fsdp", scatter_dimension=0, tiled=True
        ).astype(jnp.float32),
        lax.psum_scatter(
            block_sums[4].astype(jnp.bfloat16), "fsdp", scatter_dimension=0, tiled=True
        ).astype(jnp.float32),
        lax.psum_scatter(
            block_sums[5].astype(jnp.bfloat16), "fsdp", scatter_dimension=0, tiled=True
        ).astype(jnp.float32),
        lax.psum_scatter(
            block_sums[6].astype(jnp.bfloat16), "fsdp", scatter_dimension=0, tiled=True
        ).astype(jnp.float32),
        lax.psum_scatter(
            block_sums[7].astype(jnp.bfloat16), "fsdp", scatter_dimension=0, tiled=True
        ).astype(jnp.float32),
        lax.psum_scatter(
            block_sums[8].astype(jnp.bfloat16), "fsdp", scatter_dimension=0, tiled=True
        ).astype(jnp.float32),
        lax.psum_scatter(
            block_sums[9].astype(jnp.bfloat16), "fsdp", scatter_dimension=0, tiled=True
        ).astype(jnp.float32),
        lax.psum_scatter(
            block_sums[10].astype(jnp.bfloat16), "fsdp", scatter_dimension=0, tiled=True
        ).astype(jnp.float32),
        lax.psum_scatter(
            block_sums[11].astype(jnp.bfloat16), "fsdp", scatter_dimension=0, tiled=True
        ).astype(jnp.float32),
        lax.psum_scatter(
            block_sums[12].astype(jnp.bfloat16), "fsdp", scatter_dimension=0, tiled=True
        ).astype(jnp.float32),
        lax.psum_scatter(
            block_sums[13].astype(jnp.bfloat16), "fsdp", scatter_dimension=0, tiled=True
        ).astype(jnp.float32),
        lax.psum_scatter(
            block_sums[14].astype(jnp.bfloat16), "fsdp", scatter_dimension=0, tiled=True
        ).astype(jnp.float32),
    )
    (
        shard_qw,
        shard_kw,
        shard_vw,
        shard_ow,
        shard_uw,
        shard_turned,
        shard_qb,
        shard_vb,
        shard_ob,
        shard_ub,
        shard_db,
        shard_g1,
        shard_s1,
        shard_g2,
        shard_s2,
    ) = every_shard
    shard_dw = jnp.transpose(shard_turned)
    return (
        outputs,
        d_tokens,
        shard_qw,
        shard_kw,
        shard_vw,
        shard_ow,
        shard_uw,
        shard_dw,
        shard_qb,
        shard_vb,
        shard_ob,
        shard_ub,
        shard_db,
        shard_g1,
        shard_s1,
        shard_g2,
        shard_s2,
    )


ATTN = 4
LANES = 128
SIDE = 256


def aligned(start, size, step=None):
    return pl.ds(pl.multiple_of(start, step or size), size)


def side_loop(count, body):
    def step(i, carry):
        body(i)
        return carry

    lax.fori_loop(0, count, step, 0)


def square(full, b):
    size = full.shape[-1]
    return full.at[b].reshape(size, size)


def spread_vectors(tiles, short_ref, up_ref, depth):
    for dp in range(2 * depth):
        total = jnp.zeros((16, LANES), jnp.float32)
        for fs in range(4):
            total = total + tiles[dp // 2, dp % 2, fs // 2, fs % 2].astype(jnp.float32)
        short_ref[:, dp * LANES : (dp + 1) * LANES] = total[:8]
        for fs in range(4):
            at = (dp * 4 + fs) * LANES
            up_ref[:, at : at + LANES] = total[8 + fs : 9 + fs]


def project(x_ref, weight, out_ref, bias=None, scale=None):
    def step(n):
        cols = aligned(n * SIDE, SIDE)
        got = matmul(x_ref[...], weight[:, cols])
        if bias is not None:
            got = got + bias[:, cols]
        got = to_half(got)
        if scale is not None:
            got = got * scale
        out_ref[:, cols] = got

    side_loop(weight.shape[1] // SIDE, step)


def attend_pairs(first, last, qkvc, lse, mask):
    length = mask.shape[0]

    def pair(p):
        lanes = aligned(p * LANES, LANES)
        q, k, v = qkvc[0, :, lanes], qkvc[1, :, lanes], qkvc[2, :, lanes]
        lane = lax.broadcasted_iota(jnp.int32, (length, LANES), 1)
        lower = lane < HEAD
        total = jnp.zeros((length, LANES), jnp.float32)
        logs = lse[...]
        for h in range(2):
            here = lower if h == 0 else jnp.logical_not(lower)
            key = jnp.where(here, k, jnp.zeros_like(k))
            scores = matmul_nt(q, key) + mask[...]
            row_max = jnp.max(scores, axis=-1, keepdims=True)
            row_exp = jnp.exp(scores - row_max)
            row_total = jnp.sum(row_exp, axis=-1, keepdims=True)
            part = matmul(to_half(row_exp), v) / row_total
            total = jnp.where(here, part, total)
            logs = jnp.where(lane == 2 * p + h, row_max + jnp.log(row_total), logs)
        qkvc[3, :, lanes] = to_half(total)
        lse[...] = logs

    def step(i, carry):
        pair(i)
        return carry

    lax.fori_loop(first, last, step, 0)


def forward_kernel(
    depth, tokens, segment, cotangent, wq, wk, wv, wo, up_w, down_w, short_in, up_in,
    out_hbm, full_hbm, qkvc_hbm, lse_hbm, mid_hbm, act_hbm, dge_hbm, nhat_hbm, rstd_hbm, dsec_hbm, small_hbm,
    full, tiles, mine_vec, short, up_bias, qkvc, lse, lse_turned, mask, mid, act, dge, nhat, rstd, total, final,
    small, ss, rs, osem, wsem,
):
    length, width = tokens.shape
    z, x, y, c = place()
    fs = y * 2 + c
    rows = wq.shape[0]
    greet(depth)

    mine_vec[...] = jnp.zeros_like(mine_vec)
    mine_vec[0:8, 0:rows] = short_in[...]
    placed = pltpu.roll(mine_vec[...], fs * rows, 1)
    row_at = lax.broadcasted_iota(jnp.int32, (16, LANES), 0)
    mine_vec[...] = jnp.where(row_at == 8 + fs, jnp.broadcast_to(up_in[...], (16, LANES)), placed)

    def own(b):
        if b < ATTN:
            return to_half((wq, wk, wv, wo)[b][...])
        if b < 2 * ATTN:
            at = (b - ATTN) * width
            return to_half(up_w[:, at : at + width])
        at = (b - 2 * ATTN) * width
        return to_half(down_w[:, at : at + width])

    def block(b):
        return GatherBlock(full.at[b], lambda: own(b), ss.at[b], rs.at[b], depth)

    vec = GatherBlock(tiles, lambda: to_half(mine_vec[...]), ss.at[BLOCKS], rs.at[BLOCKS], depth)

    def keep(b):
        return pltpu.make_async_copy(full.at[b], full_hbm.at[b], wsem.at[b])

    flushed = []

    def flush(src, dst):
        copy = pltpu.make_async_copy(src, dst, osem.at[len(flushed)])
        copy.start()
        flushed.append(copy)

    def pump(t):
        for s in range(5):
            b = t - s
            if 0 <= b < BLOCKS:
                block(b).stage(s)
                if s == 4:
                    keep(b).start()
            if b == 0:
                vec.stage(s)

    pump(0)
    pump(1)
    labels = segment[...].astype(jnp.float32)
    turned = jnp.transpose(jnp.broadcast_to(labels, (LANES, length)))
    mask[...] = jnp.where(turned[:, :1] == labels, 0.0, masked_score)
    valid = jnp.where(turned[:, :1] >= 0.0, 1.0, 0.0)
    lse[...] = jnp.zeros_like(lse)
    pump(2)
    pump(3)
    pump(4)
    spread_vectors(tiles, short, up_bias, depth)
    project(tokens, square(full, 0), qkvc.at[0], short.at[0:1], 0.125)
    pump(5)
    project(tokens, square(full, 1), qkvc.at[1])
    pump(6)
    project(tokens, square(full, 2), qkvc.at[2], short.at[1:2])
    attend_pairs(0, 4, qkvc, lse, mask)
    pump(7)
    attend_pairs(4, 8, qkvc, lse, mask)
    flush(qkvc, qkvc_hbm)
    lse_turned[...] = jnp.transpose(lse[...])
    flush(lse_turned, lse_hbm)
    pump(8)

    wo_full = square(full, 3)

    def attended(n):
        cols = aligned(n * SIDE, SIDE)
        total[:, cols] = (
            matmul(qkvc[3], wo_full[:, cols]) + short[2:3, cols] + tokens[:, cols].astype(jnp.float32)
        )

    side_loop(width // SIDE, attended)

    def first_norm(i):
        at = aligned(i * LANES, LANES)
        values = total[at, :]
        center = values - jnp.mean(values, axis=-1, keepdims=True)
        spread = jnp.mean(center * center, axis=-1, keepdims=True)
        r = lax.rsqrt(spread + norm_epsilon)
        unit = center * r
        nhat[at, :] = unit
        rstd[at, :] = jnp.broadcast_to(r, (LANES, LANES))
        mid[at, :] = to_half(unit * short[4:5, :] + short[5:6, :])

    side_loop(length // LANES, first_norm)
    flush(nhat, nhat_hbm)
    flush(rstd, rstd_hbm)
    flush(mid, mid_hbm)

    def activate(j):
        weight = square(full, ATTN + j)

        def step(n):
            cols = aligned(n * SIDE, SIDE)
            pre = matmul(mid[...], weight[:, cols]) + up_bias[:, aligned(j * width + n * SIDE, SIDE)]
            cdf = 0.5 * (1.0 + lax.erf(pre * 0.7071067811865476))
            act[j, :, cols] = to_half(pre * cdf)
            pdf = jnp.exp(-0.5 * pre * pre) * 0.3989422804014327
            dge[j, :, cols] = to_half(cdf + pre * pdf)

        side_loop(width // SIDE, step)
        flush(act.at[j], act_hbm.at[j])
        flush(dge.at[j], dge_hbm.at[j])

    def contract(j):
        weight = square(full, 2 * ATTN + j)

        def step(n):
            cols = aligned(n * SIDE, SIDE)
            got = matmul_nt(act[j], weight[cols, :])
            if j == 0:
                total[:, cols] = got + short[3:4, cols] + mid[:, cols].astype(jnp.float32)
            else:
                total[:, cols] = total[:, cols] + got

        side_loop(width // SIDE, step)

    for j in range(ATTN):
        activate(j)
        pump(9 + j)
    for j in range(ATTN):
        contract(j)
        if j < ATTN - 1:
            pump(13 + j)

    small[...] = jnp.zeros_like(small)
    small[0:1, :] = short[4:5, :]

    def second_norm(i):
        at = aligned(i * LANES, LANES)
        values = total[at, :]
        center = values - jnp.mean(values, axis=-1, keepdims=True)
        spread = jnp.mean(center * center, axis=-1, keepdims=True)
        r = lax.rsqrt(spread + norm_epsilon)
        unit = center * r
        gain = short[6:7, :]
        final[at, :] = to_half(unit * gain + short[7:8, :])
        e = cotangent[at, :].astype(jnp.float32) * lse[at, 0:1]
        small[1:2, :] = small[1:2, :] + jnp.sum(e * unit, axis=0, keepdims=True)
        small[2:3, :] = small[2:3, :] + jnp.sum(e, axis=0, keepdims=True)
        eg = e * gain
        d = r * (
            eg - jnp.mean(eg, axis=-1, keepdims=True) - unit * jnp.mean(eg * unit, axis=-1, keepdims=True)
        )
        total[at, :] = d
        small[3:4, :] = small[3:4, :] + jnp.sum(to_half(d).astype(jnp.float32), axis=0, keepdims=True)

    lse[...] = jnp.broadcast_to(valid, lse.shape)
    side_loop(length // LANES, second_norm)
    flush(final, out_hbm)
    flush(total, dsec_hbm)
    flush(small, small_hbm)
    for copy in flushed:
        copy.wait()
    for b in range(BLOCKS):
        keep(b).wait()


def forward_call(depth, tokens, segment, cotangent, wq, wk, wv, wo, up_w, down_turned, short, up_bias):
    length, width = tokens.shape
    rows = wq.shape[0]
    dims = (depth, 2, 2, 2)
    bf, f32 = jnp.bfloat16, jnp.float32
    shapes = [
        ((length, width), bf),
        ((BLOCKS,) + dims + (rows, width), bf),
        ((4, length, width), bf),
        ((LANES, length), f32),
        ((length, width), bf),
        ((ATTN, length, width), bf),
        ((ATTN, length, width), bf),
        ((length, width), f32),
        ((length, LANES), f32),
        ((length, width), f32),
        ((8, width), f32),
    ]
    n = depth + 7
    scratch = [
        pltpu.VMEM((BLOCKS,) + dims + (rows, width), bf),
        pltpu.VMEM(dims + (16, LANES), bf),
        pltpu.VMEM((16, LANES), f32),
        pltpu.VMEM((8, width), f32),
        pltpu.VMEM((1, ATTN * width), f32),
        pltpu.VMEM((4, length, width), bf),
        pltpu.VMEM((length, LANES), f32),
        pltpu.VMEM((LANES, length), f32),
        pltpu.VMEM((length, length), f32),
        pltpu.VMEM((length, width), bf),
        pltpu.VMEM((ATTN, length, width), bf),
        pltpu.VMEM((ATTN, length, width), bf),
        pltpu.VMEM((length, width), f32),
        pltpu.VMEM((length, LANES), f32),
        pltpu.VMEM((length, width), f32),
        pltpu.VMEM((length, width), bf),
        pltpu.VMEM((8, width), f32),
        pltpu.SemaphoreType.DMA((BLOCKS + 1, n)),
        pltpu.SemaphoreType.DMA((BLOCKS + 1, n)),
        pltpu.SemaphoreType.DMA((16,)),
        pltpu.SemaphoreType.DMA((BLOCKS,)),
    ]
    return pl.pallas_call(
        functools.partial(forward_kernel, depth),
        out_shape=tuple(jax.ShapeDtypeStruct(*s) for s in shapes),
        in_specs=[pl.BlockSpec(memory_space=pltpu.VMEM)] * 11,
        out_specs=tuple(pl.BlockSpec(memory_space=pl.ANY) for _ in shapes),
        scratch_shapes=scratch,
        compiler_params=pltpu.CompilerParams(
            collective_id=0, has_side_effects=True, vmem_limit_bytes=60 * 2**20
        ),
        name="forward",
    )(tokens, segment, cotangent, wq, wk, wv, wo, up_w, down_turned, short, up_bias)


class SumBlock:
    def __init__(self, grad, held, r0, r1x, r1y, r2x, r2y, r3, ss, rs, depth):
        self.grad, self.held = grad, held
        self.r0, self.r1x, self.r1y, self.r2x, self.r2y, self.r3 = r0, r1x, r1y, r2x, r2y, r3
        self.ss, self.rs, self.depth = ss, rs, depth
        self.at = place()

    def move(self, name, k=0):
        z, x, y, c = self.at
        xn, yn = device(z, 1 - x, y, c), device(z, x, 1 - y, c)
        g, h, ss, rs, depth = self.grad, self.held, self.ss, self.rs, self.depth
        half = depth // 2
        low, high, every, both = pl.ds(0, half), pl.ds(half, depth - half), pl.ds(0, depth), pl.ds(0, 2)
        if name == "c":
            return send(g.at[every, both, both, 1 - c], self.r0, ss.at[0], rs.at[0], device(z, x, y, 1 - c))
        if name == "dx":
            return send(h.at[low, 1 - x, 1 - y], self.r1x, ss.at[1], rs.at[1], xn)
        if name == "dy":
            return send(h.at[high, 1 - x, 1 - y], self.r1y, ss.at[2], rs.at[2], yn)
        if name == "x":
            return send(h.at[every, 1 - x, y], self.r2x, ss.at[3], rs.at[3], xn)
        if name == "y":
            return send(h.at[every, x, 1 - y], self.r2y, ss.at[4], rs.at[4], yn)
        there = (z + k) % depth
        return send(h.at[there, x, y], self.r3.at[k - 1], ss.at[4 + k], rs.at[4 + k], device(there, x, y, c))

    def stage(self, s, out=None):
        z, x, y, c = self.at
        g, h, depth = self.grad, self.held, self.depth
        half = depth // 2
        if s == 0:
            self.move("c").start()
        if s == 1:
            self.move("c").wait()
            for zz in range(depth):
                h[zz, 1 - x, 1 - y] = g[zz, 1 - x, 1 - y, c] + self.r0[zz, 1 - x, 1 - y]
            self.move("dx").start()
            self.move("dy").start()
            for xx, yy in ((1 - x, y), (x, 1 - y), (x, y)):
                for zz in range(depth):
                    h[zz, xx, yy] = g[zz, xx, yy, c] + self.r0[zz, xx, yy]
        if s == 2:
            self.move("dx").wait_recv()
            self.move("dy").wait_recv()
            for zz in range(half):
                h[zz, x, 1 - y] = h[zz, x, 1 - y] + self.r1x[zz]
            self.move("y").start()
            for zz in range(half, depth):
                h[zz, 1 - x, y] = h[zz, 1 - x, y] + self.r1y[zz - half]
            self.move("x").start()
        if s == 3:
            self.move("x").wait_recv()
            self.move("y").wait_recv()
            for k in list(range(1, depth)) + [0]:
                zz = (z + k) % depth
                total = (
                    h[zz, x, y].astype(jnp.float32)
                    + self.r2x[zz].astype(jnp.float32)
                    + self.r2y[zz].astype(jnp.float32)
                )
                h[zz, x, y] = total.astype(jnp.bfloat16)
                if k:
                    self.move("z", k).start()
        if s == 4:
            total = h[z, x, y].astype(jnp.float32)
            for k in range(1, depth):
                self.move("z", k).wait_recv()
                total = total + self.r3[k - 1].astype(jnp.float32)
            out[...] = total
            for name in ("dx", "dy", "x", "y"):
                self.move(name).wait_send()
            for k in range(1, depth):
                self.move("z", k).wait_send()


SLOTS = (2, 4, 2, 4, 4, 4, 4, 4)


def sum_scratch(depth, rows, cols, slots, blocks):
    bf = jnp.bfloat16
    half = depth // 2
    shapes = [
        (depth, 2, 2, 2), (depth, 2, 2), (depth, 2, 2), (half,), (depth - half,), (depth,), (depth,), (depth - 1,),
    ]
    return [pltpu.VMEM((n,) + s + (rows, cols), bf) for n, s in zip(slots, shapes)] + [
        pltpu.SemaphoreType.DMA((blocks, depth + 4)),
        pltpu.SemaphoreType.DMA((blocks, depth + 4)),
    ]


def attend_back_pairs(first, last, qkvc, lse, delta, mask, grads):
    length = mask.shape[0]

    def pair(p, carry):
        lanes = aligned(p * LANES, LANES)
        q, k, v, d_context = qkvc[0, :, lanes], qkvc[1, :, lanes], qkvc[2, :, lanes], grads[3, :, lanes]
        lower = lax.broadcasted_iota(jnp.int32, (length, LANES), 1) < HEAD
        sums = [jnp.zeros((length, LANES), jnp.float32) for _ in range(3)]
        for h in range(2):
            here = lower if h == 0 else jnp.logical_not(lower)
            row = pl.ds(2 * p + h, 1)
            key = jnp.where(here, k, jnp.zeros_like(k))
            value = jnp.where(here, v, jnp.zeros_like(v))
            probs = jnp.exp(matmul_nt(key, q) + mask[...] - lse[row, :])
            d_scores = to_half(probs * (matmul_nt(value, d_context) - delta[row, :]))
            parts = (
                contract_rows(d_scores, k) * 0.125,
                matmul(d_scores, q),
                matmul(to_half(probs), d_context),
            )
            sums = [jnp.where(here, part, total) for part, total in zip(parts, sums)]
        for i in range(3):
            grads[i, :, lanes] = to_half(sums[i])
        return carry

    lax.fori_loop(first, last, pair, 0)


WEIGHT_SLOTS = 6
WEIGHT_ORDER = (8, 4, 9, 5, 10, 6, 11, 7, 3, 2, 1, 0)


def backward_kernel(
    depth, tokens_hbm, segment, full_hbm, qkvc_hbm, lse_hbm, mid_hbm, act_hbm, dge_hbm, nhat_hbm, rstd_hbm,
    dsec_hbm, small,
    dtok_hbm, gq, gk, gv, go, gup, gdown, gshort, gup_bias,
    tokens, qkvc, lse, mid, act, dge, nhat, rstd, total, half, turn_a, turn_b, mask, delta, delta_turned, weights,
    short, up_bias, tile_sum, *rest,
):
    big, vec, (isem, wsem, osem) = rest[:10], rest[10:20], rest[20:]
    length, width = tokens.shape
    rows = gq.shape[0]
    z, x, y, c = place()
    fs = y * 2 + c
    f32 = jnp.float32

    loads = {}
    for name, src, dst in (
        ("dsec", dsec_hbm, total),
        ("act0", act_hbm.at[0], act.at[0]),
        ("w0", None, None),
        ("dge0", dge_hbm.at[0], dge.at[0]),
        ("w1", None, None),
        ("act1", act_hbm.at[1], act.at[1]),
        ("w2", None, None),
        ("dge1", dge_hbm.at[1], dge.at[1]),
        ("w3", None, None),
        ("act2", act_hbm.at[2], act.at[2]),
        ("w4", None, None),
        ("dge2", dge_hbm.at[2], dge.at[2]),
        ("w5", None, None),
        ("act3", act_hbm.at[3], act.at[3]),
        ("dge3", dge_hbm.at[3], dge.at[3]),
        ("mid", mid_hbm, mid),
        ("nhat", nhat_hbm, nhat),
        ("rstd", rstd_hbm, rstd),
        ("qkvc", qkvc_hbm, qkvc),
        ("lse", lse_hbm, lse),
        ("tokens", tokens_hbm, tokens),
    ):
        if src is None:
            i = int(name[1:])
            loads[name] = pltpu.make_async_copy(full_hbm.at[WEIGHT_ORDER[i]], weights.at[i], wsem.at[i])
        else:
            loads[name] = pltpu.make_async_copy(src, dst, isem.at[len(loads)])
        loads[name].start()

    def weight(i):
        loads["w%d" % i].wait()
        return square(weights, i % WEIGHT_SLOTS)

    def refill(i):
        n = i + WEIGHT_SLOTS
        if n < BLOCKS:
            loads["w%d" % n] = pltpu.make_async_copy(
                full_hbm.at[WEIGHT_ORDER[n]], weights.at[i % WEIGHT_SLOTS], wsem.at[n]
            )
            loads["w%d" % n].start()

    greet(depth)

    outs = [gdown.at[:, i * width : (i + 1) * width] for i in range(4)]
    outs += [gup.at[:, i * width : (i + 1) * width] for i in range(4)] + [go, gv, gk, gq]

    def block(b):
        return SumBlock(
            *[ref.at[b % n] for ref, n in zip(big[:8], SLOTS)], big[8].at[b], big[9].at[b], depth
        )

    vblock = SumBlock(*[ref.at[0] for ref in vec[:8]], vec[8].at[0], vec[9].at[0], depth)

    def pump(t):
        for s in (1, 0, 2, 3, 4):
            b = t - s
            if 0 <= b < BLOCKS:
                block(b).stage(s, outs[b])
            if b == BLOCKS - 1:
                vblock.stage(s, tile_sum)

    def weight_grad(b, left, right):
        part = width // depth

        def step(zz):
            got = to_half(matmul(left[aligned(zz * part, part), :], right[...]))
            big[0][b % SLOTS[0], zz] = got.reshape(2, 2, 2, rows, width)

        side_loop(depth, step)

    def sums_of(ref, cols):
        return jnp.sum(ref.astype(f32), axis=0, keepdims=True)

    loads["dsec"].wait()
    half[...] = to_half(total[...])
    turn_a[...] = jnp.transpose(half[...])
    loads["act0"].wait()
    weight_grad(0, turn_a, act.at[0])
    pump(0)

    labels = segment[...].astype(f32)
    turned = jnp.transpose(jnp.broadcast_to(labels, (LANES, length)))
    mask[...] = jnp.where(turned[:, :1] == labels, 0.0, masked_score)
    short[...] = jnp.zeros_like(short)
    short[3:4, :] = small[3:4, :]
    short[6:7, :] = small[1:2, :]
    short[7:8, :] = small[2:3, :]

    def into_units(j):
        w = weight(2 * j)
        loads["dge%d" % j].wait()

        def step(n):
            cols = aligned(n * SIDE, SIDE)
            d_pre = to_half(matmul(half[...], w[:, cols]) * dge[j, :, cols].astype(f32))
            dge[j, :, cols] = d_pre
            up_bias[:, aligned(j * width + n * SIDE, SIDE)] = sums_of(d_pre, cols)

        side_loop(width // SIDE, step)
        refill(2 * j)

    def add_product(left, w, cols):
        total[:, cols] = total[:, cols] + matmul_nt(left[...], w[cols, :])

    def out_of_units(j):
        w = weight(2 * j + 1)

        side_loop(width // SIDE, lambda n: add_product(dge.at[j], w, aligned(n * SIDE, SIDE)))
        refill(2 * j + 1)

    for j in range(4):
        into_units(j)
        out_of_units(j)
        if j < 3:
            loads["act%d" % (j + 1)].wait()
            weight_grad(j + 1, turn_a, act.at[j + 1])
            pump(j + 1)

    loads["mid"].wait()
    turn_b[...] = jnp.transpose(mid[...])
    weight_grad(4, turn_b, dge.at[0])
    pump(4)

    loads["nhat"].wait()
    loads["rstd"].wait()

    def first_norm(i):
        at = aligned(i * LANES, LANES)
        e = total[at, :]
        unit = nhat[at, :]
        short[4:5, :] = short[4:5, :] + jnp.sum(e * unit, axis=0, keepdims=True)
        short[5:6, :] = short[5:6, :] + jnp.sum(e, axis=0, keepdims=True)
        eg = e * small[0:1, :]
        d = rstd[at, 0:1] * (
            eg - jnp.mean(eg, axis=-1, keepdims=True) - unit * jnp.mean(eg * unit, axis=-1, keepdims=True)
        )
        total[at, :] = d
        d_half = to_half(d)
        half[at, :] = d_half
        short[2:3, :] = short[2:3, :] + jnp.sum(d_half.astype(f32), axis=0, keepdims=True)

    side_loop(length // LANES, first_norm)
    loads["qkvc"].wait()
    loads["lse"].wait()
    wo = weight(8)
    delta[...] = jnp.zeros_like(delta)

    def context_back(n):
        cols = aligned(n * SIDE, SIDE)
        d_context = to_half(matmul_nt(half[...], wo[cols, :]))
        act[3, :, cols] = d_context
        product = d_context.astype(f32) * qkvc[3, :, cols].astype(f32)
        lane = lax.broadcasted_iota(jnp.int32, (length, LANES), 1)
        got = delta[...]
        for i in range(SIDE // HEAD):
            two = product[:, (i // 2) * LANES : (i // 2 + 1) * LANES]
            here = lane // HEAD == i % 2
            head = jnp.sum(jnp.where(here, two, 0.0), axis=-1, keepdims=True)
            got = jnp.where(lane == n * (SIDE // HEAD) + i, head, got)
        delta[...] = got

    side_loop(width // SIDE, context_back)
    delta_turned[...] = jnp.transpose(delta[...])
    weight_grad(5, turn_b, dge.at[1])
    pump(5)
    attend_back_pairs(0, 3, qkvc, lse, delta_turned, mask, act)
    weight_grad(6, turn_b, dge.at[2])
    pump(6)
    attend_back_pairs(3, 6, qkvc, lse, delta_turned, mask, act)
    weight_grad(7, turn_b, dge.at[3])
    pump(7)
    attend_back_pairs(6, 8, qkvc, lse, delta_turned, mask, act)
    turn_a[...] = jnp.transpose(qkvc[3])
    weight_grad(8, turn_a, half)
    pump(8)
    loads["tokens"].wait()
    turn_b[...] = jnp.transpose(tokens[...])
    weight_grad(9, turn_b, act.at[2])
    pump(9)
    weight_grad(10, turn_b, act.at[1])
    pump(10)

    def bias_sums(n):
        cols = aligned(n * SIDE, SIDE)
        short[0:1, cols] = sums_of(act[0, :, cols], cols)
        short[1:2, cols] = sums_of(act[2, :, cols], cols)

    side_loop(width // SIDE, bias_sums)
    for dp in range(2 * depth):
        for fsdp in range(4):
            at = (dp * 4 + fsdp) * LANES
            vec[0][0, dp // 2, dp % 2, fsdp // 2, fsdp % 2] = to_half(
                jnp.concatenate(
                    [
                        short[:, dp * LANES : (dp + 1) * LANES],
                        jnp.broadcast_to(up_bias[:, at : at + LANES], (8, LANES)),
                    ],
                    axis=0,
                )
            )
    weight_grad(11, turn_b, act.at[0])
    pump(11)
    for i, (w, j) in enumerate(((9, 2), (10, 1), (11, 0))):
        w = weight(w)
        side_loop(width // SIDE, lambda n: add_product(act.at[j], w, aligned(n * SIDE, SIDE)))
        if i == 2:
            done = pltpu.make_async_copy(total, dtok_hbm, osem.at[0])
            done.start()
        pump(12 + i)
    pump(15)
    moved = pltpu.roll(tile_sum[...], (4 - fs) * rows % LANES, 1)
    gshort[...] = moved[:8]
    gup_bias[...] = tile_sum[8:9, :]
    done.wait()


def backward_call(depth, tokens, segment, full, qkvc, lse, mid, act, dge, nhat, rstd, dsec, small):
    length, width = tokens.shape
    rows = full.shape[-2]
    bf, f32 = jnp.bfloat16, jnp.float32
    part = ((rows, width), f32)
    shapes = [
        ((length, width), f32), part, part, part, part, ((rows, 4 * width), f32), ((rows, 4 * width), f32),
        ((8, LANES), f32), ((1, LANES), f32),
    ]
    vmem, hbm = pl.BlockSpec(memory_space=pltpu.VMEM), pl.BlockSpec(memory_space=pl.ANY)
    scratch = [
        pltpu.VMEM((length, width), bf),
        pltpu.VMEM((4, length, width), bf),
        pltpu.VMEM((LANES, length), f32),
        pltpu.VMEM((length, width), bf),
        pltpu.VMEM((4, length, width), bf),
        pltpu.VMEM((4, length, width), bf),
        pltpu.VMEM((length, width), f32),
        pltpu.VMEM((length, LANES), f32),
        pltpu.VMEM((length, width), f32),
        pltpu.VMEM((length, width), bf),
        pltpu.VMEM((width, length), bf),
        pltpu.VMEM((width, length), bf),
        pltpu.VMEM((length, length), f32),
        pltpu.VMEM((length, LANES), f32),
        pltpu.VMEM((LANES, length), f32),
        pltpu.VMEM((WEIGHT_SLOTS,) + full.shape[1:], bf),
        pltpu.VMEM((8, width), f32),
        pltpu.VMEM((1, 4 * width), f32),
        pltpu.VMEM((16, LANES), f32),
    ]
    scratch += sum_scratch(depth, rows, width, SLOTS, BLOCKS)
    scratch += sum_scratch(depth, 16, LANES, (1,) * 8, 1)
    scratch += [pltpu.SemaphoreType.DMA((24,)), pltpu.SemaphoreType.DMA((BLOCKS,)), pltpu.SemaphoreType.DMA((1,))]
    return pl.pallas_call(
        functools.partial(backward_kernel, depth),
        out_shape=tuple(jax.ShapeDtypeStruct(*s) for s in shapes),
        in_specs=[hbm, vmem] + [hbm] * 9 + [vmem],
        out_specs=tuple([hbm] + [vmem] * 8),
        scratch_shapes=scratch,
        compiler_params=pltpu.CompilerParams(
            collective_id=1, has_side_effects=True, vmem_limit_bytes=60 * 2**20
        ),
        name="backward",
    )(tokens, segment, full, qkvc, lse, mid, act, dge, nhat, rstd, dsec, small)


def kernel_device(
    tokens, segment, cotangent, query_w, key_w, value_w, attn_out_w, up_w, down_w, query_bias, value_bias,
    attn_out_bias, up_bias, down_bias, norm1_gain, norm1_shift, norm2_gain, norm2_shift,
):
    depth = lax.axis_size("dp") // 2
    short = jnp.stack(
        [query_bias, value_bias, attn_out_bias, down_bias, norm1_gain, norm1_shift, norm2_gain, norm2_shift]
    )
    outputs, full, qkvc, logs, mid_half, act, dge, nhat, rstd, d_second, small = forward_call(
        depth, tokens, segment, cotangent, query_w, key_w, value_w, attn_out_w, up_w, jnp.transpose(down_w),
        short, up_bias[None],
    )
    d_tokens, qw, kw, vw, ow, uw, dw, short_sum, up_sum = backward_call(
        depth, tokens, segment, full, qkvc, logs, mid_half, act, dge, nhat, rstd, d_second, small
    )
    qb, vb, ob, db, g1, s1, g2, s2 = short_sum[:, : query_w.shape[0]]
    return (
        outputs, d_tokens, qw, kw, vw, ow, uw, jnp.transpose(dw), qb, vb, ob, up_sum[0], db, g1, s1, g2, s2,
    )


def solution(mesh):
    fits = mesh.shape["fsdp"] == 4 and mesh.shape["dp"] % 2 == 0 and 1024 // mesh.size == 32
    body = kernel_device if fits else plain_device
    in_specs = (
        P(("dp", "fsdp"), None),
        P(("dp", "fsdp"), None),
        P(("dp", "fsdp"), None),
        P(("dp", "fsdp"), None),
        P(("dp", "fsdp"), None),
        P(("dp", "fsdp"), None),
        P(("dp", "fsdp"), None),
        P(("dp", "fsdp"), None),
        P(None, ("dp", "fsdp")),
        P(("dp", "fsdp")),
        P(("dp", "fsdp")),
        P(("dp", "fsdp")),
        P(("dp", "fsdp")),
        P(("dp", "fsdp")),
        P(("dp", "fsdp")),
        P(("dp", "fsdp")),
        P(("dp", "fsdp")),
        P(("dp", "fsdp")),
    )
    out_specs = (
        P(("dp", "fsdp"), None),
        P(("dp", "fsdp"), None),
        P(("dp", "fsdp"), None),
        P(("dp", "fsdp"), None),
        P(("dp", "fsdp"), None),
        P(("dp", "fsdp"), None),
        P(("dp", "fsdp"), None),
        P(None, ("dp", "fsdp")),
        P(("dp", "fsdp")),
        P(("dp", "fsdp")),
        P(("dp", "fsdp")),
        P(("dp", "fsdp")),
        P(("dp", "fsdp")),
        P(("dp", "fsdp")),
        P(("dp", "fsdp")),
        P(("dp", "fsdp")),
        P(("dp", "fsdp")),
    )
    return jax.shard_map(
        body, mesh=mesh, in_specs=in_specs, out_specs=out_specs, check_vma=False
    )
```

```python
import functools

import jax
import jax.numpy as jnp
from jax import lax
from jax.experimental import pallas as pl
from jax.experimental.pallas import tpu as pltpu
from jax.sharding import PartitionSpec as P

MESH = pl.DeviceIdType.MESH
BLOCKS = 12
DP, FSDP = BOTH = ("dp", "fsdp")


class Place:
    def __init__(self):
        dp, fs = lax.axis_index(DP), lax.axis_index(FSDP)
        z, x, y, c = self.z, self.x, self.y, self.c = dp // 2, dp % 2, fs // 2, fs % 2
        self.fs = fs
        self.near = z + 1 - 2 * (z % 2)
        self.other = 3 - z
        self.low = 2 * (z // 2)
        self.high = 2 - self.low
        self.near_pair, self.far_pair = pl.ds(self.low, 2), pl.ds(self.high, 2)
        self.far_one = z // 2 * -1 + 2
        self.far_two = 3 - z // 2 * 3
        self.inside = (z == 1) | (z == 2)
        self.to_x, self.to_y = device(z, 1 - x, y, c), device(z, x, 1 - y, c)
        self.to_c = device(z, x, y, 1 - c)
        self.to_near, self.to_other = device(self.near, x, y, c), device(self.other, x, y, c)


def device(z, x, y, c):
    return (z * 2 + x, y * 2 + c)


def greet(at):
    bar = pltpu.get_barrier_semaphore()

    def hail(peer):
        pl.semaphore_signal(bar, inc=1, device_id=peer, device_id_type=MESH)

    def meet(*peers):
        for peer in peers:
            hail(peer)
        pl.semaphore_wait(bar, len(peers))

    always = (at.to_c, at.to_x, at.to_y, at.to_near)
    pl.when(at.inside)(lambda: meet(*always, at.to_other))
    pl.when(jnp.logical_not(at.inside))(lambda: meet(*always))


def send(src, dst, ssem, rsem, peer):
    return pltpu.make_async_remote_copy(
        src_ref=src, dst_ref=dst, send_sem=ssem, recv_sem=rsem, device_id=peer, device_id_type=MESH
    )


def numbered(*names):
    return {name: i for i, name in enumerate(names)}


GATHER_GETS = numbered(
    "near", "one", "two", "xn", "yn", "xf", "yf", "da", "db", "df", "xo", "yo",
    "c0", "c1", "c2", "c3", "c4", "c5", "c6", "c7",
)


C_NAMES = list(GATHER_GETS)[-8:]


class GatherBlock:
    def __init__(self, at, full, mine, ss, rs, early=False):
        self.at, self.full, self.mine, self.ss, self.rs, self.early = at, full, mine, ss, rs, early

    def piece(self, name):
        a, full = self.at, self.full
        x, y, c = a.x, a.y, a.c
        both = {"n": a.near_pair, "f": a.far_pair}
        return {
            "own": lambda: full.at[a.z, x, y, c],
            "near": lambda: full.at[a.near, x, y, c],
            "one": lambda: full.at[a.far_one, x, y, c],
            "two": lambda: full.at[a.far_two, x, y, c],
            "on": lambda: full.at[both["n"], x, y, c],
            "of": lambda: full.at[both["f"], x, y, c],
            "xn": lambda: full.at[both["n"], 1 - x, y, c],
            "xf": lambda: full.at[both["f"], 1 - x, y, c],
            "yn": lambda: full.at[both["n"], x, 1 - y, c],
            "yf": lambda: full.at[both["f"], x, 1 - y, c],
            "dn": lambda: full.at[both["n"], 1 - x, 1 - y, c],
            "df": lambda: full.at[both["f"], 1 - x, 1 - y, c],
            "xo": lambda: full.at[a.z, 1 - x, y, c],
            "yo": lambda: full.at[a.z, x, 1 - y, c],
            "x_near": lambda: full.at[a.near, 1 - x, y, c],
            "x_own": lambda: full.at[a.z, 1 - x, y, c],
            "y_near": lambda: full.at[a.near, x, 1 - y, c],
            "d_own": lambda: full.at[a.z, 1 - x, 1 - y, c],
            "d_near": lambda: full.at[a.near, 1 - x, 1 - y, c],
            "c0": lambda: full.at[both["n"], x, y, 1 - c],
            "c1": lambda: full.at[both["f"], x, y, 1 - c],
            "c2": lambda: full.at[both["n"], 1 - x, y, 1 - c],
            "c3": lambda: full.at[both["n"], x, 1 - y, 1 - c],
            "c4": lambda: full.at[both["n"], 1 - x, 1 - y, 1 - c],
            "c5": lambda: full.at[both["f"], 1 - x, y, 1 - c],
            "c6": lambda: full.at[both["f"], x, 1 - y, 1 - c],
            "c7": lambda: full.at[both["f"], 1 - x, 1 - y, 1 - c],
        }[name]()

    SENDS = {
        "own_near": ("own", "near", "to_near"),
        "own_other": ("own", "one", "to_other"),
        "near_other": ("near", "two", "to_other"),
        "one_near": ("one", "one", "to_near"),
        "two_near": ("two", "two", "to_near"),
        "xn": ("on", "xn", "to_x"),
        "yn": ("on", "yn", "to_y"),
        "xo": ("own", "xo", "to_x"),
        "yo": ("own", "yo", "to_y"),
        "xp": ("near", "xn", "to_x"),
        "yp": ("near", "yn", "to_y"),
        "xf": ("of", "xf", "to_x"),
        "yf": ("of", "yf", "to_y"),
        "da": ("x_own", "da", "to_y"),
        "db": ("y_near", "db", "to_x"),
        "d_other": ("dn", "df", "to_other"),
        "d_near": ("df", "df", "to_near"),
        "c0": ("on", "c0", "to_c"),
        "c1": ("of", "c1", "to_c"),
        "c2": ("xn", "c2", "to_c"),
        "c3": ("yn", "c3", "to_c"),
        "c4": ("dn", "c4", "to_c"),
        "c5": ("xf", "c5", "to_c"),
        "c6": ("yf", "c6", "to_c"),
        "c7": ("df", "c7", "to_c"),
    }
    ARRIVES = {"da": "d_own", "db": "d_near"}
    INSIDE = ("own_other", "near_other", "one_near", "two_near", "d_other", "d_near")

    def move(self, name):
        what, called, whom = self.SENDS[name]
        piece = self.piece(what)
        return send(
            piece, piece, self.ss.at[list(self.SENDS).index(name)], self.rs.at[GATHER_GETS[called]], getattr(self.at, whom)
        )

    def go(self, *names):
        for name in names:
            if name in self.INSIDE:
                pl.when(self.at.inside)(lambda: self.move(name).start())
            else:
                self.move(name).start()

    def get(self, name, what=None):
        piece = self.piece(what or self.ARRIVES.get(name, name))
        send(piece, piece, self.ss.at[0], self.rs.at[GATHER_GETS[name]], self.at.to_c).wait_recv()

    def stage(self, s):
        a = self.at
        if s == 0:
            self.full[a.z, a.x, a.y, a.c] = self.mine()
            self.go("own_near", "own_other")
            if self.early:
                self.go("xo", "yo")
        if s == 1:
            self.get("near")
            self.go("near_other")
            if self.early:
                self.go("xp", "yp", "c0")
            else:
                self.go("xn", "yn", "c0")
        if s == 2:
            self.get("one")
            self.go("one_near")
        if s == 3:
            self.get("two")
            self.go("two_near", "xf", "yf", "c1")
        if s == 4:
            if self.early:
                self.get("xo")
                self.go("da")
                self.get("xn", "x_near")
                self.go("c2")
                self.get("yo")
                self.get("yn", "y_near")
            else:
                self.get("xn")
                self.go("da", "c2")
                self.get("yn")
            self.go("db", "c3")
        if s == 5:
            self.get("da")
            self.get("db")
            self.go("d_other", "c4")
        if s == 6:
            self.get("xf")
            self.go("c5")
            self.get("yf")
            self.go("c6")
        if s == 7:
            self.get("df")
            self.go("d_near", "c7")
        if s == 8:
            for i in range(8):
                self.get(C_NAMES[i])
        if s == 9:
            for name in self.SENDS:
                if name not in self.INSIDE + (("xn", "yn") if self.early else ("xo", "yo", "xp", "yp")):
                    self.move(name).wait_send()

            @pl.when(a.inside)
            def _():
                for name in self.INSIDE:
                    self.move(name).wait_send()


GATHER_LAGS = (0, 1, 3, 6, 6, 7, 8, 8, 9, 11)
GATHER_ORDER = (4, 3, 5, 1, 0, 2, 6, 8, 7, 9)


HEAD = 64


norm_epsilon = 1e-12
masked_score = -1000000000.0


def to_half(array):
    return array.astype(jnp.bfloat16)


def matmul(left, right):
    return jnp.dot(left, right, preferred_element_type=jnp.float32)


def matmul_nt(left, right):
    return lax.dot_general(
        left, right, (((1,), (1,)), ((), ())), preferred_element_type=jnp.float32
    )


def contract_rows(left, right):
    return lax.dot_general(
        left, right, (((0,), (0,)), ((), ())), preferred_element_type=jnp.float32
    )


def column_sums(array):
    return jnp.sum(array.astype(jnp.float32), axis=0)


def normalize(values, gain_vec, shift_vec):
    center = values - jnp.mean(values, axis=-1, keepdims=True)
    spread = jnp.mean(center * center, axis=-1, keepdims=True)
    return center * lax.rsqrt(spread + norm_epsilon) * gain_vec + shift_vec


def gelu_exact(values):
    return jax.nn.gelu(values, approximate=False)


def split_heads(block):
    return block.reshape(block.shape[0], -1, HEAD)


def row_scores(queries, key_rows, labels):
    scores = (
        jnp.einsum("qhe,khe->hqk", queries, key_rows, preferred_element_type=jnp.float32) * 0.125
    )
    allowed = labels[:, None] == labels[None, :]
    return jnp.where(allowed[None], scores, masked_score)


def attend_row(pieces):
    queries, key_rows, value_rows, labels = pieces
    scores = row_scores(split_heads(queries), split_heads(key_rows), labels)
    row_max = jnp.max(scores, axis=-1, keepdims=True)
    row_exp = jnp.exp(scores - row_max)
    row_total = jnp.sum(row_exp, axis=-1, keepdims=True)
    probs_half = to_half(row_exp / row_total)
    context = jnp.einsum(
        "hqk,khe->qhe", probs_half, split_heads(value_rows), preferred_element_type=jnp.float32
    )
    return (to_half(context.reshape(queries.shape)), (row_max + jnp.log(row_total))[..., 0])


def attend_back(pieces):
    queries, key_rows, value_rows, labels, log_total, d_context = pieces
    query_heads = split_heads(queries)
    key_heads = split_heads(key_rows)
    context_heads = split_heads(d_context)
    scores = row_scores(query_heads, key_heads, labels)
    attn_probs = jnp.exp(scores - log_total[..., None])
    d_probs = jnp.einsum(
        "qhe,khe->hqk", context_heads, split_heads(value_rows), preferred_element_type=jnp.float32
    )
    row_delta = jnp.sum(attn_probs * d_probs, axis=-1, keepdims=True)
    d_scores = to_half(attn_probs * (d_probs - row_delta))
    d_queries = (
        jnp.einsum("hqk,khe->qhe", d_scores, key_heads, preferred_element_type=jnp.float32) * 0.125
    )
    d_keys = (
        jnp.einsum("hqk,qhe->khe", d_scores, query_heads, preferred_element_type=jnp.float32)
        * 0.125
    )
    d_values = jnp.einsum(
        "hqk,qhe->khe", to_half(attn_probs), context_heads, preferred_element_type=jnp.float32
    )
    return (
        to_half(d_queries.reshape(queries.shape)),
        to_half(d_keys.reshape(queries.shape)),
        to_half(d_values.reshape(queries.shape)),
    )


def plain_device(
    tokens,
    segment,
    cotangent,
    query_w,
    key_w,
    value_w,
    attn_out_w,
    up_w,
    down_w,
    query_bias,
    value_bias,
    attn_out_bias,
    up_bias,
    down_bias,
    norm1_gain,
    norm1_shift,
    norm2_gain,
    norm2_shift,
):
    row_count = segment.shape[0]
    row_length = segment.shape[1]
    model_width = tokens.shape[1]

    def by_rows(array):
        return array.reshape(row_count, row_length, -1)

    attn_set = (
        lax.all_gather(to_half(query_w), BOTH, axis=0, tiled=True),
        lax.all_gather(to_half(key_w), BOTH, axis=0, tiled=True),
        lax.all_gather(to_half(value_w), BOTH, axis=0, tiled=True),
        lax.all_gather(to_half(attn_out_w), BOTH, axis=0, tiled=True),
        lax.all_gather(to_half(query_bias), BOTH, axis=0, tiled=True),
        lax.all_gather(to_half(value_bias), BOTH, axis=0, tiled=True),
        lax.all_gather(to_half(attn_out_bias), BOTH, axis=0, tiled=True),
        lax.all_gather(to_half(norm1_gain), BOTH, axis=0, tiled=True),
        lax.all_gather(to_half(norm1_shift), BOTH, axis=0, tiled=True),
    )
    wq_full, wk_full, wv_full, wo_full, bias_q, bias_v, bias_o, gain_one, shift_one = attn_set
    ffn_set = (
        lax.all_gather(to_half(up_w), BOTH, axis=0, tiled=True),
        lax.all_gather(to_half(down_w), BOTH, axis=1, tiled=True),
        lax.all_gather(to_half(up_bias), BOTH, axis=0, tiled=True),
        lax.all_gather(to_half(down_bias), BOTH, axis=0, tiled=True),
        lax.all_gather(to_half(norm2_gain), BOTH, axis=0, tiled=True),
        lax.all_gather(to_half(norm2_shift), BOTH, axis=0, tiled=True),
    )
    w_up, w_down, bias_up, bias_down, gain_two, shift_two = ffn_set
    queries = to_half(matmul(tokens, wq_full) + bias_q.astype(jnp.float32))
    key_rows = to_half(matmul(tokens, wk_full))
    value_rows = to_half(matmul(tokens, wv_full) + bias_v.astype(jnp.float32))
    context, log_total = lax.map(
        attend_row, (by_rows(queries), by_rows(key_rows), by_rows(value_rows), segment)
    )
    context = context.reshape(-1, model_width)
    attended = matmul(context, wo_full) + bias_o.astype(jnp.float32)
    first_sum = tokens.astype(jnp.float32) + attended
    norm_mid, pull_one = jax.vjp(
        normalize, first_sum, gain_one.astype(jnp.float32), shift_one.astype(jnp.float32)
    )
    mid_half = to_half(norm_mid)
    pre_act = matmul(mid_half, w_up) + bias_up.astype(jnp.float32)
    act_out, pull_act = jax.vjp(gelu_exact, pre_act)
    act_half = to_half(act_out)
    ffn_out = matmul(act_half, w_down) + bias_down.astype(jnp.float32)
    second_sum = mid_half.astype(jnp.float32) + ffn_out
    final, pull_two = jax.vjp(
        normalize, second_sum, gain_two.astype(jnp.float32), shift_two.astype(jnp.float32)
    )
    outputs = to_half(final)
    valid = (segment.reshape(-1) >= 0).astype(jnp.float32)[:, None]
    d_out = cotangent.astype(jnp.float32) * valid
    d_second, d_gain_two, d_shift_two = pull_two(d_out)
    up_back, down_back = (
        lax.all_gather(to_half(up_w), BOTH, axis=0, tiled=True),
        lax.all_gather(to_half(down_w), BOTH, axis=1, tiled=True),
    )
    d_ffn = to_half(d_second)
    d_down_turned = contract_rows(d_ffn, act_half)
    d_down_bias = column_sums(d_ffn)
    (d_pre,) = pull_act(matmul_nt(d_ffn, down_back))
    d_pre_half = to_half(d_pre)
    d_up_w = contract_rows(mid_half, d_pre_half)
    d_up_bias = column_sums(d_pre_half)
    d_mid = d_second + matmul_nt(d_pre_half, up_back)
    d_first, d_gain_one, d_shift_one = pull_one(d_mid)
    wq_back, wk_back, wv_back, wo_back = (
        lax.all_gather(to_half(query_w), BOTH, axis=0, tiled=True),
        lax.all_gather(to_half(key_w), BOTH, axis=0, tiled=True),
        lax.all_gather(to_half(value_w), BOTH, axis=0, tiled=True),
        lax.all_gather(to_half(attn_out_w), BOTH, axis=0, tiled=True),
    )
    d_att = to_half(d_first)
    d_attn_out_w = contract_rows(context, d_att)
    d_attn_out_bias = column_sums(d_att)
    d_context = to_half(matmul_nt(d_att, wo_back))
    d_queries, d_keys, d_values = lax.map(
        attend_back,
        (
            by_rows(queries),
            by_rows(key_rows),
            by_rows(value_rows),
            segment,
            log_total,
            by_rows(d_context),
        ),
    )
    d_queries = d_queries.reshape(-1, model_width)
    d_keys = d_keys.reshape(-1, model_width)
    d_values = d_values.reshape(-1, model_width)
    d_query_w = contract_rows(tokens, d_queries)
    d_key_w = contract_rows(tokens, d_keys)
    d_value_w = contract_rows(tokens, d_values)
    d_query_bias = column_sums(d_queries)
    d_value_bias = column_sums(d_values)
    d_tokens = (
        d_first
        + matmul_nt(d_queries, wq_back)
        + matmul_nt(d_keys, wk_back)
        + matmul_nt(d_values, wv_back)
    )
    members = (
        d_query_w,
        d_key_w,
        d_value_w,
        d_attn_out_w,
        d_up_w,
        d_down_turned,
        d_query_bias,
        d_value_bias,
        d_attn_out_bias,
        d_up_bias,
        d_down_bias,
        d_gain_one,
        d_shift_one,
        d_gain_two,
        d_shift_two,
    )
    block_sums = (
        lax.psum_scatter(
            members[0].astype(jnp.bfloat16), DP, scatter_dimension=0, tiled=True
        ).astype(jnp.float32),
        lax.psum_scatter(
            members[1].astype(jnp.bfloat16), DP, scatter_dimension=0, tiled=True
        ).astype(jnp.float32),
        lax.psum_scatter(
            members[2].astype(jnp.bfloat16), DP, scatter_dimension=0, tiled=True
        ).astype(jnp.float32),
        lax.psum_scatter(
            members[3].astype(jnp.bfloat16), DP, scatter_dimension=0, tiled=True
        ).astype(jnp.float32),
        lax.psum_scatter(
            members[4].astype(jnp.bfloat16), DP, scatter_dimension=0, tiled=True
        ).astype(jnp.float32),
        lax.psum_scatter(
            members[5].astype(jnp.bfloat16), DP, scatter_dimension=0, tiled=True
        ).astype(jnp.float32),
        lax.psum_scatter(
            members[6].astype(jnp.bfloat16), DP, scatter_dimension=0, tiled=True
        ).astype(jnp.float32),
        lax.psum_scatter(
            members[7].astype(jnp.bfloat16), DP, scatter_dimension=0, tiled=True
        ).astype(jnp.float32),
        lax.psum_scatter(
            members[8].astype(jnp.bfloat16), DP, scatter_dimension=0, tiled=True
        ).astype(jnp.float32),
        lax.psum_scatter(
            members[9].astype(jnp.bfloat16), DP, scatter_dimension=0, tiled=True
        ).astype(jnp.float32),
        lax.psum_scatter(
            members[10].astype(jnp.bfloat16), DP, scatter_dimension=0, tiled=True
        ).astype(jnp.float32),
        lax.psum_scatter(
            members[11].astype(jnp.bfloat16), DP, scatter_dimension=0, tiled=True
        ).astype(jnp.float32),
        lax.psum_scatter(
            members[12].astype(jnp.bfloat16), DP, scatter_dimension=0, tiled=True
        ).astype(jnp.float32),
        lax.psum_scatter(
            members[13].astype(jnp.bfloat16), DP, scatter_dimension=0, tiled=True
        ).astype(jnp.float32),
        lax.psum_scatter(
            members[14].astype(jnp.bfloat16), DP, scatter_dimension=0, tiled=True
        ).astype(jnp.float32),
    )
    every_shard = (
        lax.psum_scatter(
            block_sums[0].astype(jnp.bfloat16), FSDP, scatter_dimension=0, tiled=True
        ).astype(jnp.float32),
        lax.psum_scatter(
            block_sums[1].astype(jnp.bfloat16), FSDP, scatter_dimension=0, tiled=True
        ).astype(jnp.float32),
        lax.psum_scatter(
            block_sums[2].astype(jnp.bfloat16), FSDP, scatter_dimension=0, tiled=True
        ).astype(jnp.float32),
        lax.psum_scatter(
            block_sums[3].astype(jnp.bfloat16), FSDP, scatter_dimension=0, tiled=True
        ).astype(jnp.float32),
        lax.psum_scatter(
            block_sums[4].astype(jnp.bfloat16), FSDP, scatter_dimension=0, tiled=True
        ).astype(jnp.float32),
        lax.psum_scatter(
            block_sums[5].astype(jnp.bfloat16), FSDP, scatter_dimension=0, tiled=True
        ).astype(jnp.float32),
        lax.psum_scatter(
            block_sums[6].astype(jnp.bfloat16), FSDP, scatter_dimension=0, tiled=True
        ).astype(jnp.float32),
        lax.psum_scatter(
            block_sums[7].astype(jnp.bfloat16), FSDP, scatter_dimension=0, tiled=True
        ).astype(jnp.float32),
        lax.psum_scatter(
            block_sums[8].astype(jnp.bfloat16), FSDP, scatter_dimension=0, tiled=True
        ).astype(jnp.float32),
        lax.psum_scatter(
            block_sums[9].astype(jnp.bfloat16), FSDP, scatter_dimension=0, tiled=True
        ).astype(jnp.float32),
        lax.psum_scatter(
            block_sums[10].astype(jnp.bfloat16), FSDP, scatter_dimension=0, tiled=True
        ).astype(jnp.float32),
        lax.psum_scatter(
            block_sums[11].astype(jnp.bfloat16), FSDP, scatter_dimension=0, tiled=True
        ).astype(jnp.float32),
        lax.psum_scatter(
            block_sums[12].astype(jnp.bfloat16), FSDP, scatter_dimension=0, tiled=True
        ).astype(jnp.float32),
        lax.psum_scatter(
            block_sums[13].astype(jnp.bfloat16), FSDP, scatter_dimension=0, tiled=True
        ).astype(jnp.float32),
        lax.psum_scatter(
            block_sums[14].astype(jnp.bfloat16), FSDP, scatter_dimension=0, tiled=True
        ).astype(jnp.float32),
    )
    (
        shard_qw,
        shard_kw,
        shard_vw,
        shard_ow,
        shard_uw,
        shard_turned,
        shard_qb,
        shard_vb,
        shard_ob,
        shard_ub,
        shard_db,
        shard_g1,
        shard_s1,
        shard_g2,
        shard_s2,
    ) = every_shard
    shard_dw = jnp.transpose(shard_turned)
    return (
        outputs,
        d_tokens,
        shard_qw,
        shard_kw,
        shard_vw,
        shard_ow,
        shard_uw,
        shard_dw,
        shard_qb,
        shard_vb,
        shard_ob,
        shard_ub,
        shard_db,
        shard_g1,
        shard_s1,
        shard_g2,
        shard_s2,
    )


ATTN = 4
LANES = 128
SIDE = 1024


def aligned(start, size, step=None):
    return pl.ds(pl.multiple_of(start, step or size), size)


def side_loop(count, body):
    def step(i, carry):
        body(i)
        return carry

    lax.fori_loop(0, count, step, 0)


def square(full, b):
    size = full.shape[-1]
    return full.at[b].reshape(size, size)


def spread_vectors(tiles, short_ref, up_ref, depth):
    for dp in range(2 * depth):
        total = jnp.zeros((16, LANES), jnp.float32)
        for fs in range(4):
            total = total + tiles[dp // 2, dp % 2, fs // 2, fs % 2].astype(jnp.float32)
        short_ref[:, dp * LANES : (dp + 1) * LANES] = total[:8]
        for fs in range(4):
            at = (dp * 4 + fs) * LANES
            up_ref[:, at : at + LANES] = total[8 + fs : 9 + fs]


def project(x_ref, weight, out_ref, bias=None, scale=None):
    def step(n):
        cols = aligned(n * SIDE, SIDE)
        got = matmul(x_ref[...], weight[:, cols])
        if bias is not None:
            got = got + bias[:, cols]
        got = to_half(got)
        if scale is not None:
            got = got * scale
        out_ref[:, cols] = got

    side_loop(weight.shape[1] // SIDE, step)


def attend_pairs(first, last, qkvc, lse, mask):
    length = mask.shape[0]

    def pair(p):
        lanes = aligned(p * LANES, LANES)
        q, k, v = qkvc[0, :, lanes], qkvc[1, :, lanes], qkvc[2, :, lanes]
        lane = lax.broadcasted_iota(jnp.int32, (length, LANES), 1)
        lower = lane < HEAD
        total = jnp.zeros((length, LANES), jnp.float32)
        logs = lse[...]
        for h in range(2):
            here = lower if h == 0 else jnp.logical_not(lower)
            key = jnp.where(here, k, jnp.zeros_like(k))
            scores = matmul_nt(q, key) + mask[...]
            row_max = jnp.max(scores, axis=-1, keepdims=True)
            row_exp = jnp.exp(scores - row_max)
            row_total = jnp.sum(row_exp, axis=-1, keepdims=True)
            part = matmul(to_half(row_exp), v) / row_total
            total = jnp.where(here, part, total)
            logs = jnp.where(lane == 2 * p + h, row_max + jnp.log(row_total), logs)
        qkvc[3, :, lanes] = to_half(total)
        lse[...] = logs

    def step(i, carry):
        pair(i)
        return carry

    lax.fori_loop(first, last, step, 0)


SUM_SENDS = numbered("c", "df", "dg", "da", "db", "xn", "yn", "xf", "yf", "f", "m", "n")
SUM_LAGS = (0, 1, 2, 3, 4, 3, 5, 6, 7)
SUM_ORDER = (1, 6, 4, 2, 7, 3, 0, 5, 8)
SUM_BUFFERS = {
    "grad": (2, (4, 2, 2, 2)),
    "held": (7, (4, 2, 2)),
    "c": (2, (4, 2, 2)),
    "df": (7, (2,)),
    "dg": (4, (2,)),
    "da": (2, ()),
    "db": (2, ()),
    "xn": (4, (2,)),
    "yn": (3, (2,)),
    "xf": (5, (2,)),
    "yf": (5, (2,)),
    "f": (5, (2,)),
    "m": (4, (2,)),
    "n": (4, ()),
}


def sum_scratch(rows, cols, blocks, names):
    bufs = [SUM_BUFFERS[name] for name in names]
    bufs = [pltpu.VMEM((min(slots, blocks),) + parts + (rows, cols), jnp.bfloat16) for slots, parts in bufs]
    return bufs + [pltpu.SemaphoreType.DMA((blocks, len(SUM_SENDS)))] * 2


class SumBlock:
    def __init__(self, at, refs, names, b, **others):
        self.at = at
        *bufs, ss, rs = refs
        self.ss, self.rs = ss.at[b], rs.at[b]
        self.buf = {n: ref.at[b % ref.shape[0]] for n, ref in zip(names, bufs)} | others

    def move(self, name):
        a, held = self.at, self.buf["held"]
        x, y = a.x, a.y
        every, both = pl.ds(0, 4), pl.ds(0, 2)
        src, to = {
            "c": lambda: (self.buf["grad"].at[every, both, both, 1 - a.c], a.to_c),
            "df": lambda: (held.at[a.far_pair, 1 - x, 1 - y], a.to_near),
            "dg": lambda: (held.at[a.far_pair, 1 - x, 1 - y], a.to_other),
            "da": lambda: (held.at[a.z, 1 - x, 1 - y], a.to_y),
            "db": lambda: (held.at[a.near, 1 - x, 1 - y], a.to_x),
            "xn": lambda: (held.at[a.near_pair, 1 - x, y], a.to_x),
            "yn": lambda: (held.at[a.near_pair, x, 1 - y], a.to_y),
            "xf": lambda: (held.at[a.far_pair, 1 - x, y], a.to_x),
            "yf": lambda: (held.at[a.far_pair, x, 1 - y], a.to_y),
            "f": lambda: (held.at[a.far_pair, x, y], a.to_near),
            "m": lambda: (held.at[a.far_pair, x, y], a.to_other),
            "n": lambda: (held.at[a.near, x, y], a.to_near),
        }[name]()
        i = SUM_SENDS[name]
        return send(src, self.buf[name], self.ss.at[i], self.rs.at[i], to)

    def start(self, name):
        self.move(name).start()

    def got(self, name):
        self.move(name).wait_recv()
        return self.buf[name]

    def stage(self, s, out=None):
        a, held, grad = self.at, self.buf["held"], self.buf["grad"]
        x, y, c = a.x, a.y, a.c
        inside = a.inside
        outside = jnp.logical_not(inside)

        def add(first, xx, yy, *others, count=2):
            for i in range(count):
                total = held[first + i, xx, yy].astype(jnp.float32)
                for other in others:
                    total = total + (other[i] if count == 2 else other[...]).astype(jnp.float32)
                held[first + i, xx, yy] = total.astype(jnp.bfloat16)

        if s == 0:
            self.start("c")
        if s == 1:
            self.move("c").wait()
            pair = self.buf["c"]

            def join(first, xx, yy):
                for i in range(2):
                    held[first + i, xx, yy] = grad[first + i, xx, yy, c] + pair[first + i, xx, yy]

            join(a.high, 1 - x, 1 - y)
            pl.when(outside)(lambda: self.start("df"))
            join(a.high, 1 - x, y)
            self.start("xf")
            join(a.high, x, 1 - y)
            self.start("yf")
            join(a.low, 1 - x, 1 - y)
            join(a.low, 1 - x, y)
            join(a.low, x, 1 - y)
            join(a.high, x, y)
            join(a.low, x, y)
        if s == 2:

            @pl.when(inside)
            def _():
                add(a.high, 1 - x, 1 - y, self.got("df"))
                self.start("dg")

        if s == 3:

            @pl.when(inside)
            def _():
                add(a.low, 1 - x, 1 - y, self.got("dg"))

            self.start("da")
            self.start("db")
        if s == 4:
            add(a.z, 1 - x, y, self.got("da"), count=1)
            self.start("xn")
            add(a.near, x, 1 - y, self.got("db"), count=1)
            self.start("yn")
        if s == 5:
            add(a.high, x, y, self.got("xf"), self.got("yf"))
            pl.when(outside)(lambda: self.start("f"))
        if s == 6:

            @pl.when(inside)
            def _():
                add(a.high, x, y, self.got("f"))
                self.start("m")

        if s == 7:
            add(a.low, x, y, self.got("xn"), self.got("yn"))

            @pl.when(inside)
            def _():
                add(a.low, x, y, self.got("m"))

            self.start("n")
        if s == 8:
            out[...] = held[a.z, x, y].astype(jnp.float32) + self.got("n")[...].astype(jnp.float32)
            for name in ("da", "db", "xn", "yn", "xf", "yf", "n"):
                self.move(name).wait_send()

            @pl.when(inside)
            def _():
                self.move("dg").wait_send()
                self.move("m").wait_send()

            @pl.when(outside)
            def _():
                self.move("df").wait_send()
                self.move("f").wait_send()


def attend_back_pairs(first, last, qkvc, lse, delta, mask, grads):
    length = mask.shape[0]

    def pair(p, carry):
        lanes = aligned(p * LANES, LANES)
        q, k, v, d_context = qkvc[0, :, lanes], qkvc[1, :, lanes], qkvc[2, :, lanes], grads[3, :, lanes]
        lower = lax.broadcasted_iota(jnp.int32, (length, LANES), 1) < HEAD
        sums = [jnp.zeros((length, LANES), jnp.float32) for _ in range(3)]
        for h in range(2):
            here = lower if h == 0 else jnp.logical_not(lower)
            row = pl.ds(2 * p + h, 1)
            key = jnp.where(here, k, jnp.zeros_like(k))
            value = jnp.where(here, v, jnp.zeros_like(v))
            probs = jnp.exp(matmul_nt(key, q) + mask[...] - lse[row, :])
            d_scores = to_half(probs * (matmul_nt(value, d_context) - delta[row, :]))
            parts = (
                contract_rows(d_scores, k) * 0.125,
                matmul(d_scores, q),
                matmul(to_half(probs), d_context),
            )
            sums = [jnp.where(here, part, total) for part, total in zip(parts, sums)]
        for i in range(3):
            grads[i, :, lanes] = to_half(sums[i])
        return carry

    lax.fori_loop(first, last, pair, 0)


SUM_NAMES = tuple(SUM_BUFFERS)
LENT = SUM_NAMES[:2]
OWN_BUFFERS = SUM_NAMES[2:]


def layer_kernel(
    depth, *refs,
):
    (
        tokens_hbm, segment, cotangent_hbm, wq, wk, wv, wo, up_w, down_w, *vectors,
    ) = refs[:18]
    out_hbm, dtok_hbm, gq, gk, gv, go, gup, gdown, gshort, gup_bias = refs[18:28]
    (
        full, tiles, mine_vec, short, up_bias, qkvc, lse, lse_turned, mask, mid, act, dge, nhat, rstd, total, half,
        turn_a, delta_turned, tokens, cotangent, vgrads, up_grads, tile_sum, spare, ss, rs, isem, osem, *rest,
    ) = refs[28:]
    count = len(OWN_BUFFERS) + 2
    big, vec = rest[:count], rest[count:]
    length, width = tokens.shape
    here = Place()
    fs = here.fs
    rows = wq.shape[0]
    f32 = jnp.float32

    shards = [wq, wk, wv, wo]
    for wide in (up_w, down_w):
        shards += [wide.at[:, i * width : (i + 1) * width] for i in range(ATTN)]
    loads = [
        pltpu.make_async_copy(src, total.at[i * rows : (i + 1) * rows], isem.at[i]) for i, src in enumerate(shards)
    ]
    loads.append(pltpu.make_async_copy(tokens_hbm, tokens, isem.at[BLOCKS]))
    loads.append(pltpu.make_async_copy(cotangent_hbm, cotangent, isem.at[BLOCKS + 1]))
    for load in loads:
        load.start()
    greet(here)

    mine_vec[...] = jnp.zeros_like(mine_vec)
    for i in range(8):
        mine_vec[i : i + 1, 0:rows] = vectors[i][...]
    placed = pltpu.roll(mine_vec[...], fs * rows, 1)
    row_at = lax.broadcasted_iota(jnp.int32, (16, LANES), 0)
    mine_vec[...] = jnp.where(row_at == 8 + fs, jnp.broadcast_to(vectors[8][...], (16, LANES)), placed)

    def own(b):
        loads[b].wait()
        return to_half(total[b * rows : (b + 1) * rows, :])

    def gather_block(b):
        return GatherBlock(here, full.at[b], lambda: own(b), ss.at[b], rs.at[b], b < 2)

    own_tiles = GatherBlock(here, tiles, lambda: to_half(mine_vec[...]), ss.at[BLOCKS], rs.at[BLOCKS])

    flushed = []

    def flush(src, dst):
        copy = pltpu.make_async_copy(src, dst, osem.at[len(flushed)])
        copy.start()
        flushed.append(copy)

    def gather_pump(t):
        for s in GATHER_ORDER:
            b = t - GATHER_LAGS[s]
            if 0 <= b < BLOCKS:
                gather_block(b).stage(s)
            if b == 0:
                own_tiles.stage(s)

    gather_pump(0)
    gather_pump(1)
    labels = segment[...].astype(jnp.float32)
    turned = jnp.transpose(jnp.broadcast_to(labels, (LANES, length)))
    mask[...] = jnp.where(turned[:, :1] == labels, 0.0, masked_score)
    valid = jnp.where(turned[:, :1] >= 0.0, 1.0, 0.0)
    lse[...] = jnp.zeros_like(lse)
    for t in range(2, 10):
        gather_pump(t)
    spread_vectors(tiles, short, up_bias, depth)
    loads[BLOCKS].wait()
    project(tokens, square(full, 0), qkvc.at[0], short.at[0:1], 0.125)
    gather_pump(10)
    project(tokens, square(full, 1), qkvc.at[1])
    gather_pump(11)
    project(tokens, square(full, 2), qkvc.at[2], short.at[1:2])
    attend_pairs(0, 4, qkvc, lse, mask)
    gather_pump(12)
    attend_pairs(4, 8, qkvc, lse, mask)
    lse_turned[...] = jnp.transpose(lse[...])
    gather_pump(13)

    wo_full = square(full, 3)

    def attended(n):
        cols = aligned(n * SIDE, SIDE)
        total[:, cols] = (
            matmul(qkvc[3], wo_full[:, cols]) + short[2:3, cols] + tokens[:, cols].astype(jnp.float32)
        )

    side_loop(width // SIDE, attended)

    def first_norm(i):
        at = aligned(i * LANES, LANES)
        values = total[at, :]
        center = values - jnp.mean(values, axis=-1, keepdims=True)
        spread = jnp.mean(center * center, axis=-1, keepdims=True)
        r = lax.rsqrt(spread + norm_epsilon)
        unit = center * r
        nhat[at, :] = to_half(unit)
        rstd[at, :] = jnp.broadcast_to(r, (LANES, LANES))
        mid[at, :] = to_half(unit * short[4:5, :] + short[5:6, :])

    side_loop(length // LANES, first_norm)

    def activate(j):
        weight = square(full, ATTN + j)

        def step(n):
            cols = aligned(n * SIDE, SIDE)
            pre = matmul(mid[...], weight[:, cols]) + up_bias[:, aligned(j * width + n * SIDE, SIDE)]
            cdf = 0.5 * (1.0 + lax.erf(pre * 0.7071067811865476))
            act[j, :, cols] = to_half(pre * cdf)
            pdf = jnp.exp(-0.5 * pre * pre) * 0.3989422804014327
            dge[j, :, cols] = to_half(cdf + pre * pdf)

        side_loop(width // SIDE, step)

    def contract(j):
        weight = square(full, 2 * ATTN + j)

        def step(n):
            cols = aligned(n * SIDE, SIDE)
            got = matmul_nt(act[j], weight[cols, :])
            if j == 0:
                total[:, cols] = got + short[3:4, cols] + mid[:, cols].astype(jnp.float32)
            else:
                total[:, cols] = total[:, cols] + got

        side_loop(width // SIDE, step)

    gather_pump(14)
    activate(0)
    gather_pump(15)
    activate(1)
    gather_pump(16)
    activate(2)
    gather_pump(17)
    activate(3)
    contract(0)
    gather_pump(18)
    contract(1)
    gather_pump(19)
    contract(2)
    gather_pump(20)
    contract(3)

    loads[BLOCKS + 1].wait()
    vgrads[...] = jnp.zeros_like(vgrads)

    def second_norm(i):
        at = aligned(i * LANES, LANES)
        values = total[at, :]
        center = values - jnp.mean(values, axis=-1, keepdims=True)
        spread = jnp.mean(center * center, axis=-1, keepdims=True)
        r = lax.rsqrt(spread + norm_epsilon)
        unit = center * r
        gain = short[6:7, :]
        final = to_half(unit * gain + short[7:8, :])
        e = cotangent[at, :].astype(jnp.float32) * lse[at, 0:1]
        cotangent[at, :] = final
        vgrads[6:7, :] = vgrads[6:7, :] + jnp.sum(e * unit, axis=0, keepdims=True)
        vgrads[7:8, :] = vgrads[7:8, :] + jnp.sum(e, axis=0, keepdims=True)
        eg = e * gain
        d = r * (
            eg - jnp.mean(eg, axis=-1, keepdims=True) - unit * jnp.mean(eg * unit, axis=-1, keepdims=True)
        )
        total[at, :] = d
        half[at, :] = to_half(d)
        vgrads[3:4, :] = vgrads[3:4, :] + jnp.sum(to_half(d).astype(jnp.float32), axis=0, keepdims=True)

    lse[...] = jnp.broadcast_to(valid, lse.shape)
    side_loop(length // LANES, second_norm)
    flush(cotangent, out_hbm)

    outs = [gdown.at[:, i * width : (i + 1) * width] for i in range(4)]
    outs += [gup.at[:, i * width : (i + 1) * width] for i in range(4)] + [go, gv, gk, gq]

    held_at = [(4, 0), (4, 1), (9, 0), (9, 1), (5, 0), (5, 1), (10, 0)]

    def grad_of(b):
        return full.at[2 * ATTN] if b % 2 else spare

    def block(b):
        gathered, half_at = held_at[b % len(held_at)]
        lent = dict(zip(LENT, (grad_of(b), full.at[gathered, :, :, :, half_at])))
        return SumBlock(here, big, OWN_BUFFERS, b, **lent)

    vblock = SumBlock(here, vec, SUM_NAMES, 0)
    turn_b = square(full, 6).at[:, 0:length]

    def pump(t):
        for s in SUM_ORDER:
            b = t - SUM_LAGS[s]
            if 0 <= b < BLOCKS:
                block(b).stage(s, outs[b])
            if b == BLOCKS - 1:
                vblock.stage(s, tile_sum)

    def weight_grad(b, left, right):
        got = to_half(matmul(left[...], right[...]))
        grad = grad_of(b)
        grad[...] = got.reshape(grad.shape)

    def sums_of(ref, cols):
        return jnp.sum(ref.astype(f32), axis=0, keepdims=True)

    turn_a[...] = jnp.transpose(half[...])
    weight_grad(0, turn_a, act.at[0])
    pump(0)
    for t in range(21, BLOCKS + max(GATHER_LAGS)):
        gather_pump(t)

    def into_units(j):
        w = square(full, 2 * ATTN + j)

        def step(n):
            cols = aligned(n * SIDE, SIDE)
            d_pre = to_half(matmul(half[...], w[:, cols]) * dge[j, :, cols].astype(f32))
            dge[j, :, cols] = d_pre
            up_grads[:, aligned(j * width + n * SIDE, SIDE)] = sums_of(d_pre, cols)

        side_loop(width // SIDE, step)

    def add_product(left, w, cols):
        total[:, cols] = total[:, cols] + matmul_nt(left[...], w[cols, :])

    def out_of_units(j):
        w = square(full, ATTN + j)

        side_loop(width // SIDE, lambda n: add_product(dge.at[j], w, aligned(n * SIDE, SIDE)))

    for j in range(4):
        into_units(j)
        out_of_units(j)
        if j < 3:
            weight_grad(j + 1, turn_a, act.at[j + 1])
            pump(j + 1)

    turn_b[...] = jnp.transpose(mid[...])
    weight_grad(4, turn_b, dge.at[0])
    pump(4)


    def first_norm_back(i):
        at = aligned(i * LANES, LANES)
        e = total[at, :]
        unit = nhat[at, :].astype(f32)
        vgrads[4:5, :] = vgrads[4:5, :] + jnp.sum(e * unit, axis=0, keepdims=True)
        vgrads[5:6, :] = vgrads[5:6, :] + jnp.sum(e, axis=0, keepdims=True)
        eg = e * short[4:5, :]
        d = rstd[at, 0:1] * (
            eg - jnp.mean(eg, axis=-1, keepdims=True) - unit * jnp.mean(eg * unit, axis=-1, keepdims=True)
        )
        total[at, :] = d
        d_half = to_half(d)
        half[at, :] = d_half
        vgrads[2:3, :] = vgrads[2:3, :] + jnp.sum(d_half.astype(f32), axis=0, keepdims=True)

    side_loop(length // LANES, first_norm_back)
    wo_full = square(full, 3)
    delta = lse
    delta[...] = jnp.zeros_like(delta)

    def context_back(n):
        cols = aligned(n * SIDE, SIDE)
        d_context = to_half(matmul_nt(half[...], wo_full[cols, :]))
        act[3, :, cols] = d_context
        product = d_context.astype(f32) * qkvc[3, :, cols].astype(f32)
        lane = lax.broadcasted_iota(jnp.int32, (length, LANES), 1)
        got = delta[...]
        for i in range(SIDE // HEAD):
            two = product[:, (i // 2) * LANES : (i // 2 + 1) * LANES]
            here = lane // HEAD == i % 2
            head = jnp.sum(jnp.where(here, two, 0.0), axis=-1, keepdims=True)
            got = jnp.where(lane == n * (SIDE // HEAD) + i, head, got)
        delta[...] = got

    side_loop(width // SIDE, context_back)
    delta_turned[...] = jnp.transpose(delta[...])
    weight_grad(5, turn_b, dge.at[1])
    pump(5)
    attend_back_pairs(0, 3, qkvc, lse_turned, delta_turned, mask, act)
    weight_grad(6, turn_b, dge.at[2])
    pump(6)
    attend_back_pairs(3, 6, qkvc, lse_turned, delta_turned, mask, act)
    weight_grad(7, turn_b, dge.at[3])
    pump(7)
    attend_back_pairs(6, 8, qkvc, lse_turned, delta_turned, mask, act)
    turn_a[...] = jnp.transpose(qkvc[3])
    weight_grad(8, turn_a, half)
    pump(8)
    turn_b[...] = jnp.transpose(tokens[...])
    weight_grad(9, turn_b, act.at[2])
    pump(9)
    weight_grad(10, turn_b, act.at[1])
    pump(10)

    def bias_sums(n):
        cols = aligned(n * SIDE, SIDE)
        vgrads[0:1, cols] = sums_of(act[0, :, cols], cols)
        vgrads[1:2, cols] = sums_of(act[2, :, cols], cols)

    side_loop(width // SIDE, bias_sums)
    for dp in range(2 * depth):
        for fsdp in range(4):
            at = (dp * 4 + fsdp) * LANES
            vec[0][0, dp // 2, dp % 2, fsdp // 2, fsdp % 2] = to_half(
                jnp.concatenate(
                    [
                        vgrads[:, dp * LANES : (dp + 1) * LANES],
                        jnp.broadcast_to(up_grads[:, at : at + LANES], (8, LANES)),
                    ],
                    axis=0,
                )
            )
    weight_grad(11, turn_b, act.at[0])
    pump(11)
    for i, (w, j) in enumerate(((2, 2), (1, 1), (0, 0))):
        w = square(full, w)
        side_loop(width // SIDE, lambda n: add_product(act.at[j], w, aligned(n * SIDE, SIDE)))
        if i == 2:
            done = pltpu.make_async_copy(total, dtok_hbm, osem.at[1])
            done.start()
        pump(12 + i)
    for t in range(15, BLOCKS + max(SUM_LAGS)):
        pump(t)
    moved = pltpu.roll(tile_sum[...], (4 - fs) * rows % LANES, 1)
    gshort[...] = moved[:8]
    gup_bias[...] = tile_sum[8:9, :]
    done.wait()
    for copy in flushed:
        copy.wait()


def layer_call(depth, tokens, segment, cotangent, weights, vectors):
    length, width = tokens.shape
    rows = weights[0].shape[0]
    dims = (depth, 2, 2, 2)
    bf, f32 = jnp.bfloat16, jnp.float32
    part = ((rows, width), f32)
    shapes = [
        ((length, width), bf), ((length, width), f32), part, part, part, part, ((rows, ATTN * width), f32),
        ((rows, ATTN * width), f32), ((8, LANES), f32), ((1, LANES), f32),
    ]
    vmem, hbm = pl.BlockSpec(memory_space=pltpu.VMEM), pl.BlockSpec(memory_space=pl.ANY)
    scratch = [
        pltpu.VMEM((BLOCKS,) + dims + (rows, width), bf),
        pltpu.VMEM(dims + (16, LANES), bf),
        pltpu.VMEM((16, LANES), f32),
        pltpu.VMEM((8, width), f32),
        pltpu.VMEM((1, ATTN * width), f32),
        pltpu.VMEM((4, length, width), bf),
        pltpu.VMEM((length, LANES), f32),
        pltpu.VMEM((LANES, length), f32),
        pltpu.VMEM((length, length), f32),
        pltpu.VMEM((length, width), bf),
        pltpu.VMEM((ATTN, length, width), bf),
        pltpu.VMEM((ATTN, length, width), bf),
        pltpu.VMEM((length, width), bf),
        pltpu.VMEM((length, LANES), f32),
        pltpu.VMEM((length, width), f32),
        pltpu.VMEM((length, width), bf),
        pltpu.VMEM((width, length), bf),
        pltpu.VMEM((LANES, length), f32),
        pltpu.VMEM((length, width), bf),
        pltpu.VMEM((length, width), bf),
        pltpu.VMEM((8, width), f32),
        pltpu.VMEM((1, ATTN * width), f32),
        pltpu.VMEM((16, LANES), f32),
        pltpu.VMEM(dims + (rows, width), bf),
        pltpu.SemaphoreType.DMA((BLOCKS + 1, len(GatherBlock.SENDS))),
        pltpu.SemaphoreType.DMA((BLOCKS + 1, len(GATHER_GETS))),
        pltpu.SemaphoreType.DMA((BLOCKS + 2,)),
        pltpu.SemaphoreType.DMA((2,)),
    ]
    scratch += sum_scratch(rows, width, BLOCKS, OWN_BUFFERS) + sum_scratch(16, LANES, 1, SUM_NAMES)
    return pl.pallas_call(
        functools.partial(layer_kernel, depth),
        out_shape=tuple(jax.ShapeDtypeStruct(*s) for s in shapes),
        in_specs=[hbm, vmem, hbm] + [hbm] * 6 + [vmem] * 9,
        out_specs=tuple([hbm] * 2 + [vmem] * 8),
        scratch_shapes=scratch,
        compiler_params=pltpu.CompilerParams(
            collective_id=0, has_side_effects=True, vmem_limit_bytes=63 * 2**20
        ),
        name="layer",
    )(tokens, segment, cotangent, *weights, *vectors)


def results_kernel(large, short, *refs):
    sources, targets, vectors = refs[:large], refs[large + 2 : 2 * large + 2], refs[2 * large + 2 : 2 * large + 11]
    rows, up = refs[large : large + 2]
    held, (came, gone) = refs[2 * large + 11 : -2], refs[-2:]
    ins = [pltpu.make_async_copy(src, mid, came.at[i]) for i, (src, mid) in enumerate(zip(sources, held))]
    outs = [pltpu.make_async_copy(mid, dst, gone.at[i]) for i, (mid, dst) in enumerate(zip(held, targets))]
    for copy in ins:
        copy.start()
    for i in range(8):
        vectors[i][...] = rows[i : i + 1, 0:short]
    vectors[8][...] = up[...]
    for copy, onward in zip(ins, outs):
        copy.wait()
        onward.start()
    for copy in outs:
        copy.wait()


def results_call(large, rows, up, short):
    vmem, hbm = pl.BlockSpec(memory_space=pltpu.VMEM), pl.BlockSpec(memory_space=pl.ANY)
    shapes = [jax.ShapeDtypeStruct(a.shape, a.dtype) for a in large]
    shapes += [jax.ShapeDtypeStruct((1, short), jnp.float32)] * 8 + [jax.ShapeDtypeStruct(up.shape, jnp.float32)]
    return pl.pallas_call(
        functools.partial(results_kernel, len(large), short),
        out_shape=tuple(shapes),
        in_specs=[hbm] * len(large) + [vmem] * 2,
        out_specs=tuple([hbm] * len(large) + [vmem] * 9),
        scratch_shapes=[pltpu.VMEM(a.shape, a.dtype) for a in large]
        + [pltpu.SemaphoreType.DMA((len(large),))] * 2,
        name="results",
    )(*large, rows, up)


def kernel_device(
    tokens, segment, cotangent, query_w, key_w, value_w, attn_out_w, up_w, down_w, query_bias, value_bias,
    attn_out_bias, up_bias, down_bias, norm1_gain, norm1_shift, norm2_gain, norm2_shift,
):
    depth = lax.axis_size(DP) // 2
    weights = (query_w, key_w, value_w, attn_out_w, up_w, jnp.transpose(down_w))
    vectors = (
        query_bias, value_bias, attn_out_bias, down_bias, norm1_gain, norm1_shift, norm2_gain, norm2_shift, up_bias,
    )
    outputs, d_tokens, qw, kw, vw, ow, uw, dw, short_sum, up_sum = layer_call(
        depth, tokens, segment, cotangent, weights, [vector[None] for vector in vectors]
    )
    outputs, d_tokens, qw, kw, vw, ow, uw, dw, *vectors = results_call(
        (outputs, d_tokens, qw, kw, vw, ow, uw, dw), short_sum, up_sum, query_w.shape[0]
    )
    qb, vb, ob, db, g1, s1, g2, s2, ub = [vector.reshape(-1) for vector in vectors]
    return (
        outputs, d_tokens, qw, kw, vw, ow, uw, jnp.transpose(dw), qb, vb, ob, ub, db, g1, s1, g2, s2,
    )


def solution(mesh):
    fits = mesh.shape[FSDP] == 4 and mesh.shape[DP] == 8
    body = kernel_device if fits else plain_device
    in_specs = (
        P(BOTH, None),
        P(BOTH, None),
        P(BOTH, None),
        P(BOTH, None),
        P(BOTH, None),
        P(BOTH, None),
        P(BOTH, None),
        P(BOTH, None),
        P(None, BOTH),
        P(BOTH),
        P(BOTH),
        P(BOTH),
        P(BOTH),
        P(BOTH),
        P(BOTH),
        P(BOTH),
        P(BOTH),
        P(BOTH),
    )
    out_specs = (
        P(BOTH, None),
        P(BOTH, None),
        P(BOTH, None),
        P(BOTH, None),
        P(BOTH, None),
        P(BOTH, None),
        P(BOTH, None),
        P(None, BOTH),
        P(BOTH),
        P(BOTH),
        P(BOTH),
        P(BOTH),
        P(BOTH),
        P(BOTH),
        P(BOTH),
        P(BOTH),
        P(BOTH),
    )
    return jax.shard_map(
        body, mesh=mesh, in_specs=in_specs, out_specs=out_specs, check_vma=False
    )
```

```python
import functools

import jax
import jax.numpy as jnp
from jax import lax
from jax.experimental import pallas as pl
from jax.experimental.pallas import tpu as pltpu
from jax.sharding import PartitionSpec as P

MESH = pl.DeviceIdType.MESH
BLOCKS = 12
DP, FSDP = BOTH = ("dp", "fsdp")


class Place:
    def __init__(self):
        dp, fs = lax.axis_index(DP), lax.axis_index(FSDP)
        z, x, y, c = self.z, self.x, self.y, self.c = dp // 2, dp % 2, fs // 2, fs % 2
        self.fs = fs
        self.near = z + 1 - 2 * (z % 2)
        self.other = 3 - z
        self.low = 2 * (z // 2)
        self.high = 2 - self.low
        self.near_pair, self.far_pair = pl.ds(self.low, 2), pl.ds(self.high, 2)
        self.far_one = z // 2 * -1 + 2
        self.far_two = 3 - z // 2 * 3
        self.inside = (z == 1) | (z == 2)
        self.to_x, self.to_y = device(z, 1 - x, y, c), device(z, x, 1 - y, c)
        self.to_c = device(z, x, y, 1 - c)
        self.to_near, self.to_other = device(self.near, x, y, c), device(self.other, x, y, c)


def device(z, x, y, c):
    return (z * 2 + x, y * 2 + c)


def greet(at):
    bar = pltpu.get_barrier_semaphore()

    def hail(peer):
        pl.semaphore_signal(bar, inc=1, device_id=peer, device_id_type=MESH)

    def meet(*peers):
        for peer in peers:
            hail(peer)
        pl.semaphore_wait(bar, len(peers))

    always = (at.to_c, at.to_x, at.to_y, at.to_near)
    pl.when(at.inside)(lambda: meet(*always, at.to_other))
    pl.when(jnp.logical_not(at.inside))(lambda: meet(*always))


def send(src, dst, ssem, rsem, peer):
    return pltpu.make_async_remote_copy(
        src_ref=src, dst_ref=dst, send_sem=ssem, recv_sem=rsem, device_id=peer, device_id_type=MESH
    )


def numbered(*names):
    return {name: i for i, name in enumerate(names)}


GATHER_GETS = numbered(
    "near", "one", "two", "xn", "yn", "xf", "yf", "da", "db", "df", "xo", "yo",
    "c0", "c1", "c2", "c3", "c4", "c5", "c6", "c7",
)


C_NAMES = list(GATHER_GETS)[-8:]


class GatherBlock:
    def __init__(self, at, full, mine, ss, rs, early=False):
        self.at, self.full, self.mine, self.ss, self.rs, self.early = at, full, mine, ss, rs, early

    def piece(self, name):
        a, full = self.at, self.full
        x, y, c = a.x, a.y, a.c
        both = {"n": a.near_pair, "f": a.far_pair}
        return {
            "own": lambda: full.at[a.z, x, y, c],
            "near": lambda: full.at[a.near, x, y, c],
            "one": lambda: full.at[a.far_one, x, y, c],
            "two": lambda: full.at[a.far_two, x, y, c],
            "on": lambda: full.at[both["n"], x, y, c],
            "of": lambda: full.at[both["f"], x, y, c],
            "xn": lambda: full.at[both["n"], 1 - x, y, c],
            "xf": lambda: full.at[both["f"], 1 - x, y, c],
            "yn": lambda: full.at[both["n"], x, 1 - y, c],
            "yf": lambda: full.at[both["f"], x, 1 - y, c],
            "dn": lambda: full.at[both["n"], 1 - x, 1 - y, c],
            "df": lambda: full.at[both["f"], 1 - x, 1 - y, c],
            "xo": lambda: full.at[a.z, 1 - x, y, c],
            "yo": lambda: full.at[a.z, x, 1 - y, c],
            "x_near": lambda: full.at[a.near, 1 - x, y, c],
            "x_own": lambda: full.at[a.z, 1 - x, y, c],
            "y_near": lambda: full.at[a.near, x, 1 - y, c],
            "d_own": lambda: full.at[a.z, 1 - x, 1 - y, c],
            "d_near": lambda: full.at[a.near, 1 - x, 1 - y, c],
            "c0": lambda: full.at[both["n"], x, y, 1 - c],
            "c1": lambda: full.at[both["f"], x, y, 1 - c],
            "c2": lambda: full.at[both["n"], 1 - x, y, 1 - c],
            "c3": lambda: full.at[both["n"], x, 1 - y, 1 - c],
            "c4": lambda: full.at[both["n"], 1 - x, 1 - y, 1 - c],
            "c5": lambda: full.at[both["f"], 1 - x, y, 1 - c],
            "c6": lambda: full.at[both["f"], x, 1 - y, 1 - c],
            "c7": lambda: full.at[both["f"], 1 - x, 1 - y, 1 - c],
        }[name]()

    SENDS = {
        "own_near": ("own", "near", "to_near"),
        "own_other": ("own", "one", "to_other"),
        "near_other": ("near", "two", "to_other"),
        "one_near": ("one", "one", "to_near"),
        "two_near": ("two", "two", "to_near"),
        "xn": ("on", "xn", "to_x"),
        "yn": ("on", "yn", "to_y"),
        "xo": ("own", "xo", "to_x"),
        "yo": ("own", "yo", "to_y"),
        "xp": ("near", "xn", "to_x"),
        "yp": ("near", "yn", "to_y"),
        "xf": ("of", "xf", "to_x"),
        "yf": ("of", "yf", "to_y"),
        "da": ("x_own", "da", "to_y"),
        "db": ("y_near", "db", "to_x"),
        "d_other": ("dn", "df", "to_other"),
        "d_near": ("df", "df", "to_near"),
        "c0": ("on", "c0", "to_c"),
        "c1": ("of", "c1", "to_c"),
        "c2": ("xn", "c2", "to_c"),
        "c3": ("yn", "c3", "to_c"),
        "c4": ("dn", "c4", "to_c"),
        "c5": ("xf", "c5", "to_c"),
        "c6": ("yf", "c6", "to_c"),
        "c7": ("df", "c7", "to_c"),
    }
    ARRIVES = {"da": "d_own", "db": "d_near"}
    INSIDE = ("own_other", "near_other", "one_near", "two_near", "d_other", "d_near")

    def move(self, name):
        what, called, whom = self.SENDS[name]
        piece = self.piece(what)
        return send(
            piece, piece, self.ss.at[list(self.SENDS).index(name)], self.rs.at[GATHER_GETS[called]], getattr(self.at, whom)
        )

    def go(self, *names):
        for name in names:
            if name in self.INSIDE:
                pl.when(self.at.inside)(lambda: self.move(name).start())
            else:
                self.move(name).start()

    def get(self, name, what=None):
        piece = self.piece(what or self.ARRIVES.get(name, name))
        send(piece, piece, self.ss.at[0], self.rs.at[GATHER_GETS[name]], self.at.to_c).wait_recv()

    def stage(self, s):
        a = self.at
        if s == 0:
            self.full[a.z, a.x, a.y, a.c] = self.mine()
            self.go("own_near", "own_other")
            if self.early:
                self.go("xo", "yo")
        if s == 1:
            self.get("near")
            self.go("near_other")
            if self.early:
                self.go("xp", "yp", "c0")
            else:
                self.go("xn", "yn", "c0")
        if s == 2:
            self.get("one")
            self.go("one_near")
        if s == 3:
            self.get("two")
            self.go("two_near", "xf", "yf", "c1")
        if s == 4:
            if self.early:
                self.get("xo")
                self.go("da")
                self.get("xn", "x_near")
                self.go("c2")
                self.get("yo")
                self.get("yn", "y_near")
            else:
                self.get("xn")
                self.go("da", "c2")
                self.get("yn")
            self.go("db", "c3")
        if s == 5:
            self.get("da")
            self.get("db")
            self.go("d_other", "c4")
        if s == 6:
            self.get("xf")
            self.go("c5")
            self.get("yf")
            self.go("c6")
        if s == 7:
            self.get("df")
            self.go("d_near", "c7")
        if s == 8:
            for i in range(8):
                self.get(C_NAMES[i])
        if s == 9:
            for name in self.SENDS:
                if name not in self.INSIDE + (("xn", "yn") if self.early else ("xo", "yo", "xp", "yp")):
                    self.move(name).wait_send()

            @pl.when(a.inside)
            def _():
                for name in self.INSIDE:
                    self.move(name).wait_send()


GATHER_LAGS = (0, 1, 3, 6, 6, 7, 8, 8, 9, 11)
GATHER_ORDER = (4, 3, 5, 1, 0, 2, 6, 8, 7, 9)


HEAD = 64


norm_epsilon = 1e-12
masked_score = -1000000000.0


def to_half(array):
    return array.astype(jnp.bfloat16)


def matmul(left, right):
    return jnp.dot(left, right, preferred_element_type=jnp.float32)


def matmul_nt(left, right):
    return lax.dot_general(
        left, right, (((1,), (1,)), ((), ())), preferred_element_type=jnp.float32
    )


def contract_rows(left, right):
    return lax.dot_general(
        left, right, (((0,), (0,)), ((), ())), preferred_element_type=jnp.float32
    )


def column_sums(array):
    return jnp.sum(array.astype(jnp.float32), axis=0)


def normalize(values, gain_vec, shift_vec):
    center = values - jnp.mean(values, axis=-1, keepdims=True)
    spread = jnp.mean(center * center, axis=-1, keepdims=True)
    return center * lax.rsqrt(spread + norm_epsilon) * gain_vec + shift_vec


def gelu_exact(values):
    return jax.nn.gelu(values, approximate=False)


def split_heads(block):
    return block.reshape(block.shape[0], -1, HEAD)


def row_scores(queries, key_rows, labels):
    scores = (
        jnp.einsum("qhe,khe->hqk", queries, key_rows, preferred_element_type=jnp.float32) * 0.125
    )
    allowed = labels[:, None] == labels[None, :]
    return jnp.where(allowed[None], scores, masked_score)


def attend_row(pieces):
    queries, key_rows, value_rows, labels = pieces
    scores = row_scores(split_heads(queries), split_heads(key_rows), labels)
    row_max = jnp.max(scores, axis=-1, keepdims=True)
    row_exp = jnp.exp(scores - row_max)
    row_total = jnp.sum(row_exp, axis=-1, keepdims=True)
    probs_half = to_half(row_exp / row_total)
    context = jnp.einsum(
        "hqk,khe->qhe", probs_half, split_heads(value_rows), preferred_element_type=jnp.float32
    )
    return (to_half(context.reshape(queries.shape)), (row_max + jnp.log(row_total))[..., 0])


def attend_back(pieces):
    queries, key_rows, value_rows, labels, log_total, d_context = pieces
    query_heads = split_heads(queries)
    key_heads = split_heads(key_rows)
    context_heads = split_heads(d_context)
    scores = row_scores(query_heads, key_heads, labels)
    attn_probs = jnp.exp(scores - log_total[..., None])
    d_probs = jnp.einsum(
        "qhe,khe->hqk", context_heads, split_heads(value_rows), preferred_element_type=jnp.float32
    )
    row_delta = jnp.sum(attn_probs * d_probs, axis=-1, keepdims=True)
    d_scores = to_half(attn_probs * (d_probs - row_delta))
    d_queries = (
        jnp.einsum("hqk,khe->qhe", d_scores, key_heads, preferred_element_type=jnp.float32) * 0.125
    )
    d_keys = (
        jnp.einsum("hqk,qhe->khe", d_scores, query_heads, preferred_element_type=jnp.float32)
        * 0.125
    )
    d_values = jnp.einsum(
        "hqk,qhe->khe", to_half(attn_probs), context_heads, preferred_element_type=jnp.float32
    )
    return (
        to_half(d_queries.reshape(queries.shape)),
        to_half(d_keys.reshape(queries.shape)),
        to_half(d_values.reshape(queries.shape)),
    )


def plain_device(
    tokens,
    segment,
    cotangent,
    query_w,
    key_w,
    value_w,
    attn_out_w,
    up_w,
    down_w,
    query_bias,
    value_bias,
    attn_out_bias,
    up_bias,
    down_bias,
    norm1_gain,
    norm1_shift,
    norm2_gain,
    norm2_shift,
):
    row_count = segment.shape[0]
    row_length = segment.shape[1]
    model_width = tokens.shape[1]

    def by_rows(array):
        return array.reshape(row_count, row_length, -1)

    attn_set = (
        lax.all_gather(to_half(query_w), BOTH, axis=0, tiled=True),
        lax.all_gather(to_half(key_w), BOTH, axis=0, tiled=True),
        lax.all_gather(to_half(value_w), BOTH, axis=0, tiled=True),
        lax.all_gather(to_half(attn_out_w), BOTH, axis=0, tiled=True),
        lax.all_gather(to_half(query_bias), BOTH, axis=0, tiled=True),
        lax.all_gather(to_half(value_bias), BOTH, axis=0, tiled=True),
        lax.all_gather(to_half(attn_out_bias), BOTH, axis=0, tiled=True),
        lax.all_gather(to_half(norm1_gain), BOTH, axis=0, tiled=True),
        lax.all_gather(to_half(norm1_shift), BOTH, axis=0, tiled=True),
    )
    wq_full, wk_full, wv_full, wo_full, bias_q, bias_v, bias_o, gain_one, shift_one = attn_set
    ffn_set = (
        lax.all_gather(to_half(up_w), BOTH, axis=0, tiled=True),
        lax.all_gather(to_half(down_w), BOTH, axis=1, tiled=True),
        lax.all_gather(to_half(up_bias), BOTH, axis=0, tiled=True),
        lax.all_gather(to_half(down_bias), BOTH, axis=0, tiled=True),
        lax.all_gather(to_half(norm2_gain), BOTH, axis=0, tiled=True),
        lax.all_gather(to_half(norm2_shift), BOTH, axis=0, tiled=True),
    )
    w_up, w_down, bias_up, bias_down, gain_two, shift_two = ffn_set
    queries = to_half(matmul(tokens, wq_full) + bias_q.astype(jnp.float32))
    key_rows = to_half(matmul(tokens, wk_full))
    value_rows = to_half(matmul(tokens, wv_full) + bias_v.astype(jnp.float32))
    context, log_total = lax.map(
        attend_row, (by_rows(queries), by_rows(key_rows), by_rows(value_rows), segment)
    )
    context = context.reshape(-1, model_width)
    attended = matmul(context, wo_full) + bias_o.astype(jnp.float32)
    first_sum = tokens.astype(jnp.float32) + attended
    norm_mid, pull_one = jax.vjp(
        normalize, first_sum, gain_one.astype(jnp.float32), shift_one.astype(jnp.float32)
    )
    mid_half = to_half(norm_mid)
    pre_act = matmul(mid_half, w_up) + bias_up.astype(jnp.float32)
    act_out, pull_act = jax.vjp(gelu_exact, pre_act)
    act_half = to_half(act_out)
    ffn_out = matmul(act_half, w_down) + bias_down.astype(jnp.float32)
    second_sum = mid_half.astype(jnp.float32) + ffn_out
    final, pull_two = jax.vjp(
        normalize, second_sum, gain_two.astype(jnp.float32), shift_two.astype(jnp.float32)
    )
    outputs = to_half(final)
    valid = (segment.reshape(-1) >= 0).astype(jnp.float32)[:, None]
    d_out = cotangent.astype(jnp.float32) * valid
    d_second, d_gain_two, d_shift_two = pull_two(d_out)
    up_back, down_back = (
        lax.all_gather(to_half(up_w), BOTH, axis=0, tiled=True),
        lax.all_gather(to_half(down_w), BOTH, axis=1, tiled=True),
    )
    d_ffn = to_half(d_second)
    d_down_turned = contract_rows(d_ffn, act_half)
    d_down_bias = column_sums(d_ffn)
    (d_pre,) = pull_act(matmul_nt(d_ffn, down_back))
    d_pre_half = to_half(d_pre)
    d_up_w = contract_rows(mid_half, d_pre_half)
    d_up_bias = column_sums(d_pre_half)
    d_mid = d_second + matmul_nt(d_pre_half, up_back)
    d_first, d_gain_one, d_shift_one = pull_one(d_mid)
    wq_back, wk_back, wv_back, wo_back = (
        lax.all_gather(to_half(query_w), BOTH, axis=0, tiled=True),
        lax.all_gather(to_half(key_w), BOTH, axis=0, tiled=True),
        lax.all_gather(to_half(value_w), BOTH, axis=0, tiled=True),
        lax.all_gather(to_half(attn_out_w), BOTH, axis=0, tiled=True),
    )
    d_att = to_half(d_first)
    d_attn_out_w = contract_rows(context, d_att)
    d_attn_out_bias = column_sums(d_att)
    d_context = to_half(matmul_nt(d_att, wo_back))
    d_queries, d_keys, d_values = lax.map(
        attend_back,
        (
            by_rows(queries),
            by_rows(key_rows),
            by_rows(value_rows),
            segment,
            log_total,
            by_rows(d_context),
        ),
    )
    d_queries = d_queries.reshape(-1, model_width)
    d_keys = d_keys.reshape(-1, model_width)
    d_values = d_values.reshape(-1, model_width)
    d_query_w = contract_rows(tokens, d_queries)
    d_key_w = contract_rows(tokens, d_keys)
    d_value_w = contract_rows(tokens, d_values)
    d_query_bias = column_sums(d_queries)
    d_value_bias = column_sums(d_values)
    d_tokens = (
        d_first
        + matmul_nt(d_queries, wq_back)
        + matmul_nt(d_keys, wk_back)
        + matmul_nt(d_values, wv_back)
    )
    members = (
        d_query_w,
        d_key_w,
        d_value_w,
        d_attn_out_w,
        d_up_w,
        d_down_turned,
        d_query_bias,
        d_value_bias,
        d_attn_out_bias,
        d_up_bias,
        d_down_bias,
        d_gain_one,
        d_shift_one,
        d_gain_two,
        d_shift_two,
    )
    block_sums = (
        lax.psum_scatter(
            members[0].astype(jnp.bfloat16), DP, scatter_dimension=0, tiled=True
        ).astype(jnp.float32),
        lax.psum_scatter(
            members[1].astype(jnp.bfloat16), DP, scatter_dimension=0, tiled=True
        ).astype(jnp.float32),
        lax.psum_scatter(
            members[2].astype(jnp.bfloat16), DP, scatter_dimension=0, tiled=True
        ).astype(jnp.float32),
        lax.psum_scatter(
            members[3].astype(jnp.bfloat16), DP, scatter_dimension=0, tiled=True
        ).astype(jnp.float32),
        lax.psum_scatter(
            members[4].astype(jnp.bfloat16), DP, scatter_dimension=0, tiled=True
        ).astype(jnp.float32),
        lax.psum_scatter(
            members[5].astype(jnp.bfloat16), DP, scatter_dimension=0, tiled=True
        ).astype(jnp.float32),
        lax.psum_scatter(
            members[6].astype(jnp.bfloat16), DP, scatter_dimension=0, tiled=True
        ).astype(jnp.float32),
        lax.psum_scatter(
            members[7].astype(jnp.bfloat16), DP, scatter_dimension=0, tiled=True
        ).astype(jnp.float32),
        lax.psum_scatter(
            members[8].astype(jnp.bfloat16), DP, scatter_dimension=0, tiled=True
        ).astype(jnp.float32),
        lax.psum_scatter(
            members[9].astype(jnp.bfloat16), DP, scatter_dimension=0, tiled=True
        ).astype(jnp.float32),
        lax.psum_scatter(
            members[10].astype(jnp.bfloat16), DP, scatter_dimension=0, tiled=True
        ).astype(jnp.float32),
        lax.psum_scatter(
            members[11].astype(jnp.bfloat16), DP, scatter_dimension=0, tiled=True
        ).astype(jnp.float32),
        lax.psum_scatter(
            members[12].astype(jnp.bfloat16), DP, scatter_dimension=0, tiled=True
        ).astype(jnp.float32),
        lax.psum_scatter(
            members[13].astype(jnp.bfloat16), DP, scatter_dimension=0, tiled=True
        ).astype(jnp.float32),
        lax.psum_scatter(
            members[14].astype(jnp.bfloat16), DP, scatter_dimension=0, tiled=True
        ).astype(jnp.float32),
    )
    every_shard = (
        lax.psum_scatter(
            block_sums[0].astype(jnp.bfloat16), FSDP, scatter_dimension=0, tiled=True
        ).astype(jnp.float32),
        lax.psum_scatter(
            block_sums[1].astype(jnp.bfloat16), FSDP, scatter_dimension=0, tiled=True
        ).astype(jnp.float32),
        lax.psum_scatter(
            block_sums[2].astype(jnp.bfloat16), FSDP, scatter_dimension=0, tiled=True
        ).astype(jnp.float32),
        lax.psum_scatter(
            block_sums[3].astype(jnp.bfloat16), FSDP, scatter_dimension=0, tiled=True
        ).astype(jnp.float32),
        lax.psum_scatter(
            block_sums[4].astype(jnp.bfloat16), FSDP, scatter_dimension=0, tiled=True
        ).astype(jnp.float32),
        lax.psum_scatter(
            block_sums[5].astype(jnp.bfloat16), FSDP, scatter_dimension=0, tiled=True
        ).astype(jnp.float32),
        lax.psum_scatter(
            block_sums[6].astype(jnp.bfloat16), FSDP, scatter_dimension=0, tiled=True
        ).astype(jnp.float32),
        lax.psum_scatter(
            block_sums[7].astype(jnp.bfloat16), FSDP, scatter_dimension=0, tiled=True
        ).astype(jnp.float32),
        lax.psum_scatter(
            block_sums[8].astype(jnp.bfloat16), FSDP, scatter_dimension=0, tiled=True
        ).astype(jnp.float32),
        lax.psum_scatter(
            block_sums[9].astype(jnp.bfloat16), FSDP, scatter_dimension=0, tiled=True
        ).astype(jnp.float32),
        lax.psum_scatter(
            block_sums[10].astype(jnp.bfloat16), FSDP, scatter_dimension=0, tiled=True
        ).astype(jnp.float32),
        lax.psum_scatter(
            block_sums[11].astype(jnp.bfloat16), FSDP, scatter_dimension=0, tiled=True
        ).astype(jnp.float32),
        lax.psum_scatter(
            block_sums[12].astype(jnp.bfloat16), FSDP, scatter_dimension=0, tiled=True
        ).astype(jnp.float32),
        lax.psum_scatter(
            block_sums[13].astype(jnp.bfloat16), FSDP, scatter_dimension=0, tiled=True
        ).astype(jnp.float32),
        lax.psum_scatter(
            block_sums[14].astype(jnp.bfloat16), FSDP, scatter_dimension=0, tiled=True
        ).astype(jnp.float32),
    )
    (
        shard_qw,
        shard_kw,
        shard_vw,
        shard_ow,
        shard_uw,
        shard_turned,
        shard_qb,
        shard_vb,
        shard_ob,
        shard_ub,
        shard_db,
        shard_g1,
        shard_s1,
        shard_g2,
        shard_s2,
    ) = every_shard
    shard_dw = jnp.transpose(shard_turned)
    return (
        outputs,
        d_tokens,
        shard_qw,
        shard_kw,
        shard_vw,
        shard_ow,
        shard_uw,
        shard_dw,
        shard_qb,
        shard_vb,
        shard_ob,
        shard_ub,
        shard_db,
        shard_g1,
        shard_s1,
        shard_g2,
        shard_s2,
    )


ATTN = 4
LANES = 128
SIDE = 1024
V_LANE, R_LANE = 32, 64


def aligned(start, size, step=None):
    return pl.ds(pl.multiple_of(start, step or size), size)


def side_loop(count, body):
    def step(i, carry):
        body(i)
        return carry

    lax.fori_loop(0, count, step, 0)


def square(full, b):
    size = full.shape[-1]
    return full.at[b].reshape(size, size)


def spread_vectors(tiles, short_ref, up_ref, depth):
    for dp in range(2 * depth):
        total = jnp.zeros((16, LANES), jnp.float32)
        for fs in range(4):
            total = total + tiles[dp // 2, dp % 2, fs // 2, fs % 2].astype(jnp.float32)
        short_ref[:, dp * LANES : (dp + 1) * LANES] = total[:8]
        for fs in range(4):
            at = (dp * 4 + fs) * LANES
            up_ref[:, at : at + LANES] = total[8 + fs : 9 + fs]


def stepwise(body, after):
    def step(i):
        body(i)
        for k, follow in enumerate(after):
            pl.when(i == k)(follow)

    side_loop(len(after), step)


def nothing():
    pass


def attend_pairs(first, last, qkvc, lse, mask):
    length = mask.shape[0]

    def pair(p):
        lanes = aligned(p * LANES, LANES)
        q, k, v = qkvc[0, :, lanes], qkvc[1, :, lanes], qkvc[2, :, lanes]
        lane = lax.broadcasted_iota(jnp.int32, (length, LANES), 1)
        lower = lane < HEAD
        total = jnp.zeros((length, LANES), jnp.float32)
        logs = lse[...]
        for h in range(2):
            here = lower if h == 0 else jnp.logical_not(lower)
            key = jnp.where(here, k, jnp.zeros_like(k))
            scores = matmul_nt(q, key) + mask[...]
            row_max = jnp.max(scores, axis=-1, keepdims=True)
            row_exp = jnp.exp(scores - row_max)
            row_total = jnp.sum(row_exp, axis=-1, keepdims=True)
            part = matmul(to_half(row_exp), v) / row_total
            total = jnp.where(here, part, total)
            logs = jnp.where(lane == 2 * p + h, row_max + jnp.log(row_total), logs)
        qkvc[3, :, lanes] = to_half(total)
        lse[...] = logs

    def step(i, carry):
        pair(i)
        return carry

    lax.fori_loop(first, last, step, 0)


SUM_SENDS = numbered("c", "df", "dg", "da", "db", "xn", "yn", "xf", "yf", "f", "m", "n")
SUM_LAGS = (0, 1, 2, 3, 4, 3, 5, 6, 7)
SUM_ORDER = (1, 6, 4, 2, 7, 3, 0, 5, 8)
SUM_BUFFERS = {
    "grad": (2, (4, 2, 2, 2)),
    "held": (7, (4, 2, 2)),
    "c": (2, (4, 2, 2)),
    "df": (7, (2,)),
    "dg": (4, (2,)),
    "da": (2, ()),
    "db": (2, ()),
    "xn": (4, (2,)),
    "yn": (3, (2,)),
    "xf": (5, (2,)),
    "yf": (5, (2,)),
    "f": (5, (2,)),
    "m": (4, (2,)),
    "n": (4, ()),
}


def sum_scratch(rows, cols, blocks, names):
    bufs = [SUM_BUFFERS[name] for name in names]
    bufs = [pltpu.VMEM((min(slots, blocks),) + parts + (rows, cols), jnp.bfloat16) for slots, parts in bufs]
    return bufs + [pltpu.SemaphoreType.DMA((blocks, len(SUM_SENDS)))] * 2


class SumBlock:
    def __init__(self, at, refs, names, b, **others):
        self.at = at
        *bufs, ss, rs = refs
        self.ss, self.rs = ss.at[b], rs.at[b]
        self.buf = {n: ref.at[b % ref.shape[0]] for n, ref in zip(names, bufs)} | others

    def move(self, name):
        a, held = self.at, self.buf["held"]
        x, y = a.x, a.y
        every, both = pl.ds(0, 4), pl.ds(0, 2)
        src, to = {
            "c": lambda: (self.buf["grad"].at[every, both, both, 1 - a.c], a.to_c),
            "df": lambda: (held.at[a.far_pair, 1 - x, 1 - y], a.to_near),
            "dg": lambda: (held.at[a.far_pair, 1 - x, 1 - y], a.to_other),
            "da": lambda: (held.at[a.z, 1 - x, 1 - y], a.to_y),
            "db": lambda: (held.at[a.near, 1 - x, 1 - y], a.to_x),
            "xn": lambda: (held.at[a.near_pair, 1 - x, y], a.to_x),
            "yn": lambda: (held.at[a.near_pair, x, 1 - y], a.to_y),
            "xf": lambda: (held.at[a.far_pair, 1 - x, y], a.to_x),
            "yf": lambda: (held.at[a.far_pair, x, 1 - y], a.to_y),
            "f": lambda: (held.at[a.far_pair, x, y], a.to_near),
            "m": lambda: (held.at[a.far_pair, x, y], a.to_other),
            "n": lambda: (held.at[a.near, x, y], a.to_near),
        }[name]()
        i = SUM_SENDS[name]
        return send(src, self.buf[name], self.ss.at[i], self.rs.at[i], to)

    def start(self, name):
        self.move(name).start()

    def got(self, name):
        self.move(name).wait_recv()
        return self.buf[name]

    def stage(self, s, out=None):
        a, held, grad = self.at, self.buf["held"], self.buf["grad"]
        x, y, c = a.x, a.y, a.c
        inside = a.inside
        outside = jnp.logical_not(inside)

        def add(first, xx, yy, *others, count=2):
            for i in range(count):
                total = held[first + i, xx, yy].astype(jnp.float32)
                for other in others:
                    total = total + (other[i] if count == 2 else other[...]).astype(jnp.float32)
                held[first + i, xx, yy] = total.astype(jnp.bfloat16)

        if s == 0:
            self.start("c")
        if s == 1:
            self.move("c").wait()
            pair = self.buf["c"]

            def join(first, xx, yy):
                for i in range(2):
                    held[first + i, xx, yy] = grad[first + i, xx, yy, c] + pair[first + i, xx, yy]

            join(a.high, 1 - x, 1 - y)
            pl.when(outside)(lambda: self.start("df"))
            join(a.high, 1 - x, y)
            self.start("xf")
            join(a.high, x, 1 - y)
            self.start("yf")
            join(a.low, 1 - x, 1 - y)
            join(a.low, 1 - x, y)
            join(a.low, x, 1 - y)
            join(a.high, x, y)
            join(a.low, x, y)
        if s == 2:

            @pl.when(inside)
            def _():
                add(a.high, 1 - x, 1 - y, self.got("df"))
                self.start("dg")

        if s == 3:

            @pl.when(inside)
            def _():
                add(a.low, 1 - x, 1 - y, self.got("dg"))

            self.start("da")
            self.start("db")
        if s == 4:
            add(a.z, 1 - x, y, self.got("da"), count=1)
            self.start("xn")
            add(a.near, x, 1 - y, self.got("db"), count=1)
            self.start("yn")
        if s == 5:
            add(a.high, x, y, self.got("xf"), self.got("yf"))
            pl.when(outside)(lambda: self.start("f"))
        if s == 6:

            @pl.when(inside)
            def _():
                add(a.high, x, y, self.got("f"))
                self.start("m")

        if s == 7:
            add(a.low, x, y, self.got("xn"), self.got("yn"))

            @pl.when(inside)
            def _():
                add(a.low, x, y, self.got("m"))

            self.start("n")
        if s == 8:
            out[...] = held[a.z, x, y].astype(jnp.float32) + self.got("n")[...].astype(jnp.float32)
            for name in ("da", "db", "xn", "yn", "xf", "yf", "n"):
                self.move(name).wait_send()

            @pl.when(inside)
            def _():
                self.move("dg").wait_send()
                self.move("m").wait_send()

            @pl.when(outside)
            def _():
                self.move("df").wait_send()
                self.move("f").wait_send()


def attend_back_pairs(first, last, qkvc, lse, delta, mask, grads):
    length = mask.shape[0]

    def pair(p, carry):
        lanes = aligned(p * LANES, LANES)
        q, k, v, d_context = qkvc[0, :, lanes], qkvc[1, :, lanes], qkvc[2, :, lanes], grads[3, :, lanes]
        lower = lax.broadcasted_iota(jnp.int32, (length, LANES), 1) < HEAD
        sums = [jnp.zeros((length, LANES), jnp.float32) for _ in range(3)]
        for h in range(2):
            here = lower if h == 0 else jnp.logical_not(lower)
            row = pl.ds(2 * p + h, 1)
            key = jnp.where(here, k, jnp.zeros_like(k))
            value = jnp.where(here, v, jnp.zeros_like(v))
            probs = jnp.exp(matmul_nt(key, q) + mask[...] - lse[row, :])
            d_scores = to_half(probs * (matmul_nt(value, d_context) - delta[row, :]))
            parts = (
                contract_rows(d_scores, k) * 0.125,
                matmul(d_scores, q),
                matmul(to_half(probs), d_context),
            )
            sums = [jnp.where(here, part, total) for part, total in zip(parts, sums)]
        for i in range(3):
            grads[i, :, lanes] = to_half(sums[i])
        return carry

    lax.fori_loop(first, last, pair, 0)


SUM_NAMES = tuple(SUM_BUFFERS)
LENT = SUM_NAMES[:2]
OWN_BUFFERS = SUM_NAMES[2:]


def layer_kernel(depth, *refs):
    tokens_hbm, segment, cotangent_hbm, wq, wk, wv, wo, up_w, down_w, *vectors = refs[:18]
    out_hbm, dtok_hbm, gq, gk, gv, go, gup, gdown, gshort, gup_bias = refs[18:28]
    (
        full, tiles, mine_vec, short, up_bias, qkvc, lse, lse_turned, mask, mid, act, dge, nhat, total, half,
        turn_a, delta_turned, cotangent, vgrads, tile_sum, spare, staged, ss, rs, isem, osem, *rest,
    ) = refs[28:]
    count = len(OWN_BUFFERS) + 2
    big, vec = rest[:count], rest[count:]
    length, width = mid.shape
    tokens = mid
    here = Place()
    fs = here.fs
    rows = wq.shape[0]
    f32 = jnp.float32

    shards = [wq, wk, wv, wo]
    for wide in (up_w, down_w):
        shards += [wide.at[:, i * width : (i + 1) * width] for i in range(ATTN)]
    loads = [
        pltpu.make_async_copy(src, total.at[i * rows : (i + 1) * rows], isem.at[i]) for i, src in enumerate(shards)
    ]
    loads.append(pltpu.make_async_copy(tokens_hbm, tokens, isem.at[BLOCKS]))
    loads.append(pltpu.make_async_copy(cotangent_hbm, cotangent, isem.at[BLOCKS + 1]))
    for load in loads:
        load.start()
    greet(here)

    mine_vec[...] = jnp.zeros_like(mine_vec)
    for i in range(8):
        mine_vec[i : i + 1, 0:rows] = vectors[i][...]
    placed = pltpu.roll(mine_vec[...], fs * rows, 1)
    row_at = lax.broadcasted_iota(jnp.int32, (16, LANES), 0)
    mine_vec[...] = jnp.where(row_at == 8 + fs, jnp.broadcast_to(vectors[8][...], (16, LANES)), placed)

    def own(b):
        loads[b].wait()
        return to_half(total[b * rows : (b + 1) * rows, :])

    def gather_block(b):
        return GatherBlock(here, full.at[b], lambda: own(b), ss.at[b], rs.at[b], b < 2)

    own_tiles = GatherBlock(here, tiles, lambda: to_half(mine_vec[...]), ss.at[BLOCKS], rs.at[BLOCKS])

    def gather_pump(t):
        for s in GATHER_ORDER:
            b = t - GATHER_LAGS[s]
            if 0 <= b < BLOCKS:
                gather_block(b).stage(s)
            if b == 0:
                own_tiles.stage(s)

    gather_pump(0)
    gather_pump(1)
    labels = segment[...].astype(jnp.float32)
    turned = jnp.transpose(jnp.broadcast_to(labels, (LANES, length)))
    mask[...] = jnp.where(turned[:, :1] == labels, 0.0, masked_score)
    lse[...] = jnp.where(turned >= 0.0, 1.0, 0.0)
    for t in range(2, 10):
        gather_pump(t)
    spread_vectors(tiles, short, up_bias, depth)
    loads[BLOCKS].wait()

    def project(i):
        biased = jnp.where(i == 1, 0.0, 1.0)
        scale = jnp.where(i == 0, 0.125, 1.0)
        bias = short[pl.ds(i // 2, 1), :] * biased
        qkvc[i] = to_half(to_half(matmul(tokens[...], square(full, i)[...]) + bias).astype(f32) * scale)

    stepwise(project, [lambda: gather_pump(10), lambda: gather_pump(11), nothing])
    stepwise(
        lambda i: attend_pairs(i * 4, i * 4 + 4, qkvc, lse, mask),
        [lambda: gather_pump(12), nothing],
    )
    lse_turned[...] = jnp.transpose(lse[...])[: lse_turned.shape[0]]
    gather_pump(13)

    wo_full = square(full, 3)

    def attended(n):
        cols = aligned(n * SIDE, SIDE)
        total[:, cols] = (
            matmul(qkvc[3], wo_full[:, cols]) + short[2:3, cols] + tokens[:, cols].astype(jnp.float32)
        )

    side_loop(width // SIDE, attended)

    lane_at = lax.broadcasted_iota(jnp.int32, (LANES, LANES), 1)

    def first_norm(i):
        at = aligned(i * LANES, LANES)
        values = total[at, :]
        center = values - jnp.mean(values, axis=-1, keepdims=True)
        spread = jnp.mean(center * center, axis=-1, keepdims=True)
        r = lax.rsqrt(spread + norm_epsilon)
        unit = center * r
        nhat[at, :] = to_half(unit)
        lse[at, :] = jnp.where(lane_at >= R_LANE, r, lse[at, :])
        mid[at, :] = to_half(unit * short[4:5, :] + short[5:6, :])

    side_loop(length // LANES, first_norm)

    def activate(j):
        weight = square(full, ATTN + j)
        for part in range(2):
            cols = slice(part * width // 2, (part + 1) * width // 2)
            pre = matmul(mid[...], weight[:, cols]) + up_bias[:, aligned(j * width + part * width // 2, width // 2)]
            cdf = 0.5 * (1.0 + lax.erf(pre * 0.7071067811865476))
            act[j, :, cols] = to_half(pre * cdf)
            pdf = jnp.exp(-0.5 * pre * pre) * 0.3989422804014327
            dge[j, :, cols] = to_half(cdf + pre * pdf)

    def contract(j):
        total[...] = total[...] + matmul_nt(act[j], square(full, 2 * ATTN + j)[...])

    gather_pump(14)
    stepwise(activate, [lambda: gather_pump(15), lambda: gather_pump(16), lambda: gather_pump(17), nothing])
    total[...] = mid[...].astype(f32) + short[3:4, :]
    stepwise(contract, [lambda: gather_pump(18), lambda: gather_pump(19), lambda: gather_pump(20), nothing])

    loads[BLOCKS + 1].wait()
    vgrads[...] = jnp.zeros_like(vgrads)

    def second_norm(i):
        at = aligned(i * LANES, LANES)
        values = total[at, :]
        center = values - jnp.mean(values, axis=-1, keepdims=True)
        spread = jnp.mean(center * center, axis=-1, keepdims=True)
        r = lax.rsqrt(spread + norm_epsilon)
        unit = center * r
        gain = short[6:7, :]
        final = to_half(unit * gain + short[7:8, :])
        e = cotangent[at, :].astype(jnp.float32) * lse[at, V_LANE : V_LANE + 1]
        cotangent[at, :] = final
        vgrads[6:7, :] = vgrads[6:7, :] + jnp.sum(e * unit, axis=0, keepdims=True)
        vgrads[7:8, :] = vgrads[7:8, :] + jnp.sum(e, axis=0, keepdims=True)
        eg = e * gain
        d = r * (
            eg - jnp.mean(eg, axis=-1, keepdims=True) - unit * jnp.mean(eg * unit, axis=-1, keepdims=True)
        )
        total[at, :] = d
        half[at, :] = to_half(d)
        vgrads[3:4, :] = vgrads[3:4, :] + jnp.sum(to_half(d).astype(jnp.float32), axis=0, keepdims=True)

    side_loop(length // LANES, second_norm)
    pltpu.make_async_copy(cotangent, out_hbm, osem.at[0]).start()

    outs = [gdown.at[:, i * width : (i + 1) * width] for i in range(4)]
    outs += [gup.at[:, i * width : (i + 1) * width] for i in range(4)] + [go, gv, gk, gq]

    held_at = [(4, 0), (4, 1), (9, 0), (9, 1), (5, 0), (5, 1), (10, 0)]

    def grad_of(b):
        return spare.at[b % 2]

    def block(b):
        gathered, half_at = held_at[b % len(held_at)]
        lent = dict(zip(LENT, (grad_of(b), full.at[gathered, :, :, :, half_at])))
        return SumBlock(here, big, OWN_BUFFERS, b, **lent)

    vblock = SumBlock(here, vec, SUM_NAMES, 0)
    turn_b = square(full, 6).at[:, 0:length]

    def leave(b):
        return pltpu.make_async_copy(staged.at[b % 2], outs[b], osem.at[2 + b % 2])

    def pump(t):
        for s in SUM_ORDER:
            b = t - SUM_LAGS[s]
            if 0 <= b < BLOCKS:
                if s == 8 and b > 1:
                    leave(b - 2).wait()
                block(b).stage(s, staged.at[b % 2])
                if s == 8:
                    leave(b).start()
            if b == BLOCKS - 1:
                vblock.stage(s, tile_sum)

    def weight_grad(b, left, right):
        grad = grad_of(b)
        for part in range(2):
            got = to_half(matmul(left[part * width // 2 : (part + 1) * width // 2, :], right[...]))
            grad[2 * part : 2 * part + 2] = got.reshape((2,) + grad.shape[1:])

    def sums_of(values):
        return jnp.sum(values.astype(f32), axis=0, keepdims=True)

    turn_a[...] = jnp.transpose(half[...])
    weight_grad(0, turn_a, act.at[0])
    pump(0)
    for t in range(21, BLOCKS + max(GATHER_LAGS)):
        gather_pump(t)

    up_grads = up_bias

    def units_back(j):
        d_pre = to_half(matmul(half[...], square(full, 2 * ATTN + j)[...]) * dge[j].astype(f32))
        dge[j] = d_pre
        up_grads[:, aligned(j * width, width)] = sums_of(d_pre)
        add_product(dge.at[j], square(full, ATTN + j))

        @pl.when(j < ATTN - 1)
        def _():
            weight_grad(j + 1, turn_a, act.at[j + 1])

    def add_product(left, weight):
        total[...] = total[...] + matmul_nt(left[...], weight[...])

    stepwise(units_back, [lambda: pump(1), lambda: pump(2), lambda: pump(3), nothing])
    turn_b[...] = jnp.transpose(mid[...])
    loads[BLOCKS].start()
    weight_grad(4, turn_b, dge.at[0])
    pump(4)


    def first_norm_back(i):
        at = aligned(i * LANES, LANES)
        e = total[at, :]
        unit = nhat[at, :].astype(f32)
        vgrads[4:5, :] = vgrads[4:5, :] + jnp.sum(e * unit, axis=0, keepdims=True)
        vgrads[5:6, :] = vgrads[5:6, :] + jnp.sum(e, axis=0, keepdims=True)
        eg = e * short[4:5, :]
        d = lse[at, R_LANE : R_LANE + 1] * (
            eg - jnp.mean(eg, axis=-1, keepdims=True) - unit * jnp.mean(eg * unit, axis=-1, keepdims=True)
        )
        total[at, :] = d
        d_half = to_half(d)
        half[at, :] = d_half
        vgrads[2:3, :] = vgrads[2:3, :] + jnp.sum(d_half.astype(f32), axis=0, keepdims=True)

    side_loop(length // LANES, first_norm_back)
    wo_full = square(full, 3)
    delta = lse

    def context_back(n):
        cols = aligned(n * SIDE, SIDE)
        d_context = to_half(matmul_nt(half[...], wo_full[cols, :]))
        act[3, :, cols] = d_context
        product = d_context.astype(f32) * qkvc[3, :, cols].astype(f32)
        lane = lax.broadcasted_iota(jnp.int32, (length, LANES), 1)
        got = delta[...]
        for i in range(SIDE // HEAD):
            two = product[:, (i // 2) * LANES : (i // 2 + 1) * LANES]
            here = lane // HEAD == i % 2
            head = jnp.sum(jnp.where(here, two, 0.0), axis=-1, keepdims=True)
            got = jnp.where(lane == n * (SIDE // HEAD) + i, head, got)
        delta[...] = got

    side_loop(width // SIDE, context_back)
    delta_turned[...] = jnp.transpose(delta[...])[: delta_turned.shape[0]]
    weight_grad(5, turn_b, dge.at[1])
    pump(5)

    def attention_step(i):
        attend_back_pairs(3 * i, jnp.minimum(3 * i + 3, 8), qkvc, lse_turned, delta_turned, mask, act)

        @pl.when(i < 2)
        def _():
            weight_grad(6 + i, turn_b, dge.at[2 + i])

    stepwise(attention_step, [lambda: pump(6), lambda: pump(7), nothing])
    turn_a[...] = jnp.transpose(qkvc[3])
    weight_grad(8, turn_a, half)
    pump(8)
    loads[BLOCKS].wait()
    turn_b[...] = jnp.transpose(tokens[...])

    def place_vectors():
        vgrads[0:1, :] = sums_of(act[0])
        vgrads[1:2, :] = sums_of(act[2])
        for dp in range(2 * depth):
            for fsdp in range(4):
                at = (dp * 4 + fsdp) * LANES
                vec[0][0, dp // 2, dp % 2, fsdp // 2, fsdp % 2] = to_half(
                    jnp.concatenate(
                        [
                            vgrads[:, dp * LANES : (dp + 1) * LANES],
                            jnp.broadcast_to(up_grads[:, at : at + LANES], (8, LANES)),
                        ],
                        axis=0,
                    )
                )

    def last_pump():
        place_vectors()
        pump(11)

    stepwise(
        lambda i: weight_grad(9 + i, turn_b, act.at[2 - i]), [lambda: pump(9), lambda: pump(10), last_pump]
    )

    def hand_back():
        pltpu.make_async_copy(total, dtok_hbm, osem.at[1]).start()
        pump(14)

    stepwise(
        lambda i: add_product(act.at[2 - i], square(full, 2 - i)), [lambda: pump(12), lambda: pump(13), hand_back]
    )
    for t in range(15, BLOCKS + max(SUM_LAGS)):
        pump(t)
    leave(BLOCKS - 2).wait()
    leave(BLOCKS - 1).wait()
    moved = pltpu.roll(tile_sum[...], (4 - fs) * rows % LANES, 1)
    gshort[...] = moved[:8]
    gup_bias[...] = tile_sum[8:9, :]
    pltpu.make_async_copy(total, dtok_hbm, osem.at[1]).wait()
    pltpu.make_async_copy(cotangent, out_hbm, osem.at[0]).wait()


def layer_call(depth, tokens, segment, cotangent, weights, vectors):
    length, width = tokens.shape
    rows = weights[0].shape[0]
    dims = (depth, 2, 2, 2)
    bf, f32 = jnp.bfloat16, jnp.float32
    part = ((rows, width), f32)
    shapes = [
        ((length, width), bf), ((length, width), f32), part, part, part, part, ((rows, ATTN * width), f32),
        ((rows, ATTN * width), f32), ((8, LANES), f32), ((1, LANES), f32),
    ]
    vmem, hbm = pl.BlockSpec(memory_space=pltpu.VMEM), pl.BlockSpec(memory_space=pl.ANY)
    scratch = [
        pltpu.VMEM((BLOCKS,) + dims + (rows, width), bf),
        pltpu.VMEM(dims + (16, LANES), bf),
        pltpu.VMEM((16, LANES), f32),
        pltpu.VMEM((8, width), f32),
        pltpu.VMEM((1, ATTN * width), f32),
        pltpu.VMEM((4, length, width), bf),
        pltpu.VMEM((length, LANES), f32),
        pltpu.VMEM((width // HEAD, length), f32),
        pltpu.VMEM((length, length), f32),
        pltpu.VMEM((length, width), bf),
        pltpu.VMEM((ATTN, length, width), bf),
        pltpu.VMEM((ATTN, length, width), bf),
        pltpu.VMEM((length, width), bf),
        pltpu.VMEM((length, width), f32),
        pltpu.VMEM((length, width), bf),
        pltpu.VMEM((width, length), bf),
        pltpu.VMEM((width // HEAD, length), f32),
        pltpu.VMEM((length, width), bf),
        pltpu.VMEM((8, width), f32),
        pltpu.VMEM((16, LANES), f32),
        pltpu.VMEM((2,) + dims + (rows, width), bf),
        pltpu.VMEM((2, rows, width), f32),
        pltpu.SemaphoreType.DMA((BLOCKS + 1, len(GatherBlock.SENDS))),
        pltpu.SemaphoreType.DMA((BLOCKS + 1, len(GATHER_GETS))),
        pltpu.SemaphoreType.DMA((BLOCKS + 2,)),
        pltpu.SemaphoreType.DMA((4,)),
    ]
    scratch += sum_scratch(rows, width, BLOCKS, OWN_BUFFERS) + sum_scratch(16, LANES, 1, SUM_NAMES)
    return pl.pallas_call(
        functools.partial(layer_kernel, depth),
        out_shape=tuple(jax.ShapeDtypeStruct(*s) for s in shapes),
        in_specs=[hbm, vmem, hbm] + [hbm] * 6 + [vmem] * 9,
        out_specs=tuple([hbm] * 8 + [vmem] * 2),
        scratch_shapes=scratch,
        compiler_params=pltpu.CompilerParams(
            collective_id=0, has_side_effects=True, vmem_limit_bytes=63 * 2**20
        ),
        name="layer",
    )(tokens, segment, cotangent, *weights, *vectors)


PIECE = 1024


def results_kernel(large, short, *refs):
    sources, targets, vectors = refs[:large], refs[large + 2 : 2 * large + 2], refs[2 * large + 2 : 2 * large + 11]
    rows, up = refs[large : large + 2]
    held, (came, gone) = refs[2 * large + 11 : -2], refs[-2:]
    ins, outs = [], []
    for src, mid, dst in zip(sources, held, targets):
        for start in range(0, src.shape[0], PIECE):
            at = pl.ds(start, min(PIECE, src.shape[0]))
            i = len(ins)
            ins.append(pltpu.make_async_copy(src.at[at], mid.at[at], came.at[i]))
            outs.append(pltpu.make_async_copy(mid.at[at], dst.at[at], gone.at[i]))
    for copy in ins:
        copy.start()
    for i in range(8):
        vectors[i][...] = rows[i : i + 1, 0:short]
    vectors[8][...] = up[...]
    for copy, onward in zip(ins, outs):
        copy.wait()
        onward.start()
    for copy in outs:
        copy.wait()


def results_call(large, rows, up, short):
    vmem, hbm = pl.BlockSpec(memory_space=pltpu.VMEM), pl.BlockSpec(memory_space=pl.ANY)
    shapes = [jax.ShapeDtypeStruct(a.shape, a.dtype) for a in large]
    shapes += [jax.ShapeDtypeStruct((1, short), jnp.float32)] * 8 + [jax.ShapeDtypeStruct(up.shape, jnp.float32)]
    return pl.pallas_call(
        functools.partial(results_kernel, len(large), short),
        out_shape=tuple(shapes),
        in_specs=[hbm] * len(large) + [vmem] * 2,
        out_specs=tuple([hbm] * len(large) + [vmem] * 9),
        scratch_shapes=[pltpu.VMEM(a.shape, a.dtype) for a in large]
        + [pltpu.SemaphoreType.DMA((sum(-(-a.shape[0] // PIECE) for a in large),))] * 2,
        name="results",
    )(*large, rows, up)


def kernel_device(
    tokens, segment, cotangent, query_w, key_w, value_w, attn_out_w, up_w, down_w, query_bias, value_bias,
    attn_out_bias, up_bias, down_bias, norm1_gain, norm1_shift, norm2_gain, norm2_shift,
):
    depth = lax.axis_size(DP) // 2
    weights = (query_w, key_w, value_w, attn_out_w, up_w, jnp.transpose(down_w))
    vectors = (
        query_bias, value_bias, attn_out_bias, down_bias, norm1_gain, norm1_shift, norm2_gain, norm2_shift, up_bias,
    )
    outputs, d_tokens, qw, kw, vw, ow, uw, dw, short_sum, up_sum = layer_call(
        depth, tokens, segment, cotangent, weights, [vector[None] for vector in vectors]
    )
    outputs, d_tokens, qw, kw, vw, ow, uw, dw, *vectors = results_call(
        (outputs, d_tokens, qw, kw, vw, ow, uw, dw), short_sum, up_sum, query_w.shape[0]
    )
    qb, vb, ob, db, g1, s1, g2, s2, ub = [vector.reshape(-1) for vector in vectors]
    return (
        outputs, d_tokens, qw, kw, vw, ow, uw, jnp.transpose(dw), qb, vb, ob, ub, db, g1, s1, g2, s2,
    )


def solution(mesh):
    fits = mesh.shape[FSDP] == 4 and mesh.shape[DP] == 8
    body = kernel_device if fits else plain_device
    in_specs = (
        P(BOTH, None),
        P(BOTH, None),
        P(BOTH, None),
        P(BOTH, None),
        P(BOTH, None),
        P(BOTH, None),
        P(BOTH, None),
        P(BOTH, None),
        P(None, BOTH),
        P(BOTH),
        P(BOTH),
        P(BOTH),
        P(BOTH),
        P(BOTH),
        P(BOTH),
        P(BOTH),
        P(BOTH),
        P(BOTH),
    )
    out_specs = (
        P(BOTH, None),
        P(BOTH, None),
        P(BOTH, None),
        P(BOTH, None),
        P(BOTH, None),
        P(BOTH, None),
        P(BOTH, None),
        P(None, BOTH),
        P(BOTH),
        P(BOTH),
        P(BOTH),
        P(BOTH),
        P(BOTH),
        P(BOTH),
        P(BOTH),
        P(BOTH),
        P(BOTH),
    )
    return jax.shard_map(
        body, mesh=mesh, in_specs=in_specs, out_specs=out_specs, check_vma=False
    )
```

```python
import functools

import jax
import jax.numpy as jnp
from jax import lax
from jax.experimental import pallas as pl
from jax.experimental.pallas import tpu as pltpu
from jax.sharding import PartitionSpec as P

MESH = pl.DeviceIdType.MESH
BLOCKS = 12
DP, FSDP = BOTH = ("dp", "fsdp")


class Place:
    def __init__(self):
        dp, fs = lax.axis_index(DP), lax.axis_index(FSDP)
        z, x, y, c = self.z, self.x, self.y, self.c = dp // 2, dp % 2, fs // 2, fs % 2
        self.fs = fs
        self.near = z + 1 - 2 * (z % 2)
        self.other = 3 - z
        self.low = 2 * (z // 2)
        self.high = 2 - self.low
        self.near_pair, self.far_pair = pl.ds(self.low, 2), pl.ds(self.high, 2)
        self.far_one = z // 2 * -1 + 2
        self.far_two = 3 - z // 2 * 3
        self.inside = (z == 1) | (z == 2)
        self.to_x, self.to_y = device(z, 1 - x, y, c), device(z, x, 1 - y, c)
        self.to_c = device(z, x, y, 1 - c)
        self.to_near, self.to_other = device(self.near, x, y, c), device(self.other, x, y, c)


def device(z, x, y, c):
    return (z * 2 + x, y * 2 + c)


def greet(at):
    bar = pltpu.get_barrier_semaphore()

    def hail(peer):
        pl.semaphore_signal(bar, inc=1, device_id=peer, device_id_type=MESH)

    def meet(*peers):
        for peer in peers:
            hail(peer)
        pl.semaphore_wait(bar, len(peers))

    always = (at.to_c, at.to_x, at.to_y, at.to_near)
    pl.when(at.inside)(lambda: meet(*always, at.to_other))
    pl.when(jnp.logical_not(at.inside))(lambda: meet(*always))


def send(src, dst, ssem, rsem, peer):
    return pltpu.make_async_remote_copy(
        src_ref=src, dst_ref=dst, send_sem=ssem, recv_sem=rsem, device_id=peer, device_id_type=MESH
    )


def numbered(*names):
    return {name: i for i, name in enumerate(names)}


GATHER_GETS = numbered(
    "near", "one", "two", "xn", "yn", "xf", "yf", "da", "db", "df", "xo", "yo",
    "c0", "c1", "c2", "c3", "c4", "c5", "c6", "c7",
)


C_NAMES = list(GATHER_GETS)[-8:]


class GatherBlock:
    def __init__(self, at, full, mine, ss, rs, early=False):
        self.at, self.full, self.mine, self.ss, self.rs, self.early = at, full, mine, ss, rs, early

    def piece(self, name):
        a, full = self.at, self.full
        x, y, c = a.x, a.y, a.c
        both = {"n": a.near_pair, "f": a.far_pair}
        return {
            "own": lambda: full.at[a.z, x, y, c],
            "near": lambda: full.at[a.near, x, y, c],
            "one": lambda: full.at[a.far_one, x, y, c],
            "two": lambda: full.at[a.far_two, x, y, c],
            "on": lambda: full.at[both["n"], x, y, c],
            "of": lambda: full.at[both["f"], x, y, c],
            "xn": lambda: full.at[both["n"], 1 - x, y, c],
            "xf": lambda: full.at[both["f"], 1 - x, y, c],
            "yn": lambda: full.at[both["n"], x, 1 - y, c],
            "yf": lambda: full.at[both["f"], x, 1 - y, c],
            "dn": lambda: full.at[both["n"], 1 - x, 1 - y, c],
            "df": lambda: full.at[both["f"], 1 - x, 1 - y, c],
            "xo": lambda: full.at[a.z, 1 - x, y, c],
            "yo": lambda: full.at[a.z, x, 1 - y, c],
            "x_near": lambda: full.at[a.near, 1 - x, y, c],
            "x_own": lambda: full.at[a.z, 1 - x, y, c],
            "y_near": lambda: full.at[a.near, x, 1 - y, c],
            "d_own": lambda: full.at[a.z, 1 - x, 1 - y, c],
            "d_near": lambda: full.at[a.near, 1 - x, 1 - y, c],
            "c0": lambda: full.at[both["n"], x, y, 1 - c],
            "c1": lambda: full.at[both["f"], x, y, 1 - c],
            "c2": lambda: full.at[both["n"], 1 - x, y, 1 - c],
            "c3": lambda: full.at[both["n"], x, 1 - y, 1 - c],
            "c4": lambda: full.at[both["n"], 1 - x, 1 - y, 1 - c],
            "c5": lambda: full.at[both["f"], 1 - x, y, 1 - c],
            "c6": lambda: full.at[both["f"], x, 1 - y, 1 - c],
            "c7": lambda: full.at[both["f"], 1 - x, 1 - y, 1 - c],
        }[name]()

    SENDS = {
        "own_near": ("own", "near", "to_near"),
        "own_other": ("own", "one", "to_other"),
        "near_other": ("near", "two", "to_other"),
        "one_near": ("one", "one", "to_near"),
        "two_near": ("two", "two", "to_near"),
        "xn": ("on", "xn", "to_x"),
        "yn": ("on", "yn", "to_y"),
        "xo": ("own", "xo", "to_x"),
        "yo": ("own", "yo", "to_y"),
        "xp": ("near", "xn", "to_x"),
        "yp": ("near", "yn", "to_y"),
        "xf": ("of", "xf", "to_x"),
        "yf": ("of", "yf", "to_y"),
        "da": ("x_own", "da", "to_y"),
        "db": ("y_near", "db", "to_x"),
        "d_other": ("dn", "df", "to_other"),
        "d_near": ("df", "df", "to_near"),
        "c0": ("on", "c0", "to_c"),
        "c1": ("of", "c1", "to_c"),
        "c2": ("xn", "c2", "to_c"),
        "c3": ("yn", "c3", "to_c"),
        "c4": ("dn", "c4", "to_c"),
        "c5": ("xf", "c5", "to_c"),
        "c6": ("yf", "c6", "to_c"),
        "c7": ("df", "c7", "to_c"),
    }
    ARRIVES = {"da": "d_own", "db": "d_near"}
    INSIDE = ("own_other", "near_other", "one_near", "two_near", "d_other", "d_near")

    def move(self, name):
        what, called, whom = self.SENDS[name]
        piece = self.piece(what)
        return send(
            piece, piece, self.ss.at[list(self.SENDS).index(name)], self.rs.at[GATHER_GETS[called]], getattr(self.at, whom)
        )

    def go(self, *names):
        for name in names:
            if name in self.INSIDE:
                pl.when(self.at.inside)(lambda: self.move(name).start())
            else:
                self.move(name).start()

    def get(self, name, what=None):
        piece = self.piece(what or self.ARRIVES.get(name, name))
        send(piece, piece, self.ss.at[0], self.rs.at[GATHER_GETS[name]], self.at.to_c).wait_recv()

    def stage(self, s):
        a = self.at
        if s == 0:
            self.full[a.z, a.x, a.y, a.c] = self.mine()
            self.go("own_near", "own_other")
            if self.early:
                self.go("xo", "yo")
        if s == 1:
            self.get("near")
            self.go("near_other")
            if self.early:
                self.go("xp", "yp", "c0")
            else:
                self.go("xn", "yn", "c0")
        if s == 2:
            self.get("one")
            self.go("one_near")
        if s == 3:
            self.get("two")
            self.go("two_near", "xf", "yf", "c1")
        if s == 4:
            if self.early:
                self.get("xo")
                self.go("da")
                self.get("xn", "x_near")
                self.go("c2")
                self.get("yo")
                self.get("yn", "y_near")
            else:
                self.get("xn")
                self.go("da", "c2")
                self.get("yn")
            self.go("db", "c3")
        if s == 5:
            self.get("da")
            self.get("db")
            self.go("d_other", "c4")
        if s == 6:
            self.get("xf")
            self.go("c5")
            self.get("yf")
            self.go("c6")
        if s == 7:
            self.get("df")
            self.go("d_near", "c7")
        if s == 8:
            for i in range(8):
                self.get(C_NAMES[i])
        if s == 9:
            for name in self.SENDS:
                if name not in self.INSIDE + (("xn", "yn") if self.early else ("xo", "yo", "xp", "yp")):
                    self.move(name).wait_send()

            @pl.when(a.inside)
            def _():
                for name in self.INSIDE:
                    self.move(name).wait_send()


GATHER_LAGS = (0, 1, 3, 5, 5, 7, 8, 8, 9, 11)
GATHER_ORDER = (0, 2, 5, 6, 4, 7, 1, 3, 8, 9)


HEAD = 64


norm_epsilon = 1e-12
masked_score = -1000000000.0


def to_half(array):
    return array.astype(jnp.bfloat16)


def matmul(left, right):
    return jnp.dot(left, right, preferred_element_type=jnp.float32)


def matmul_nt(left, right):
    return lax.dot_general(
        left, right, (((1,), (1,)), ((), ())), preferred_element_type=jnp.float32
    )


def contract_rows(left, right):
    return lax.dot_general(
        left, right, (((0,), (0,)), ((), ())), preferred_element_type=jnp.float32
    )


def column_sums(array):
    return jnp.sum(array.astype(jnp.float32), axis=0)


def normalize(values, gain_vec, shift_vec):
    center = values - jnp.mean(values, axis=-1, keepdims=True)
    spread = jnp.mean(center * center, axis=-1, keepdims=True)
    return center * lax.rsqrt(spread + norm_epsilon) * gain_vec + shift_vec


def gelu_exact(values):
    return jax.nn.gelu(values, approximate=False)


def split_heads(block):
    return block.reshape(block.shape[0], -1, HEAD)


def row_scores(queries, key_rows, labels):
    scores = (
        jnp.einsum("qhe,khe->hqk", queries, key_rows, preferred_element_type=jnp.float32) * 0.125
    )
    allowed = labels[:, None] == labels[None, :]
    return jnp.where(allowed[None], scores, masked_score)


def attend_row(pieces):
    queries, key_rows, value_rows, labels = pieces
    scores = row_scores(split_heads(queries), split_heads(key_rows), labels)
    row_max = jnp.max(scores, axis=-1, keepdims=True)
    row_exp = jnp.exp(scores - row_max)
    row_total = jnp.sum(row_exp, axis=-1, keepdims=True)
    probs_half = to_half(row_exp / row_total)
    context = jnp.einsum(
        "hqk,khe->qhe", probs_half, split_heads(value_rows), preferred_element_type=jnp.float32
    )
    return (to_half(context.reshape(queries.shape)), (row_max + jnp.log(row_total))[..., 0])


def attend_back(pieces):
    queries, key_rows, value_rows, labels, log_total, d_context = pieces
    query_heads = split_heads(queries)
    key_heads = split_heads(key_rows)
    context_heads = split_heads(d_context)
    scores = row_scores(query_heads, key_heads, labels)
    attn_probs = jnp.exp(scores - log_total[..., None])
    d_probs = jnp.einsum(
        "qhe,khe->hqk", context_heads, split_heads(value_rows), preferred_element_type=jnp.float32
    )
    row_delta = jnp.sum(attn_probs * d_probs, axis=-1, keepdims=True)
    d_scores = to_half(attn_probs * (d_probs - row_delta))
    d_queries = (
        jnp.einsum("hqk,khe->qhe", d_scores, key_heads, preferred_element_type=jnp.float32) * 0.125
    )
    d_keys = (
        jnp.einsum("hqk,qhe->khe", d_scores, query_heads, preferred_element_type=jnp.float32)
        * 0.125
    )
    d_values = jnp.einsum(
        "hqk,qhe->khe", to_half(attn_probs), context_heads, preferred_element_type=jnp.float32
    )
    return (
        to_half(d_queries.reshape(queries.shape)),
        to_half(d_keys.reshape(queries.shape)),
        to_half(d_values.reshape(queries.shape)),
    )


def plain_device(
    tokens,
    segment,
    cotangent,
    query_w,
    key_w,
    value_w,
    attn_out_w,
    up_w,
    down_w,
    query_bias,
    value_bias,
    attn_out_bias,
    up_bias,
    down_bias,
    norm1_gain,
    norm1_shift,
    norm2_gain,
    norm2_shift,
):
    row_count = segment.shape[0]
    row_length = segment.shape[1]
    model_width = tokens.shape[1]

    def by_rows(array):
        return array.reshape(row_count, row_length, -1)

    attn_set = (
        lax.all_gather(to_half(query_w), BOTH, axis=0, tiled=True),
        lax.all_gather(to_half(key_w), BOTH, axis=0, tiled=True),
        lax.all_gather(to_half(value_w), BOTH, axis=0, tiled=True),
        lax.all_gather(to_half(attn_out_w), BOTH, axis=0, tiled=True),
        lax.all_gather(to_half(query_bias), BOTH, axis=0, tiled=True),
        lax.all_gather(to_half(value_bias), BOTH, axis=0, tiled=True),
        lax.all_gather(to_half(attn_out_bias), BOTH, axis=0, tiled=True),
        lax.all_gather(to_half(norm1_gain), BOTH, axis=0, tiled=True),
        lax.all_gather(to_half(norm1_shift), BOTH, axis=0, tiled=True),
    )
    wq_full, wk_full, wv_full, wo_full, bias_q, bias_v, bias_o, gain_one, shift_one = attn_set
    ffn_set = (
        lax.all_gather(to_half(up_w), BOTH, axis=0, tiled=True),
        lax.all_gather(to_half(down_w), BOTH, axis=1, tiled=True),
        lax.all_gather(to_half(up_bias), BOTH, axis=0, tiled=True),
        lax.all_gather(to_half(down_bias), BOTH, axis=0, tiled=True),
        lax.all_gather(to_half(norm2_gain), BOTH, axis=0, tiled=True),
        lax.all_gather(to_half(norm2_shift), BOTH, axis=0, tiled=True),
    )
    w_up, w_down, bias_up, bias_down, gain_two, shift_two = ffn_set
    queries = to_half(matmul(tokens, wq_full) + bias_q.astype(jnp.float32))
    key_rows = to_half(matmul(tokens, wk_full))
    value_rows = to_half(matmul(tokens, wv_full) + bias_v.astype(jnp.float32))
    context, log_total = lax.map(
        attend_row, (by_rows(queries), by_rows(key_rows), by_rows(value_rows), segment)
    )
    context = context.reshape(-1, model_width)
    attended = matmul(context, wo_full) + bias_o.astype(jnp.float32)
    first_sum = tokens.astype(jnp.float32) + attended
    norm_mid, pull_one = jax.vjp(
        normalize, first_sum, gain_one.astype(jnp.float32), shift_one.astype(jnp.float32)
    )
    mid_half = to_half(norm_mid)
    pre_act = matmul(mid_half, w_up) + bias_up.astype(jnp.float32)
    act_out, pull_act = jax.vjp(gelu_exact, pre_act)
    act_half = to_half(act_out)
    ffn_out = matmul(act_half, w_down) + bias_down.astype(jnp.float32)
    second_sum = mid_half.astype(jnp.float32) + ffn_out
    final, pull_two = jax.vjp(
        normalize, second_sum, gain_two.astype(jnp.float32), shift_two.astype(jnp.float32)
    )
    outputs = to_half(final)
    valid = (segment.reshape(-1) >= 0).astype(jnp.float32)[:, None]
    d_out = cotangent.astype(jnp.float32) * valid
    d_second, d_gain_two, d_shift_two = pull_two(d_out)
    up_back, down_back = (
        lax.all_gather(to_half(up_w), BOTH, axis=0, tiled=True),
        lax.all_gather(to_half(down_w), BOTH, axis=1, tiled=True),
    )
    d_ffn = to_half(d_second)
    d_down_turned = contract_rows(d_ffn, act_half)
    d_down_bias = column_sums(d_ffn)
    (d_pre,) = pull_act(matmul_nt(d_ffn, down_back))
    d_pre_half = to_half(d_pre)
    d_up_w = contract_rows(mid_half, d_pre_half)
    d_up_bias = column_sums(d_pre_half)
    d_mid = d_second + matmul_nt(d_pre_half, up_back)
    d_first, d_gain_one, d_shift_one = pull_one(d_mid)
    wq_back, wk_back, wv_back, wo_back = (
        lax.all_gather(to_half(query_w), BOTH, axis=0, tiled=True),
        lax.all_gather(to_half(key_w), BOTH, axis=0, tiled=True),
        lax.all_gather(to_half(value_w), BOTH, axis=0, tiled=True),
        lax.all_gather(to_half(attn_out_w), BOTH, axis=0, tiled=True),
    )
    d_att = to_half(d_first)
    d_attn_out_w = contract_rows(context, d_att)
    d_attn_out_bias = column_sums(d_att)
    d_context = to_half(matmul_nt(d_att, wo_back))
    d_queries, d_keys, d_values = lax.map(
        attend_back,
        (
            by_rows(queries),
            by_rows(key_rows),
            by_rows(value_rows),
            segment,
            log_total,
            by_rows(d_context),
        ),
    )
    d_queries = d_queries.reshape(-1, model_width)
    d_keys = d_keys.reshape(-1, model_width)
    d_values = d_values.reshape(-1, model_width)
    d_query_w = contract_rows(tokens, d_queries)
    d_key_w = contract_rows(tokens, d_keys)
    d_value_w = contract_rows(tokens, d_values)
    d_query_bias = column_sums(d_queries)
    d_value_bias = column_sums(d_values)
    d_tokens = (
        d_first
        + matmul_nt(d_queries, wq_back)
        + matmul_nt(d_keys, wk_back)
        + matmul_nt(d_values, wv_back)
    )
    members = (
        d_query_w,
        d_key_w,
        d_value_w,
        d_attn_out_w,
        d_up_w,
        d_down_turned,
        d_query_bias,
        d_value_bias,
        d_attn_out_bias,
        d_up_bias,
        d_down_bias,
        d_gain_one,
        d_shift_one,
        d_gain_two,
        d_shift_two,
    )
    block_sums = (
        lax.psum_scatter(
            members[0].astype(jnp.bfloat16), DP, scatter_dimension=0, tiled=True
        ).astype(jnp.float32),
        lax.psum_scatter(
            members[1].astype(jnp.bfloat16), DP, scatter_dimension=0, tiled=True
        ).astype(jnp.float32),
        lax.psum_scatter(
            members[2].astype(jnp.bfloat16), DP, scatter_dimension=0, tiled=True
        ).astype(jnp.float32),
        lax.psum_scatter(
            members[3].astype(jnp.bfloat16), DP, scatter_dimension=0, tiled=True
        ).astype(jnp.float32),
        lax.psum_scatter(
            members[4].astype(jnp.bfloat16), DP, scatter_dimension=0, tiled=True
        ).astype(jnp.float32),
        lax.psum_scatter(
            members[5].astype(jnp.bfloat16), DP, scatter_dimension=0, tiled=True
        ).astype(jnp.float32),
        lax.psum_scatter(
            members[6].astype(jnp.bfloat16), DP, scatter_dimension=0, tiled=True
        ).astype(jnp.float32),
        lax.psum_scatter(
            members[7].astype(jnp.bfloat16), DP, scatter_dimension=0, tiled=True
        ).astype(jnp.float32),
        lax.psum_scatter(
            members[8].astype(jnp.bfloat16), DP, scatter_dimension=0, tiled=True
        ).astype(jnp.float32),
        lax.psum_scatter(
            members[9].astype(jnp.bfloat16), DP, scatter_dimension=0, tiled=True
        ).astype(jnp.float32),
        lax.psum_scatter(
            members[10].astype(jnp.bfloat16), DP, scatter_dimension=0, tiled=True
        ).astype(jnp.float32),
        lax.psum_scatter(
            members[11].astype(jnp.bfloat16), DP, scatter_dimension=0, tiled=True
        ).astype(jnp.float32),
        lax.psum_scatter(
            members[12].astype(jnp.bfloat16), DP, scatter_dimension=0, tiled=True
        ).astype(jnp.float32),
        lax.psum_scatter(
            members[13].astype(jnp.bfloat16), DP, scatter_dimension=0, tiled=True
        ).astype(jnp.float32),
        lax.psum_scatter(
            members[14].astype(jnp.bfloat16), DP, scatter_dimension=0, tiled=True
        ).astype(jnp.float32),
    )
    every_shard = (
        lax.psum_scatter(
            block_sums[0].astype(jnp.bfloat16), FSDP, scatter_dimension=0, tiled=True
        ).astype(jnp.float32),
        lax.psum_scatter(
            block_sums[1].astype(jnp.bfloat16), FSDP, scatter_dimension=0, tiled=True
        ).astype(jnp.float32),
        lax.psum_scatter(
            block_sums[2].astype(jnp.bfloat16), FSDP, scatter_dimension=0, tiled=True
        ).astype(jnp.float32),
        lax.psum_scatter(
            block_sums[3].astype(jnp.bfloat16), FSDP, scatter_dimension=0, tiled=True
        ).astype(jnp.float32),
        lax.psum_scatter(
            block_sums[4].astype(jnp.bfloat16), FSDP, scatter_dimension=0, tiled=True
        ).astype(jnp.float32),
        lax.psum_scatter(
            block_sums[5].astype(jnp.bfloat16), FSDP, scatter_dimension=0, tiled=True
        ).astype(jnp.float32),
        lax.psum_scatter(
            block_sums[6].astype(jnp.bfloat16), FSDP, scatter_dimension=0, tiled=True
        ).astype(jnp.float32),
        lax.psum_scatter(
            block_sums[7].astype(jnp.bfloat16), FSDP, scatter_dimension=0, tiled=True
        ).astype(jnp.float32),
        lax.psum_scatter(
            block_sums[8].astype(jnp.bfloat16), FSDP, scatter_dimension=0, tiled=True
        ).astype(jnp.float32),
        lax.psum_scatter(
            block_sums[9].astype(jnp.bfloat16), FSDP, scatter_dimension=0, tiled=True
        ).astype(jnp.float32),
        lax.psum_scatter(
            block_sums[10].astype(jnp.bfloat16), FSDP, scatter_dimension=0, tiled=True
        ).astype(jnp.float32),
        lax.psum_scatter(
            block_sums[11].astype(jnp.bfloat16), FSDP, scatter_dimension=0, tiled=True
        ).astype(jnp.float32),
        lax.psum_scatter(
            block_sums[12].astype(jnp.bfloat16), FSDP, scatter_dimension=0, tiled=True
        ).astype(jnp.float32),
        lax.psum_scatter(
            block_sums[13].astype(jnp.bfloat16), FSDP, scatter_dimension=0, tiled=True
        ).astype(jnp.float32),
        lax.psum_scatter(
            block_sums[14].astype(jnp.bfloat16), FSDP, scatter_dimension=0, tiled=True
        ).astype(jnp.float32),
    )
    (
        shard_qw,
        shard_kw,
        shard_vw,
        shard_ow,
        shard_uw,
        shard_turned,
        shard_qb,
        shard_vb,
        shard_ob,
        shard_ub,
        shard_db,
        shard_g1,
        shard_s1,
        shard_g2,
        shard_s2,
    ) = every_shard
    shard_dw = jnp.transpose(shard_turned)
    return (
        outputs,
        d_tokens,
        shard_qw,
        shard_kw,
        shard_vw,
        shard_ow,
        shard_uw,
        shard_dw,
        shard_qb,
        shard_vb,
        shard_ob,
        shard_ub,
        shard_db,
        shard_g1,
        shard_s1,
        shard_g2,
        shard_s2,
    )


ATTN = 4
LANES = 128
SIDE = 1024
V_LANE, R_LANE = 32, 64


def aligned(start, size, step=None):
    return pl.ds(pl.multiple_of(start, step or size), size)


def side_loop(count, body):
    def step(i, carry):
        body(i)
        return carry

    lax.fori_loop(0, count, step, 0)


def square(full, b):
    size = full.shape[-1]
    return full.at[b].reshape(size, size)


def spread_vectors(tiles, short_ref, up_ref, depth):
    for dp in range(2 * depth):
        total = jnp.zeros((16, LANES), jnp.float32)
        for fs in range(4):
            total = total + tiles[dp // 2, dp % 2, fs // 2, fs % 2].astype(jnp.float32)
        short_ref[:, dp * LANES : (dp + 1) * LANES] = total[:8]
        for fs in range(4):
            at = (dp * 4 + fs) * LANES
            up_ref[:, at : at + LANES] = total[8 + fs : 9 + fs]


def stepwise(body, after):
    def step(i):
        body(i)
        for k, follow in enumerate(after):
            pl.when(i == k)(follow)

    side_loop(len(after), step)


def nothing():
    pass


def attend_pairs(first, last, qkvc, lse, mask):
    length = mask.shape[0]

    def pair(p):
        lanes = aligned(p * LANES, LANES)
        q, k, v = qkvc[0, :, lanes], qkvc[1, :, lanes], qkvc[2, :, lanes]
        lane = lax.broadcasted_iota(jnp.int32, (length, LANES), 1)
        lower = lane < HEAD
        total = jnp.zeros((length, LANES), jnp.float32)
        logs = lse[...]
        for h in range(2):
            here = lower if h == 0 else jnp.logical_not(lower)
            key = jnp.where(here, k, jnp.zeros_like(k))
            scores = matmul_nt(q, key) + mask[...]
            row_max = jnp.max(scores, axis=-1, keepdims=True)
            row_exp = jnp.exp(scores - row_max)
            row_total = jnp.sum(row_exp, axis=-1, keepdims=True)
            part = matmul(to_half(row_exp), v) / row_total
            total = jnp.where(here, part, total)
            logs = jnp.where(lane == 2 * p + h, row_max + jnp.log(row_total), logs)
        qkvc[3, :, lanes] = to_half(total)
        lse[...] = logs

    def step(i, carry):
        pair(i)
        return carry

    lax.fori_loop(first, last, step, 0)


SUM_SENDS = numbered("c", "df", "dg", "da", "db", "xn", "yn", "xf", "yf", "f", "m", "n")
SUM_LAGS = (0, 1, 2, 3, 4, 3, 5, 6, 7)
SUM_ORDER = (6, 1, 2, 3, 4, 5, 7, 8, 0)
SUM_BUFFERS = {
    "grad": (2, (4, 2, 2, 2)),
    "held": (7, (4, 2, 2)),
    "c": (2, (4, 2, 2)),
    "df": (7, (2,)),
    "dg": (4, (2,)),
    "da": (4, ()),
    "db": (4, ()),
    "xn": (5, (2,)),
    "yn": (4, (2,)),
    "xf": (5, (2,)),
    "yf": (5, (2,)),
    "f": (5, (2,)),
    "m": (4, (2,)),
    "n": (4, ()),
}


def sum_scratch(rows, cols, blocks, names):
    bufs = [SUM_BUFFERS[name] for name in names]
    bufs = [pltpu.VMEM((min(slots, blocks),) + parts + (rows, cols), jnp.bfloat16) for slots, parts in bufs]
    return bufs + [pltpu.SemaphoreType.DMA((blocks, len(SUM_SENDS)))] * 2


class SumBlock:
    def __init__(self, at, refs, names, b, **others):
        self.at = at
        *bufs, ss, rs = refs
        self.ss, self.rs = ss.at[b], rs.at[b]
        self.buf = {n: ref.at[b % ref.shape[0]] for n, ref in zip(names, bufs)} | others

    def move(self, name):
        a, held = self.at, self.buf["held"]
        x, y = a.x, a.y
        every, both = pl.ds(0, 4), pl.ds(0, 2)
        src, to = {
            "c": lambda: (self.buf["grad"].at[every, both, both, 1 - a.c], a.to_c),
            "df": lambda: (held.at[a.far_pair, 1 - x, 1 - y], a.to_near),
            "dg": lambda: (held.at[a.far_pair, 1 - x, 1 - y], a.to_other),
            "da": lambda: (held.at[a.z, 1 - x, 1 - y], a.to_y),
            "db": lambda: (held.at[a.near, 1 - x, 1 - y], a.to_x),
            "xn": lambda: (held.at[a.near_pair, 1 - x, y], a.to_x),
            "yn": lambda: (held.at[a.near_pair, x, 1 - y], a.to_y),
            "xf": lambda: (held.at[a.far_pair, 1 - x, y], a.to_x),
            "yf": lambda: (held.at[a.far_pair, x, 1 - y], a.to_y),
            "f": lambda: (held.at[a.far_pair, x, y], a.to_near),
            "m": lambda: (held.at[a.far_pair, x, y], a.to_other),
            "n": lambda: (held.at[a.near, x, y], a.to_near),
        }[name]()
        i = SUM_SENDS[name]
        return send(src, self.buf[name], self.ss.at[i], self.rs.at[i], to)

    def start(self, name):
        self.move(name).start()

    def got(self, name):
        self.move(name).wait_recv()
        return self.buf[name]

    def stage(self, s, out=None):
        a, held, grad = self.at, self.buf["held"], self.buf["grad"]
        x, y, c = a.x, a.y, a.c
        inside = a.inside
        outside = jnp.logical_not(inside)

        def add(first, xx, yy, *others, count=2):
            for i in range(count):
                total = held[first + i, xx, yy].astype(jnp.float32)
                for other in others:
                    total = total + (other[i] if count == 2 else other[...]).astype(jnp.float32)
                held[first + i, xx, yy] = total.astype(jnp.bfloat16)

        if s == 0:
            self.start("c")
        if s == 1:
            self.move("c").wait()
            pair = self.buf["c"]

            def join(first, xx, yy):
                for i in range(2):
                    held[first + i, xx, yy] = grad[first + i, xx, yy, c] + pair[first + i, xx, yy]

            join(a.high, 1 - x, 1 - y)
            pl.when(outside)(lambda: self.start("df"))
            join(a.high, 1 - x, y)
            self.start("xf")
            join(a.high, x, 1 - y)
            self.start("yf")
            join(a.low, 1 - x, 1 - y)
            join(a.low, 1 - x, y)
            join(a.low, x, 1 - y)
            join(a.high, x, y)
            join(a.low, x, y)
        if s == 2:

            @pl.when(inside)
            def _():
                add(a.high, 1 - x, 1 - y, self.got("df"))
                self.start("dg")

        if s == 3:

            @pl.when(inside)
            def _():
                add(a.low, 1 - x, 1 - y, self.got("dg"))

            self.start("da")
            self.start("db")
        if s == 4:
            add(a.z, 1 - x, y, self.got("da"), count=1)
            self.start("xn")
            add(a.near, x, 1 - y, self.got("db"), count=1)
            self.start("yn")
        if s == 5:
            add(a.high, x, y, self.got("xf"), self.got("yf"))
            pl.when(outside)(lambda: self.start("f"))
        if s == 6:

            @pl.when(inside)
            def _():
                add(a.high, x, y, self.got("f"))
                self.start("m")

        if s == 7:
            add(a.low, x, y, self.got("xn"), self.got("yn"))

            @pl.when(inside)
            def _():
                add(a.low, x, y, self.got("m"))

            self.start("n")
        if s == 8:
            out[...] = held[a.z, x, y].astype(jnp.float32) + self.got("n")[...].astype(jnp.float32)
            for name in ("da", "db", "xn", "yn", "xf", "yf", "n"):
                self.move(name).wait_send()

            @pl.when(inside)
            def _():
                self.move("dg").wait_send()
                self.move("m").wait_send()

            @pl.when(outside)
            def _():
                self.move("df").wait_send()
                self.move("f").wait_send()


def attend_back_pairs(first, last, qkvc, lse, delta, mask, grads):
    length = mask.shape[0]

    def pair(p, carry):
        lanes = aligned(p * LANES, LANES)
        q, k, v, d_context = qkvc[0, :, lanes], qkvc[1, :, lanes], qkvc[2, :, lanes], grads[3, :, lanes]
        lower = lax.broadcasted_iota(jnp.int32, (length, LANES), 1) < HEAD
        sums = [jnp.zeros((length, LANES), jnp.float32) for _ in range(3)]
        for h in range(2):
            here = lower if h == 0 else jnp.logical_not(lower)
            row = pl.ds(2 * p + h, 1)
            key = jnp.where(here, k, jnp.zeros_like(k))
            value = jnp.where(here, v, jnp.zeros_like(v))
            probs = jnp.exp(matmul_nt(key, q) + mask[...] - lse[row, :])
            d_scores = to_half(probs * (matmul_nt(value, d_context) - delta[row, :]))
            parts = (
                contract_rows(d_scores, k) * 0.125,
                matmul(d_scores, q),
                matmul(to_half(probs), d_context),
            )
            sums = [jnp.where(here, part, total) for part, total in zip(parts, sums)]
        for i in range(3):
            grads[i, :, lanes] = to_half(sums[i])
        return carry

    lax.fori_loop(first, last, pair, 0)


SUM_NAMES = tuple(SUM_BUFFERS)
LENT = SUM_NAMES[:2]
OWN_BUFFERS = SUM_NAMES[2:]


def layer_kernel(depth, *refs):
    tokens_hbm, segment, cotangent_hbm, wq, wk, wv, wo, up_w, down_w, *vectors = refs[:18]
    out_hbm, dtok_hbm, gq, gk, gv, go, gup, gdown, gshort, gup_bias = refs[18:28]
    (
        full, tiles, mine_vec, short, up_bias, qkvc, lse, lse_turned, mask, mid, act, dge, nhat, total, half,
        turn_a, delta_turned, cotangent, vgrads, tile_sum, spare, staged, ss, rs, isem, osem, *rest,
    ) = refs[28:]
    count = len(OWN_BUFFERS) + 2
    big, vec = rest[:count], rest[count:]
    length, width = mid.shape
    tokens = mid
    here = Place()
    fs = here.fs
    rows = wq.shape[0]
    f32 = jnp.float32

    shards = [wq, wk, wv, wo]
    for wide in (up_w, down_w):
        shards += [wide.at[:, i * width : (i + 1) * width] for i in range(ATTN)]
    loads = [
        pltpu.make_async_copy(src, total.at[i * rows : (i + 1) * rows], isem.at[i]) for i, src in enumerate(shards)
    ]
    loads.append(pltpu.make_async_copy(tokens_hbm, tokens, isem.at[BLOCKS]))
    loads.append(pltpu.make_async_copy(cotangent_hbm, cotangent, isem.at[BLOCKS + 1]))
    for load in loads:
        load.start()
    greet(here)

    mine_vec[...] = jnp.zeros_like(mine_vec)
    for i in range(8):
        mine_vec[i : i + 1, 0:rows] = vectors[i][...]
    placed = pltpu.roll(mine_vec[...], fs * rows, 1)
    row_at = lax.broadcasted_iota(jnp.int32, (16, LANES), 0)
    mine_vec[...] = jnp.where(row_at == 8 + fs, jnp.broadcast_to(vectors[8][...], (16, LANES)), placed)

    def own(b):
        loads[b].wait()
        return to_half(total[b * rows : (b + 1) * rows, :])

    def gather_block(b):
        return GatherBlock(here, full.at[b], lambda: own(b), ss.at[b], rs.at[b], b < 2)

    own_tiles = GatherBlock(here, tiles, lambda: to_half(mine_vec[...]), ss.at[BLOCKS], rs.at[BLOCKS])

    def gather_pump(t):
        for s in GATHER_ORDER:
            b = t - GATHER_LAGS[s]
            if 0 <= b < BLOCKS:
                gather_block(b).stage(s)
            if b == 0:
                own_tiles.stage(s)

    gather_pump(0)
    gather_pump(1)
    labels = segment[...].astype(jnp.float32)
    turned = jnp.transpose(jnp.broadcast_to(labels, (LANES, length)))
    mask[...] = jnp.where(turned[:, :1] == labels, 0.0, masked_score)
    lse[...] = jnp.where(turned >= 0.0, 1.0, 0.0)
    ready = GATHER_LAGS[8]
    for t in range(2, ready + 1):
        gather_pump(t)
    spread_vectors(tiles, short, up_bias, depth)
    loads[BLOCKS].wait()

    def project(i):
        biased = jnp.where(i == 1, 0.0, 1.0)
        scale = jnp.where(i == 0, 0.125, 1.0)
        bias = short[pl.ds(i // 2, 1), :] * biased
        qkvc[i] = to_half(to_half(matmul(tokens[...], square(full, i)[...]) + bias).astype(f32) * scale)

    stepwise(project, [lambda: gather_pump(ready + 1), lambda: gather_pump(ready + 2), nothing])
    stepwise(
        lambda i: attend_pairs(i * 4, i * 4 + 4, qkvc, lse, mask),
        [lambda: gather_pump(ready + 3), nothing],
    )
    lse_turned[...] = jnp.transpose(lse[...])[: lse_turned.shape[0]]
    gather_pump(ready + 4)

    wo_full = square(full, 3)

    def attended(n):
        cols = aligned(n * SIDE, SIDE)
        total[:, cols] = (
            matmul(qkvc[3], wo_full[:, cols]) + short[2:3, cols] + tokens[:, cols].astype(jnp.float32)
        )

    side_loop(width // SIDE, attended)

    lane_at = lax.broadcasted_iota(jnp.int32, (LANES, LANES), 1)

    def first_norm(i):
        at = aligned(i * LANES, LANES)
        values = total[at, :]
        center = values - jnp.mean(values, axis=-1, keepdims=True)
        spread = jnp.mean(center * center, axis=-1, keepdims=True)
        r = lax.rsqrt(spread + norm_epsilon)
        unit = center * r
        nhat[at, :] = to_half(unit)
        lse[at, :] = jnp.where(lane_at >= R_LANE, r, lse[at, :])
        mid[at, :] = to_half(unit * short[4:5, :] + short[5:6, :])

    side_loop(length // LANES, first_norm)

    def activate(j):
        weight = square(full, ATTN + j)
        for part in range(2):
            cols = slice(part * width // 2, (part + 1) * width // 2)
            pre = matmul(mid[...], weight[:, cols]) + up_bias[:, aligned(j * width + part * width // 2, width // 2)]
            cdf = 0.5 * (1.0 + lax.erf(pre * 0.7071067811865476))
            act[j, :, cols] = to_half(pre * cdf)
            pdf = jnp.exp(-0.5 * pre * pre) * 0.3989422804014327
            dge[j, :, cols] = to_half(cdf + pre * pdf)

    def contract(j):
        total[...] = total[...] + matmul_nt(act[j], square(full, 2 * ATTN + j)[...])

    gather_pump(ready + 5)
    stepwise(activate, [lambda: gather_pump(ready + 6), lambda: gather_pump(ready + 7), lambda: gather_pump(ready + 8), nothing])
    total[...] = mid[...].astype(f32) + short[3:4, :]
    stepwise(contract, [lambda: gather_pump(ready + 9), lambda: gather_pump(ready + 10), lambda: gather_pump(ready + 11), nothing])

    loads[BLOCKS + 1].wait()
    vgrads[...] = jnp.zeros_like(vgrads)

    def second_norm(i):
        at = aligned(i * LANES, LANES)
        values = total[at, :]
        center = values - jnp.mean(values, axis=-1, keepdims=True)
        spread = jnp.mean(center * center, axis=-1, keepdims=True)
        r = lax.rsqrt(spread + norm_epsilon)
        unit = center * r
        gain = short[6:7, :]
        final = to_half(unit * gain + short[7:8, :])
        e = cotangent[at, :].astype(jnp.float32) * lse[at, V_LANE : V_LANE + 1]
        cotangent[at, :] = final
        vgrads[6:7, :] = vgrads[6:7, :] + jnp.sum(e * unit, axis=0, keepdims=True)
        vgrads[7:8, :] = vgrads[7:8, :] + jnp.sum(e, axis=0, keepdims=True)
        eg = e * gain
        d = r * (
            eg - jnp.mean(eg, axis=-1, keepdims=True) - unit * jnp.mean(eg * unit, axis=-1, keepdims=True)
        )
        total[at, :] = d
        half[at, :] = to_half(d)
        vgrads[3:4, :] = vgrads[3:4, :] + jnp.sum(to_half(d).astype(jnp.float32), axis=0, keepdims=True)

    side_loop(length // LANES, second_norm)
    pltpu.make_async_copy(cotangent, out_hbm, osem.at[0]).start()

    outs = [gdown.at[:, i * width : (i + 1) * width] for i in range(4)]
    outs += [gup.at[:, i * width : (i + 1) * width] for i in range(4)] + [go, gv, gk, gq]

    held_at = [(4, 0), (4, 1), (9, 0), (9, 1), (5, 0), (5, 1), (10, 0)]

    def grad_of(b):
        return spare.at[b % 2]

    def block(b):
        gathered, half_at = held_at[b % len(held_at)]
        lent = dict(zip(LENT, (grad_of(b), full.at[gathered, :, :, :, half_at])))
        return SumBlock(here, big, OWN_BUFFERS, b, **lent)

    vblock = SumBlock(here, vec, SUM_NAMES, 0)
    turn_b = square(full, 6).at[:, 0:length]

    def leave(b):
        return pltpu.make_async_copy(staged.at[b % 2], outs[b], osem.at[2 + b % 2])

    def pump(t):
        for s in SUM_ORDER:
            b = t - SUM_LAGS[s]
            if 0 <= b < BLOCKS:
                if s == 8 and b > 1:
                    leave(b - 2).wait()
                block(b).stage(s, staged.at[b % 2])
                if s == 8:
                    leave(b).start()
            if b == BLOCKS - 1:
                vblock.stage(s, tile_sum)

    def weight_grad(b, left, right):
        grad = grad_of(b)
        for part in range(2):
            got = to_half(matmul(left[part * width // 2 : (part + 1) * width // 2, :], right[...]))
            grad[2 * part : 2 * part + 2] = got.reshape((2,) + grad.shape[1:])

    def sums_of(values):
        return jnp.sum(values.astype(f32), axis=0, keepdims=True)

    turn_a[...] = jnp.transpose(half[...])
    weight_grad(0, turn_a, act.at[0])
    pump(0)
    for t in range(ready + 12, BLOCKS + max(GATHER_LAGS)):
        gather_pump(t)

    up_grads = up_bias

    def units_back(j):
        d_pre = to_half(matmul(half[...], square(full, 2 * ATTN + j)[...]) * dge[j].astype(f32))
        dge[j] = d_pre
        up_grads[:, aligned(j * width, width)] = sums_of(d_pre)
        add_product(dge.at[j], square(full, ATTN + j))

        @pl.when(j < ATTN - 1)
        def _():
            weight_grad(j + 1, turn_a, act.at[j + 1])

    def add_product(left, weight):
        total[...] = total[...] + matmul_nt(left[...], weight[...])

    stepwise(units_back, [lambda: pump(1), lambda: pump(2), lambda: pump(3), nothing])
    turn_b[...] = jnp.transpose(mid[...])
    loads[BLOCKS].start()
    weight_grad(4, turn_b, dge.at[0])
    pump(4)


    def first_norm_back(i):
        at = aligned(i * LANES, LANES)
        e = total[at, :]
        unit = nhat[at, :].astype(f32)
        vgrads[4:5, :] = vgrads[4:5, :] + jnp.sum(e * unit, axis=0, keepdims=True)
        vgrads[5:6, :] = vgrads[5:6, :] + jnp.sum(e, axis=0, keepdims=True)
        eg = e * short[4:5, :]
        d = lse[at, R_LANE : R_LANE + 1] * (
            eg - jnp.mean(eg, axis=-1, keepdims=True) - unit * jnp.mean(eg * unit, axis=-1, keepdims=True)
        )
        total[at, :] = d
        d_half = to_half(d)
        half[at, :] = d_half
        vgrads[2:3, :] = vgrads[2:3, :] + jnp.sum(d_half.astype(f32), axis=0, keepdims=True)

    side_loop(length // LANES, first_norm_back)
    wo_full = square(full, 3)
    delta = lse

    def context_back(n):
        cols = aligned(n * SIDE, SIDE)
        d_context = to_half(matmul_nt(half[...], wo_full[cols, :]))
        act[3, :, cols] = d_context
        product = d_context.astype(f32) * qkvc[3, :, cols].astype(f32)
        lane = lax.broadcasted_iota(jnp.int32, (length, LANES), 1)
        got = delta[...]
        for i in range(SIDE // HEAD):
            two = product[:, (i // 2) * LANES : (i // 2 + 1) * LANES]
            here = lane // HEAD == i % 2
            head = jnp.sum(jnp.where(here, two, 0.0), axis=-1, keepdims=True)
            got = jnp.where(lane == n * (SIDE // HEAD) + i, head, got)
        delta[...] = got

    side_loop(width // SIDE, context_back)
    delta_turned[...] = jnp.transpose(delta[...])[: delta_turned.shape[0]]
    weight_grad(5, turn_b, dge.at[1])
    pump(5)

    def attention_step(i):
        attend_back_pairs(3 * i, jnp.minimum(3 * i + 3, 8), qkvc, lse_turned, delta_turned, mask, act)

        @pl.when(i < 2)
        def _():
            weight_grad(6 + i, turn_b, dge.at[2 + i])

    stepwise(attention_step, [lambda: pump(6), lambda: pump(7), nothing])
    turn_a[...] = jnp.transpose(qkvc[3])
    weight_grad(8, turn_a, half)
    pump(8)
    loads[BLOCKS].wait()
    turn_b[...] = jnp.transpose(tokens[...])

    def place_vectors():
        vgrads[0:1, :] = sums_of(act[0])
        vgrads[1:2, :] = sums_of(act[2])
        for dp in range(2 * depth):
            for fsdp in range(4):
                at = (dp * 4 + fsdp) * LANES
                vec[0][0, dp // 2, dp % 2, fsdp // 2, fsdp % 2] = to_half(
                    jnp.concatenate(
                        [
                            vgrads[:, dp * LANES : (dp + 1) * LANES],
                            jnp.broadcast_to(up_grads[:, at : at + LANES], (8, LANES)),
                        ],
                        axis=0,
                    )
                )

    def middle_pump():
        pump(9)
        place_vectors()

    stepwise(
        lambda i: weight_grad(9 + i, turn_b, act.at[2 - i]), [middle_pump, lambda: pump(10), lambda: pump(11)]
    )

    def hand_back():
        pltpu.make_async_copy(total, dtok_hbm, osem.at[1]).start()
        pump(14)

    stepwise(
        lambda i: add_product(act.at[2 - i], square(full, 2 - i)), [lambda: pump(12), lambda: pump(13), hand_back]
    )
    for t in range(15, BLOCKS + max(SUM_LAGS)):
        pump(t)
    leave(BLOCKS - 2).wait()
    leave(BLOCKS - 1).wait()
    moved = pltpu.roll(tile_sum[...], (4 - fs) * rows % LANES, 1)
    gshort[...] = moved[:8]
    gup_bias[...] = tile_sum[8:9, :]
    pltpu.make_async_copy(total, dtok_hbm, osem.at[1]).wait()
    pltpu.make_async_copy(cotangent, out_hbm, osem.at[0]).wait()


def layer_call(depth, tokens, segment, cotangent, weights, vectors):
    length, width = tokens.shape
    rows = weights[0].shape[0]
    dims = (depth, 2, 2, 2)
    bf, f32 = jnp.bfloat16, jnp.float32
    part = ((rows, width), f32)
    shapes = [
        ((length, width), bf), ((length, width), f32), part, part, part, part, ((rows, ATTN * width), f32),
        ((rows, ATTN * width), f32), ((8, LANES), f32), ((1, LANES), f32),
    ]
    vmem, hbm = pl.BlockSpec(memory_space=pltpu.VMEM), pl.BlockSpec(memory_space=pl.ANY)
    scratch = [
        pltpu.VMEM((BLOCKS,) + dims + (rows, width), bf),
        pltpu.VMEM(dims + (16, LANES), bf),
        pltpu.VMEM((16, LANES), f32),
        pltpu.VMEM((8, width), f32),
        pltpu.VMEM((1, ATTN * width), f32),
        pltpu.VMEM((4, length, width), bf),
        pltpu.VMEM((length, LANES), f32),
        pltpu.VMEM((width // HEAD, length), f32),
        pltpu.VMEM((length, length), f32),
        pltpu.VMEM((length, width), bf),
        pltpu.VMEM((ATTN, length, width), bf),
        pltpu.VMEM((ATTN, length, width), bf),
        pltpu.VMEM((length, width), bf),
        pltpu.VMEM((length, width), f32),
        pltpu.VMEM((length, width), bf),
        pltpu.VMEM((width, length), bf),
        pltpu.VMEM((width // HEAD, length), f32),
        pltpu.VMEM((length, width), bf),
        pltpu.VMEM((8, width), f32),
        pltpu.VMEM((16, LANES), f32),
        pltpu.VMEM((2,) + dims + (rows, width), bf),
        pltpu.VMEM((2, rows, width), f32),
        pltpu.SemaphoreType.DMA((BLOCKS + 1, len(GatherBlock.SENDS))),
        pltpu.SemaphoreType.DMA((BLOCKS + 1, len(GATHER_GETS))),
        pltpu.SemaphoreType.DMA((BLOCKS + 2,)),
        pltpu.SemaphoreType.DMA((4,)),
    ]
    scratch += sum_scratch(rows, width, BLOCKS, OWN_BUFFERS) + sum_scratch(16, LANES, 1, SUM_NAMES)
    return pl.pallas_call(
        functools.partial(layer_kernel, depth),
        out_shape=tuple(jax.ShapeDtypeStruct(*s) for s in shapes),
        in_specs=[hbm, vmem, hbm] + [hbm] * 6 + [vmem] * 9,
        out_specs=tuple([hbm] * 8 + [vmem] * 2),
        scratch_shapes=scratch,
        compiler_params=pltpu.CompilerParams(
            collective_id=0, has_side_effects=True, vmem_limit_bytes=63 * 2**20
        ),
        name="layer",
    )(tokens, segment, cotangent, *weights, *vectors)


PIECE = 1024


def results_kernel(large, short, *refs):
    sources, targets, vectors = refs[:large], refs[large + 2 : 2 * large + 2], refs[2 * large + 2 : 2 * large + 11]
    rows, up = refs[large : large + 2]
    held, (came, gone) = refs[2 * large + 11 : -2], refs[-2:]
    ins, outs = [], []
    for src, mid, dst in zip(sources, held, targets):
        for start in range(0, src.shape[0], PIECE):
            at = pl.ds(start, min(PIECE, src.shape[0]))
            i = len(ins)
            ins.append(pltpu.make_async_copy(src.at[at], mid.at[at], came.at[i]))
            outs.append(pltpu.make_async_copy(mid.at[at], dst.at[at], gone.at[i]))
    for copy in ins:
        copy.start()
    for i in range(8):
        vectors[i][...] = rows[i : i + 1, 0:short]
    vectors[8][...] = up[...]
    for copy, onward in zip(ins, outs):
        copy.wait()
        onward.start()
    for copy in outs:
        copy.wait()


def results_call(large, rows, up, short):
    vmem, hbm = pl.BlockSpec(memory_space=pltpu.VMEM), pl.BlockSpec(memory_space=pl.ANY)
    shapes = [jax.ShapeDtypeStruct(a.shape, a.dtype) for a in large]
    shapes += [jax.ShapeDtypeStruct((1, short), jnp.float32)] * 8 + [jax.ShapeDtypeStruct(up.shape, jnp.float32)]
    return pl.pallas_call(
        functools.partial(results_kernel, len(large), short),
        out_shape=tuple(shapes),
        in_specs=[hbm] * len(large) + [vmem] * 2,
        out_specs=tuple([hbm] * len(large) + [vmem] * 9),
        scratch_shapes=[pltpu.VMEM(a.shape, a.dtype) for a in large]
        + [pltpu.SemaphoreType.DMA((sum(-(-a.shape[0] // PIECE) for a in large),))] * 2,
        name="results",
    )(*large, rows, up)


def kernel_device(
    tokens, segment, cotangent, query_w, key_w, value_w, attn_out_w, up_w, down_w, query_bias, value_bias,
    attn_out_bias, up_bias, down_bias, norm1_gain, norm1_shift, norm2_gain, norm2_shift,
):
    depth = lax.axis_size(DP) // 2
    weights = (query_w, key_w, value_w, attn_out_w, up_w, jnp.transpose(down_w))
    vectors = (
        query_bias, value_bias, attn_out_bias, down_bias, norm1_gain, norm1_shift, norm2_gain, norm2_shift, up_bias,
    )
    outputs, d_tokens, qw, kw, vw, ow, uw, dw, short_sum, up_sum = layer_call(
        depth, tokens, segment, cotangent, weights, [vector[None] for vector in vectors]
    )
    outputs, d_tokens, qw, kw, vw, ow, uw, dw, *vectors = results_call(
        (outputs, d_tokens, qw, kw, vw, ow, uw, dw), short_sum, up_sum, query_w.shape[0]
    )
    qb, vb, ob, db, g1, s1, g2, s2, ub = [vector.reshape(-1) for vector in vectors]
    return (
        outputs, d_tokens, qw, kw, vw, ow, uw, jnp.transpose(dw), qb, vb, ob, ub, db, g1, s1, g2, s2,
    )


def solution(mesh):
    fits = mesh.shape[FSDP] == 4 and mesh.shape[DP] == 8
    body = kernel_device if fits else plain_device
    in_specs = (
        P(BOTH, None),
        P(BOTH, None),
        P(BOTH, None),
        P(BOTH, None),
        P(BOTH, None),
        P(BOTH, None),
        P(BOTH, None),
        P(BOTH, None),
        P(None, BOTH),
        P(BOTH),
        P(BOTH),
        P(BOTH),
        P(BOTH),
        P(BOTH),
        P(BOTH),
        P(BOTH),
        P(BOTH),
        P(BOTH),
    )
    out_specs = (
        P(BOTH, None),
        P(BOTH, None),
        P(BOTH, None),
        P(BOTH, None),
        P(BOTH, None),
        P(BOTH, None),
        P(BOTH, None),
        P(None, BOTH),
        P(BOTH),
        P(BOTH),
        P(BOTH),
        P(BOTH),
        P(BOTH),
        P(BOTH),
        P(BOTH),
        P(BOTH),
        P(BOTH),
    )
    return jax.shard_map(
        body, mesh=mesh, in_specs=in_specs, out_specs=out_specs, check_vma=False
    )
```

```python
import functools

import jax
import jax.numpy as jnp
from jax import lax
from jax.experimental import pallas as pl
from jax.experimental.pallas import tpu as pltpu
from jax.sharding import PartitionSpec as P

MESH = pl.DeviceIdType.MESH
BLOCKS = 12
DP, FSDP = BOTH = ("dp", "fsdp")


class Place:
    def __init__(self):
        dp, fs = lax.axis_index(DP), lax.axis_index(FSDP)
        z, x, y, c = self.z, self.x, self.y, self.c = dp // 2, dp % 2, fs // 2, fs % 2
        self.fs = fs
        self.near = z + 1 - 2 * (z % 2)
        self.other = 3 - z
        self.low = 2 * (z // 2)
        self.high = 2 - self.low
        self.near_pair, self.far_pair = pl.ds(self.low, 2), pl.ds(self.high, 2)
        self.far_one = z // 2 * -1 + 2
        self.far_two = 3 - z // 2 * 3
        self.inside = (z == 1) | (z == 2)
        self.to_x, self.to_y = device(z, 1 - x, y, c), device(z, x, 1 - y, c)
        self.to_c = device(z, x, y, 1 - c)
        self.to_near, self.to_other = device(self.near, x, y, c), device(self.other, x, y, c)


def device(z, x, y, c):
    return (z * 2 + x, y * 2 + c)


def greet(at):
    bar = pltpu.get_barrier_semaphore()

    def hail(peer):
        pl.semaphore_signal(bar, inc=1, device_id=peer, device_id_type=MESH)

    def meet(*peers):
        for peer in peers:
            hail(peer)
        pl.semaphore_wait(bar, len(peers))

    always = (at.to_c, at.to_x, at.to_y, at.to_near)
    pl.when(at.inside)(lambda: meet(*always, at.to_other))
    pl.when(jnp.logical_not(at.inside))(lambda: meet(*always))


def send(src, dst, ssem, rsem, peer):
    return pltpu.make_async_remote_copy(
        src_ref=src, dst_ref=dst, send_sem=ssem, recv_sem=rsem, device_id=peer, device_id_type=MESH
    )


def numbered(*names):
    return {name: i for i, name in enumerate(names)}


GATHER_GETS = numbered(
    "near", "one", "two", "xn", "yn", "xf", "yf", "da", "db", "df", "xo", "yo",
    "c0", "c1", "c2", "c3", "c4", "c5", "c6", "c7",
)


C_NAMES = list(GATHER_GETS)[-8:]


class GatherBlock:
    def __init__(self, at, full, mine, ss, rs, early=False):
        self.at, self.full, self.mine, self.ss, self.rs, self.early = at, full, mine, ss, rs, early

    def piece(self, name):
        a, full = self.at, self.full
        x, y, c = a.x, a.y, a.c
        both = {"n": a.near_pair, "f": a.far_pair}
        return {
            "own": lambda: full.at[a.z, x, y, c],
            "near": lambda: full.at[a.near, x, y, c],
            "one": lambda: full.at[a.far_one, x, y, c],
            "two": lambda: full.at[a.far_two, x, y, c],
            "on": lambda: full.at[both["n"], x, y, c],
            "of": lambda: full.at[both["f"], x, y, c],
            "xn": lambda: full.at[both["n"], 1 - x, y, c],
            "xf": lambda: full.at[both["f"], 1 - x, y, c],
            "yn": lambda: full.at[both["n"], x, 1 - y, c],
            "yf": lambda: full.at[both["f"], x, 1 - y, c],
            "dn": lambda: full.at[both["n"], 1 - x, 1 - y, c],
            "df": lambda: full.at[both["f"], 1 - x, 1 - y, c],
            "xo": lambda: full.at[a.z, 1 - x, y, c],
            "yo": lambda: full.at[a.z, x, 1 - y, c],
            "x_near": lambda: full.at[a.near, 1 - x, y, c],
            "x_own": lambda: full.at[a.z, 1 - x, y, c],
            "y_near": lambda: full.at[a.near, x, 1 - y, c],
            "d_own": lambda: full.at[a.z, 1 - x, 1 - y, c],
            "d_near": lambda: full.at[a.near, 1 - x, 1 - y, c],
            "c0": lambda: full.at[both["n"], x, y, 1 - c],
            "c1": lambda: full.at[both["f"], x, y, 1 - c],
            "c2": lambda: full.at[both["n"], 1 - x, y, 1 - c],
            "c3": lambda: full.at[both["n"], x, 1 - y, 1 - c],
            "c4": lambda: full.at[both["n"], 1 - x, 1 - y, 1 - c],
            "c5": lambda: full.at[both["f"], 1 - x, y, 1 - c],
            "c6": lambda: full.at[both["f"], x, 1 - y, 1 - c],
            "c7": lambda: full.at[both["f"], 1 - x, 1 - y, 1 - c],
        }[name]()

    SENDS = {
        "own_near": ("own", "near", "to_near"),
        "own_other": ("own", "one", "to_other"),
        "near_other": ("near", "two", "to_other"),
        "one_near": ("one", "one", "to_near"),
        "two_near": ("two", "two", "to_near"),
        "xn": ("on", "xn", "to_x"),
        "yn": ("on", "yn", "to_y"),
        "xo": ("own", "xo", "to_x"),
        "yo": ("own", "yo", "to_y"),
        "xp": ("near", "xn", "to_x"),
        "yp": ("near", "yn", "to_y"),
        "xf": ("of", "xf", "to_x"),
        "yf": ("of", "yf", "to_y"),
        "da": ("x_own", "da", "to_y"),
        "db": ("y_near", "db", "to_x"),
        "d_other": ("dn", "df", "to_other"),
        "d_near": ("df", "df", "to_near"),
        "c0": ("on", "c0", "to_c"),
        "c1": ("of", "c1", "to_c"),
        "c2": ("xn", "c2", "to_c"),
        "c3": ("yn", "c3", "to_c"),
        "c4": ("dn", "c4", "to_c"),
        "c5": ("xf", "c5", "to_c"),
        "c6": ("yf", "c6", "to_c"),
        "c7": ("df", "c7", "to_c"),
    }
    ARRIVES = {"da": "d_own", "db": "d_near"}
    INSIDE = ("own_other", "near_other", "one_near", "two_near", "d_other", "d_near")

    def move(self, name):
        what, called, whom = self.SENDS[name]
        piece = self.piece(what)
        return send(
            piece, piece, self.ss.at[list(self.SENDS).index(name)], self.rs.at[GATHER_GETS[called]], getattr(self.at, whom)
        )

    def go(self, *names):
        for name in names:
            if name in self.INSIDE:
                pl.when(self.at.inside)(lambda: self.move(name).start())
            else:
                self.move(name).start()

    def get(self, name, what=None):
        piece = self.piece(what or self.ARRIVES.get(name, name))
        send(piece, piece, self.ss.at[0], self.rs.at[GATHER_GETS[name]], self.at.to_c).wait_recv()

    def stage(self, s):
        a = self.at
        if s == 0:
            self.full[a.z, a.x, a.y, a.c] = self.mine()
            self.go("own_near", "own_other")
            if self.early:
                self.go("xo", "yo")
        if s == 1:
            self.get("near")
            self.go("near_other")
            if self.early:
                self.go("xp", "yp", "c0")
            else:
                self.go("xn", "yn", "c0")
        if s == 2:
            self.get("one")
            self.go("one_near")
        if s == 3:
            self.get("two")
            self.go("two_near", "xf", "yf", "c1")
        if s == 4:
            if self.early:
                self.get("xo")
                self.go("da")
                self.get("xn", "x_near")
                self.go("c2")
                self.get("yo")
                self.get("yn", "y_near")
            else:
                self.get("xn")
                self.go("da", "c2")
                self.get("yn")
            self.go("db", "c3")
        if s == 5:
            self.get("da")
            self.get("db")
            self.go("d_other", "c4")
        if s == 6:
            self.get("xf")
            self.go("c5")
            self.get("yf")
            self.go("c6")
        if s == 7:
            self.get("df")
            self.go("d_near", "c7")
        if s == 8:
            for i in range(8):
                self.get(C_NAMES[i])
        if s == 9:
            for name in self.SENDS:
                if name not in self.INSIDE + (("xn", "yn") if self.early else ("xo", "yo", "xp", "yp")):
                    self.move(name).wait_send()

            @pl.when(a.inside)
            def _():
                for name in self.INSIDE:
                    self.move(name).wait_send()


GATHER_LAGS = (0, 1, 3, 5, 5, 7, 8, 8, 9, 11)
GATHER_ORDER = (0, 2, 5, 6, 4, 7, 1, 3, 8, 9)


HEAD = 64


norm_epsilon = 1e-12
masked_score = -1000000000.0


def to_half(array):
    return array.astype(jnp.bfloat16)


def matmul(left, right):
    return jnp.dot(left, right, preferred_element_type=jnp.float32)


def matmul_nt(left, right):
    return lax.dot_general(
        left, right, (((1,), (1,)), ((), ())), preferred_element_type=jnp.float32
    )


def contract_rows(left, right):
    return lax.dot_general(
        left, right, (((0,), (0,)), ((), ())), preferred_element_type=jnp.float32
    )


def column_sums(array):
    return jnp.sum(array.astype(jnp.float32), axis=0)


def normalize(values, gain_vec, shift_vec):
    center = values - jnp.mean(values, axis=-1, keepdims=True)
    spread = jnp.mean(center * center, axis=-1, keepdims=True)
    return center * lax.rsqrt(spread + norm_epsilon) * gain_vec + shift_vec


def gelu_exact(values):
    return jax.nn.gelu(values, approximate=False)


def split_heads(block):
    return block.reshape(block.shape[0], -1, HEAD)


def row_scores(queries, key_rows, labels):
    scores = (
        jnp.einsum("qhe,khe->hqk", queries, key_rows, preferred_element_type=jnp.float32) * 0.125
    )
    allowed = labels[:, None] == labels[None, :]
    return jnp.where(allowed[None], scores, masked_score)


def attend_row(pieces):
    queries, key_rows, value_rows, labels = pieces
    scores = row_scores(split_heads(queries), split_heads(key_rows), labels)
    row_max = jnp.max(scores, axis=-1, keepdims=True)
    row_exp = jnp.exp(scores - row_max)
    row_total = jnp.sum(row_exp, axis=-1, keepdims=True)
    probs_half = to_half(row_exp / row_total)
    context = jnp.einsum(
        "hqk,khe->qhe", probs_half, split_heads(value_rows), preferred_element_type=jnp.float32
    )
    return (to_half(context.reshape(queries.shape)), (row_max + jnp.log(row_total))[..., 0])


def attend_back(pieces):
    queries, key_rows, value_rows, labels, log_total, d_context = pieces
    query_heads = split_heads(queries)
    key_heads = split_heads(key_rows)
    context_heads = split_heads(d_context)
    scores = row_scores(query_heads, key_heads, labels)
    attn_probs = jnp.exp(scores - log_total[..., None])
    d_probs = jnp.einsum(
        "qhe,khe->hqk", context_heads, split_heads(value_rows), preferred_element_type=jnp.float32
    )
    row_delta = jnp.sum(attn_probs * d_probs, axis=-1, keepdims=True)
    d_scores = to_half(attn_probs * (d_probs - row_delta))
    d_queries = (
        jnp.einsum("hqk,khe->qhe", d_scores, key_heads, preferred_element_type=jnp.float32) * 0.125
    )
    d_keys = (
        jnp.einsum("hqk,qhe->khe", d_scores, query_heads, preferred_element_type=jnp.float32)
        * 0.125
    )
    d_values = jnp.einsum(
        "hqk,qhe->khe", to_half(attn_probs), context_heads, preferred_element_type=jnp.float32
    )
    return (
        to_half(d_queries.reshape(queries.shape)),
        to_half(d_keys.reshape(queries.shape)),
        to_half(d_values.reshape(queries.shape)),
    )


def plain_device(
    tokens,
    segment,
    cotangent,
    query_w,
    key_w,
    value_w,
    attn_out_w,
    up_w,
    down_w,
    query_bias,
    value_bias,
    attn_out_bias,
    up_bias,
    down_bias,
    norm1_gain,
    norm1_shift,
    norm2_gain,
    norm2_shift,
):
    row_count = segment.shape[0]
    row_length = segment.shape[1]
    model_width = tokens.shape[1]

    def by_rows(array):
        return array.reshape(row_count, row_length, -1)

    attn_set = (
        lax.all_gather(to_half(query_w), BOTH, axis=0, tiled=True),
        lax.all_gather(to_half(key_w), BOTH, axis=0, tiled=True),
        lax.all_gather(to_half(value_w), BOTH, axis=0, tiled=True),
        lax.all_gather(to_half(attn_out_w), BOTH, axis=0, tiled=True),
        lax.all_gather(to_half(query_bias), BOTH, axis=0, tiled=True),
        lax.all_gather(to_half(value_bias), BOTH, axis=0, tiled=True),
        lax.all_gather(to_half(attn_out_bias), BOTH, axis=0, tiled=True),
        lax.all_gather(to_half(norm1_gain), BOTH, axis=0, tiled=True),
        lax.all_gather(to_half(norm1_shift), BOTH, axis=0, tiled=True),
    )
    wq_full, wk_full, wv_full, wo_full, bias_q, bias_v, bias_o, gain_one, shift_one = attn_set
    ffn_set = (
        lax.all_gather(to_half(up_w), BOTH, axis=0, tiled=True),
        lax.all_gather(to_half(down_w), BOTH, axis=1, tiled=True),
        lax.all_gather(to_half(up_bias), BOTH, axis=0, tiled=True),
        lax.all_gather(to_half(down_bias), BOTH, axis=0, tiled=True),
        lax.all_gather(to_half(norm2_gain), BOTH, axis=0, tiled=True),
        lax.all_gather(to_half(norm2_shift), BOTH, axis=0, tiled=True),
    )
    w_up, w_down, bias_up, bias_down, gain_two, shift_two = ffn_set
    queries = to_half(matmul(tokens, wq_full) + bias_q.astype(jnp.float32))
    key_rows = to_half(matmul(tokens, wk_full))
    value_rows = to_half(matmul(tokens, wv_full) + bias_v.astype(jnp.float32))
    context, log_total = lax.map(
        attend_row, (by_rows(queries), by_rows(key_rows), by_rows(value_rows), segment)
    )
    context = context.reshape(-1, model_width)
    attended = matmul(context, wo_full) + bias_o.astype(jnp.float32)
    first_sum = tokens.astype(jnp.float32) + attended
    norm_mid, pull_one = jax.vjp(
        normalize, first_sum, gain_one.astype(jnp.float32), shift_one.astype(jnp.float32)
    )
    mid_half = to_half(norm_mid)
    pre_act = matmul(mid_half, w_up) + bias_up.astype(jnp.float32)
    act_out, pull_act = jax.vjp(gelu_exact, pre_act)
    act_half = to_half(act_out)
    ffn_out = matmul(act_half, w_down) + bias_down.astype(jnp.float32)
    second_sum = mid_half.astype(jnp.float32) + ffn_out
    final, pull_two = jax.vjp(
        normalize, second_sum, gain_two.astype(jnp.float32), shift_two.astype(jnp.float32)
    )
    outputs = to_half(final)
    valid = (segment.reshape(-1) >= 0).astype(jnp.float32)[:, None]
    d_out = cotangent.astype(jnp.float32) * valid
    d_second, d_gain_two, d_shift_two = pull_two(d_out)
    up_back, down_back = (
        lax.all_gather(to_half(up_w), BOTH, axis=0, tiled=True),
        lax.all_gather(to_half(down_w), BOTH, axis=1, tiled=True),
    )
    d_ffn = to_half(d_second)
    d_down_turned = contract_rows(d_ffn, act_half)
    d_down_bias = column_sums(d_ffn)
    (d_pre,) = pull_act(matmul_nt(d_ffn, down_back))
    d_pre_half = to_half(d_pre)
    d_up_w = contract_rows(mid_half, d_pre_half)
    d_up_bias = column_sums(d_pre_half)
    d_mid = d_second + matmul_nt(d_pre_half, up_back)
    d_first, d_gain_one, d_shift_one = pull_one(d_mid)
    wq_back, wk_back, wv_back, wo_back = (
        lax.all_gather(to_half(query_w), BOTH, axis=0, tiled=True),
        lax.all_gather(to_half(key_w), BOTH, axis=0, tiled=True),
        lax.all_gather(to_half(value_w), BOTH, axis=0, tiled=True),
        lax.all_gather(to_half(attn_out_w), BOTH, axis=0, tiled=True),
    )
    d_att = to_half(d_first)
    d_attn_out_w = contract_rows(context, d_att)
    d_attn_out_bias = column_sums(d_att)
    d_context = to_half(matmul_nt(d_att, wo_back))
    d_queries, d_keys, d_values = lax.map(
        attend_back,
        (
            by_rows(queries),
            by_rows(key_rows),
            by_rows(value_rows),
            segment,
            log_total,
            by_rows(d_context),
        ),
    )
    d_queries = d_queries.reshape(-1, model_width)
    d_keys = d_keys.reshape(-1, model_width)
    d_values = d_values.reshape(-1, model_width)
    d_query_w = contract_rows(tokens, d_queries)
    d_key_w = contract_rows(tokens, d_keys)
    d_value_w = contract_rows(tokens, d_values)
    d_query_bias = column_sums(d_queries)
    d_value_bias = column_sums(d_values)
    d_tokens = (
        d_first
        + matmul_nt(d_queries, wq_back)
        + matmul_nt(d_keys, wk_back)
        + matmul_nt(d_values, wv_back)
    )
    members = (
        d_query_w,
        d_key_w,
        d_value_w,
        d_attn_out_w,
        d_up_w,
        d_down_turned,
        d_query_bias,
        d_value_bias,
        d_attn_out_bias,
        d_up_bias,
        d_down_bias,
        d_gain_one,
        d_shift_one,
        d_gain_two,
        d_shift_two,
    )
    block_sums = (
        lax.psum_scatter(
            members[0].astype(jnp.bfloat16), DP, scatter_dimension=0, tiled=True
        ).astype(jnp.float32),
        lax.psum_scatter(
            members[1].astype(jnp.bfloat16), DP, scatter_dimension=0, tiled=True
        ).astype(jnp.float32),
        lax.psum_scatter(
            members[2].astype(jnp.bfloat16), DP, scatter_dimension=0, tiled=True
        ).astype(jnp.float32),
        lax.psum_scatter(
            members[3].astype(jnp.bfloat16), DP, scatter_dimension=0, tiled=True
        ).astype(jnp.float32),
        lax.psum_scatter(
            members[4].astype(jnp.bfloat16), DP, scatter_dimension=0, tiled=True
        ).astype(jnp.float32),
        lax.psum_scatter(
            members[5].astype(jnp.bfloat16), DP, scatter_dimension=0, tiled=True
        ).astype(jnp.float32),
        lax.psum_scatter(
            members[6].astype(jnp.bfloat16), DP, scatter_dimension=0, tiled=True
        ).astype(jnp.float32),
        lax.psum_scatter(
            members[7].astype(jnp.bfloat16), DP, scatter_dimension=0, tiled=True
        ).astype(jnp.float32),
        lax.psum_scatter(
            members[8].astype(jnp.bfloat16), DP, scatter_dimension=0, tiled=True
        ).astype(jnp.float32),
        lax.psum_scatter(
            members[9].astype(jnp.bfloat16), DP, scatter_dimension=0, tiled=True
        ).astype(jnp.float32),
        lax.psum_scatter(
            members[10].astype(jnp.bfloat16), DP, scatter_dimension=0, tiled=True
        ).astype(jnp.float32),
        lax.psum_scatter(
            members[11].astype(jnp.bfloat16), DP, scatter_dimension=0, tiled=True
        ).astype(jnp.float32),
        lax.psum_scatter(
            members[12].astype(jnp.bfloat16), DP, scatter_dimension=0, tiled=True
        ).astype(jnp.float32),
        lax.psum_scatter(
            members[13].astype(jnp.bfloat16), DP, scatter_dimension=0, tiled=True
        ).astype(jnp.float32),
        lax.psum_scatter(
            members[14].astype(jnp.bfloat16), DP, scatter_dimension=0, tiled=True
        ).astype(jnp.float32),
    )
    every_shard = (
        lax.psum_scatter(
            block_sums[0].astype(jnp.bfloat16), FSDP, scatter_dimension=0, tiled=True
        ).astype(jnp.float32),
        lax.psum_scatter(
            block_sums[1].astype(jnp.bfloat16), FSDP, scatter_dimension=0, tiled=True
        ).astype(jnp.float32),
        lax.psum_scatter(
            block_sums[2].astype(jnp.bfloat16), FSDP, scatter_dimension=0, tiled=True
        ).astype(jnp.float32),
        lax.psum_scatter(
            block_sums[3].astype(jnp.bfloat16), FSDP, scatter_dimension=0, tiled=True
        ).astype(jnp.float32),
        lax.psum_scatter(
            block_sums[4].astype(jnp.bfloat16), FSDP, scatter_dimension=0, tiled=True
        ).astype(jnp.float32),
        lax.psum_scatter(
            block_sums[5].astype(jnp.bfloat16), FSDP, scatter_dimension=0, tiled=True
        ).astype(jnp.float32),
        lax.psum_scatter(
            block_sums[6].astype(jnp.bfloat16), FSDP, scatter_dimension=0, tiled=True
        ).astype(jnp.float32),
        lax.psum_scatter(
            block_sums[7].astype(jnp.bfloat16), FSDP, scatter_dimension=0, tiled=True
        ).astype(jnp.float32),
        lax.psum_scatter(
            block_sums[8].astype(jnp.bfloat16), FSDP, scatter_dimension=0, tiled=True
        ).astype(jnp.float32),
        lax.psum_scatter(
            block_sums[9].astype(jnp.bfloat16), FSDP, scatter_dimension=0, tiled=True
        ).astype(jnp.float32),
        lax.psum_scatter(
            block_sums[10].astype(jnp.bfloat16), FSDP, scatter_dimension=0, tiled=True
        ).astype(jnp.float32),
        lax.psum_scatter(
            block_sums[11].astype(jnp.bfloat16), FSDP, scatter_dimension=0, tiled=True
        ).astype(jnp.float32),
        lax.psum_scatter(
            block_sums[12].astype(jnp.bfloat16), FSDP, scatter_dimension=0, tiled=True
        ).astype(jnp.float32),
        lax.psum_scatter(
            block_sums[13].astype(jnp.bfloat16), FSDP, scatter_dimension=0, tiled=True
        ).astype(jnp.float32),
        lax.psum_scatter(
            block_sums[14].astype(jnp.bfloat16), FSDP, scatter_dimension=0, tiled=True
        ).astype(jnp.float32),
    )
    (
        shard_qw,
        shard_kw,
        shard_vw,
        shard_ow,
        shard_uw,
        shard_turned,
        shard_qb,
        shard_vb,
        shard_ob,
        shard_ub,
        shard_db,
        shard_g1,
        shard_s1,
        shard_g2,
        shard_s2,
    ) = every_shard
    shard_dw = jnp.transpose(shard_turned)
    return (
        outputs,
        d_tokens,
        shard_qw,
        shard_kw,
        shard_vw,
        shard_ow,
        shard_uw,
        shard_dw,
        shard_qb,
        shard_vb,
        shard_ob,
        shard_ub,
        shard_db,
        shard_g1,
        shard_s1,
        shard_g2,
        shard_s2,
    )


ATTN = 4
NORM_ROWS = 256
LANES = 128
SIDE = 1024
V_LANE, R_LANE = 32, 64


def aligned(start, size, step=None):
    return pl.ds(pl.multiple_of(start, step or size), size)


def side_loop(count, body):
    def step(i, carry):
        body(i)
        return carry

    lax.fori_loop(0, count, step, 0)


def square(full, b):
    size = full.shape[-1]
    return full.at[b].reshape(size, size)


def spread_vectors(tiles, short_ref, up_ref, depth):
    for dp in range(2 * depth):
        total = jnp.zeros((16, LANES), jnp.float32)
        for fs in range(4):
            total = total + tiles[dp // 2, dp % 2, fs // 2, fs % 2].astype(jnp.float32)
        short_ref[:, dp * LANES : (dp + 1) * LANES] = total[:8]
        for fs in range(4):
            at = (dp * 4 + fs) * LANES
            up_ref[:, at : at + LANES] = total[8 + fs : 9 + fs]


def stepwise(body, after):
    def step(i):
        body(i)
        for k, follow in enumerate(after):
            pl.when(i == k)(follow)

    side_loop(len(after), step)


def nothing():
    pass


def attend_pairs(first, last, qkvc, lse, mask):
    length = mask.shape[0]

    def pair(p):
        lanes = aligned(p * LANES, LANES)
        q, k, v = qkvc[0, :, lanes], qkvc[1, :, lanes], qkvc[2, :, lanes]
        lane = lax.broadcasted_iota(jnp.int32, (length, LANES), 1)
        lower = lane < HEAD
        total = jnp.zeros((length, LANES), jnp.float32)
        logs = lse[...]
        for h in range(2):
            here = lower if h == 0 else jnp.logical_not(lower)
            key = jnp.where(here, k, jnp.zeros_like(k))
            scores = matmul_nt(q, key) + mask[...]
            row_max = jnp.max(scores, axis=-1, keepdims=True)
            row_exp = jnp.exp(scores - row_max)
            row_total = jnp.sum(row_exp, axis=-1, keepdims=True)
            part = matmul(to_half(row_exp), v) / row_total
            total = jnp.where(here, part, total)
            logs = jnp.where(lane == 2 * p + h, row_max + jnp.log(row_total), logs)
        qkvc[3, :, lanes] = to_half(total)
        lse[...] = logs

    def step(i, carry):
        pair(i)
        return carry

    lax.fori_loop(first, last, step, 0)


SUM_SENDS = numbered("c", "df", "dg", "da", "db", "xn", "yn", "xf", "yf", "f", "m", "n")
SUM_LAGS = (0, 1, 2, 3, 4, 3, 5, 6, 7)
SUM_ORDER = (6, 3, 1, 2, 4, 5, 0, 7, 8)
SUM_BUFFERS = {
    "grad": (2, (4, 2, 2, 2)),
    "held": (7, (4, 2, 2)),
    "c": (2, (4, 2, 2)),
    "df": (7, (2,)),
    "dg": (2, (2,)),
    "da": (4, ()),
    "db": (4, ()),
    "xn": (5, (2,)),
    "yn": (4, (2,)),
    "xf": (5, (2,)),
    "yf": (5, (2,)),
    "f": (5, (2,)),
    "m": (4, (2,)),
    "n": (4, ()),
}


def sum_scratch(rows, cols, blocks, names):
    bufs = [SUM_BUFFERS[name] for name in names]
    bufs = [pltpu.VMEM((min(slots, blocks),) + parts + (rows, cols), jnp.bfloat16) for slots, parts in bufs]
    return bufs + [pltpu.SemaphoreType.DMA((blocks, len(SUM_SENDS)))] * 2


class SumBlock:
    def __init__(self, at, refs, names, b, **others):
        self.at = at
        *bufs, ss, rs = refs
        self.ss, self.rs = ss.at[b], rs.at[b]
        self.buf = {n: ref.at[b % ref.shape[0]] for n, ref in zip(names, bufs)} | others

    def move(self, name):
        a, held = self.at, self.buf["held"]
        x, y = a.x, a.y
        every, both = pl.ds(0, 4), pl.ds(0, 2)
        src, to = {
            "c": lambda: (self.buf["grad"].at[every, both, both, 1 - a.c], a.to_c),
            "df": lambda: (held.at[a.far_pair, 1 - x, 1 - y], a.to_near),
            "dg": lambda: (held.at[a.far_pair, 1 - x, 1 - y], a.to_other),
            "da": lambda: (held.at[a.z, 1 - x, 1 - y], a.to_y),
            "db": lambda: (held.at[a.near, 1 - x, 1 - y], a.to_x),
            "xn": lambda: (held.at[a.near_pair, 1 - x, y], a.to_x),
            "yn": lambda: (held.at[a.near_pair, x, 1 - y], a.to_y),
            "xf": lambda: (held.at[a.far_pair, 1 - x, y], a.to_x),
            "yf": lambda: (held.at[a.far_pair, x, 1 - y], a.to_y),
            "f": lambda: (held.at[a.far_pair, x, y], a.to_near),
            "m": lambda: (held.at[a.far_pair, x, y], a.to_other),
            "n": lambda: (held.at[a.near, x, y], a.to_near),
        }[name]()
        i = SUM_SENDS[name]
        return send(src, self.buf[name], self.ss.at[i], self.rs.at[i], to)

    def start(self, name):
        self.move(name).start()

    def got(self, name):
        self.move(name).wait_recv()
        return self.buf[name]

    def stage(self, s, out=None):
        a, held, grad = self.at, self.buf["held"], self.buf["grad"]
        x, y, c = a.x, a.y, a.c
        inside = a.inside
        outside = jnp.logical_not(inside)

        def add(first, xx, yy, *others, count=2):
            for i in range(count):
                total = held[first + i, xx, yy].astype(jnp.float32)
                for other in others:
                    total = total + (other[i] if count == 2 else other[...]).astype(jnp.float32)
                held[first + i, xx, yy] = total.astype(jnp.bfloat16)

        if s == 0:
            self.start("c")
        if s == 1:
            self.move("c").wait()
            pair = self.buf["c"]

            def join(first, xx, yy):
                for i in range(2):
                    held[first + i, xx, yy] = grad[first + i, xx, yy, c] + pair[first + i, xx, yy]

            join(a.high, 1 - x, 1 - y)
            pl.when(outside)(lambda: self.start("df"))
            join(a.high, 1 - x, y)
            self.start("xf")
            join(a.high, x, 1 - y)
            self.start("yf")
            join(a.low, 1 - x, 1 - y)
            join(a.low, 1 - x, y)
            join(a.low, x, 1 - y)
            join(a.high, x, y)
            join(a.low, x, y)
        if s == 2:

            @pl.when(inside)
            def _():
                add(a.high, 1 - x, 1 - y, self.got("df"))
                self.start("dg")

        if s == 3:

            @pl.when(inside)
            def _():
                add(a.low, 1 - x, 1 - y, self.got("dg"))

            self.start("da")
            self.start("db")
        if s == 4:
            add(a.z, 1 - x, y, self.got("da"), count=1)
            self.start("xn")
            add(a.near, x, 1 - y, self.got("db"), count=1)
            self.start("yn")
        if s == 5:
            add(a.high, x, y, self.got("xf"), self.got("yf"))
            pl.when(outside)(lambda: self.start("f"))
        if s == 6:

            @pl.when(inside)
            def _():
                add(a.high, x, y, self.got("f"))
                self.start("m")

        if s == 7:
            add(a.low, x, y, self.got("xn"), self.got("yn"))

            @pl.when(inside)
            def _():
                add(a.low, x, y, self.got("m"))

            self.start("n")
        if s == 8:
            out[...] = held[a.z, x, y].astype(jnp.float32) + self.got("n")[...].astype(jnp.float32)
            for name in ("da", "db", "xn", "yn", "xf", "yf", "n"):
                self.move(name).wait_send()

            @pl.when(inside)
            def _():
                self.move("dg").wait_send()
                self.move("m").wait_send()

            @pl.when(outside)
            def _():
                self.move("df").wait_send()
                self.move("f").wait_send()


def attend_back_pairs(first, last, qkvc, lse, delta, mask, grads):
    length = mask.shape[0]

    def pair(p, carry):
        lanes = aligned(p * LANES, LANES)
        q, k, v, d_context = qkvc[0, :, lanes], qkvc[1, :, lanes], qkvc[2, :, lanes], grads[3, :, lanes]
        lower = lax.broadcasted_iota(jnp.int32, (length, LANES), 1) < HEAD
        sums = [jnp.zeros((length, LANES), jnp.float32) for _ in range(3)]
        for h in range(2):
            here = lower if h == 0 else jnp.logical_not(lower)
            row = pl.ds(2 * p + h, 1)
            key = jnp.where(here, k, jnp.zeros_like(k))
            value = jnp.where(here, v, jnp.zeros_like(v))
            probs = jnp.exp(matmul_nt(key, q) + mask[...] - lse[row, :])
            d_scores = to_half(probs * (matmul_nt(value, d_context) - delta[row, :]))
            parts = (
                contract_rows(d_scores, k) * 0.125,
                matmul(d_scores, q),
                matmul(to_half(probs), d_context),
            )
            sums = [jnp.where(here, part, total) for part, total in zip(parts, sums)]
        for i in range(3):
            grads[i, :, lanes] = to_half(sums[i])
        return carry

    lax.fori_loop(first, last, pair, 0)


SUM_NAMES = tuple(SUM_BUFFERS)
LENT = SUM_NAMES[:2]
OWN_BUFFERS = SUM_NAMES[2:]


def layer_kernel(depth, *refs):
    tokens_hbm, segment, cotangent_hbm, wq, wk, wv, wo, up_w, down_w, *vectors = refs[:18]
    out_hbm, dtok_hbm, gq, gk, gv, go, gup, gdown, gshort, gup_bias = refs[18:28]
    (
        full, tiles, mine_vec, short, up_bias, qkvc, lse, lse_turned, mask, mid, act, dge, nhat, total, half,
        turn_a, delta_turned, cotangent, vgrads, tile_sum, spare, staged, ss, rs, isem, osem, *rest,
    ) = refs[28:]
    count = len(OWN_BUFFERS) + 2
    big, vec = rest[:count], rest[count:]
    length, width = mid.shape
    tokens = mid
    here = Place()
    fs = here.fs
    rows = wq.shape[0]
    f32 = jnp.float32

    shards = [wq, wk, wv, wo]
    for wide in (up_w, down_w):
        shards += [wide.at[:, i * width : (i + 1) * width] for i in range(ATTN)]
    loads = [
        pltpu.make_async_copy(src, total.at[i * rows : (i + 1) * rows], isem.at[i]) for i, src in enumerate(shards)
    ]
    loads.append(pltpu.make_async_copy(tokens_hbm, tokens, isem.at[BLOCKS]))
    loads.append(pltpu.make_async_copy(cotangent_hbm, cotangent, isem.at[BLOCKS + 1]))
    for load in loads:
        load.start()
    greet(here)

    mine_vec[...] = jnp.zeros_like(mine_vec)
    for i in range(8):
        mine_vec[i : i + 1, 0:rows] = vectors[i][...]
    placed = pltpu.roll(mine_vec[...], fs * rows, 1)
    row_at = lax.broadcasted_iota(jnp.int32, (16, LANES), 0)
    mine_vec[...] = jnp.where(row_at == 8 + fs, jnp.broadcast_to(vectors[8][...], (16, LANES)), placed)

    def own(b):
        loads[b].wait()
        return to_half(total[b * rows : (b + 1) * rows, :])

    def gather_block(b):
        return GatherBlock(here, full.at[b], lambda: own(b), ss.at[b], rs.at[b], b < 6)

    own_tiles = GatherBlock(here, tiles, lambda: to_half(mine_vec[...]), ss.at[BLOCKS], rs.at[BLOCKS])

    def gather_pump(t):
        for s in GATHER_ORDER:
            b = t - GATHER_LAGS[s]
            if 0 <= b < BLOCKS:
                gather_block(b).stage(s)
            if b == 0:
                own_tiles.stage(s)

    gather_pump(0)
    gather_pump(1)
    labels = segment[...].astype(jnp.float32)
    turned = jnp.transpose(jnp.broadcast_to(labels, (LANES, length)))
    mask[...] = jnp.where(turned[:, :1] == labels, 0.0, masked_score)
    lse[...] = jnp.where(turned >= 0.0, 1.0, 0.0)
    ready = GATHER_LAGS[8]
    for t in range(2, ready + 1):
        gather_pump(t)
    spread_vectors(tiles, short, up_bias, depth)
    loads[BLOCKS].wait()

    def project(i):
        biased = jnp.where(i == 1, 0.0, 1.0)
        scale = jnp.where(i == 0, 0.125, 1.0)
        bias = short[pl.ds(i // 2, 1), :] * biased
        qkvc[i] = to_half(to_half(matmul(tokens[...], square(full, i)[...]) + bias).astype(f32) * scale)

    stepwise(project, [lambda: gather_pump(ready + 1), lambda: gather_pump(ready + 2), nothing])
    stepwise(
        lambda i: attend_pairs(i * 4, i * 4 + 4, qkvc, lse, mask),
        [lambda: gather_pump(ready + 3), nothing],
    )
    lse_turned[...] = jnp.transpose(lse[...])[: lse_turned.shape[0]]
    gather_pump(ready + 4)

    wo_full = square(full, 3)

    def attended(n):
        cols = aligned(n * SIDE, SIDE)
        total[:, cols] = (
            matmul(qkvc[3], wo_full[:, cols]) + short[2:3, cols] + tokens[:, cols].astype(jnp.float32)
        )

    side_loop(width // SIDE, attended)

    lane_at = lax.broadcasted_iota(jnp.int32, (NORM_ROWS, LANES), 1)

    def first_norm(i):
        at = aligned(i * NORM_ROWS, NORM_ROWS)
        values = total[at, :]
        center = values - jnp.mean(values, axis=-1, keepdims=True)
        spread = jnp.mean(center * center, axis=-1, keepdims=True)
        r = lax.rsqrt(spread + norm_epsilon)
        unit = center * r
        nhat[at, :] = to_half(unit)
        lse[at, :] = jnp.where(lane_at >= R_LANE, r, lse[at, :])
        mid[at, :] = to_half(unit * short[4:5, :] + short[5:6, :])

    side_loop(length // NORM_ROWS, first_norm)

    def activate(j):
        weight = square(full, ATTN + j)
        for part in range(2):
            cols = slice(part * width // 2, (part + 1) * width // 2)
            pre = matmul(mid[...], weight[:, cols]) + up_bias[:, aligned(j * width + part * width // 2, width // 2)]
            cdf = 0.5 * (1.0 + lax.erf(pre * 0.7071067811865476))
            act[j, :, cols] = to_half(pre * cdf)
            pdf = jnp.exp(-0.5 * pre * pre) * 0.3989422804014327
            dge[j, :, cols] = to_half(cdf + pre * pdf)

    def contract(j):
        total[...] = total[...] + matmul_nt(act[j], square(full, 2 * ATTN + j)[...])

    gather_pump(ready + 5)
    stepwise(activate, [lambda: gather_pump(ready + 6), lambda: gather_pump(ready + 7), lambda: gather_pump(ready + 8), nothing])
    total[...] = mid[...].astype(f32) + short[3:4, :]
    stepwise(contract, [lambda: gather_pump(ready + 9), lambda: gather_pump(ready + 10), lambda: gather_pump(ready + 11), nothing])

    loads[BLOCKS + 1].wait()
    vgrads[...] = jnp.zeros_like(vgrads)

    def second_norm(i):
        at = aligned(i * NORM_ROWS, NORM_ROWS)
        values = total[at, :]
        center = values - jnp.mean(values, axis=-1, keepdims=True)
        spread = jnp.mean(center * center, axis=-1, keepdims=True)
        r = lax.rsqrt(spread + norm_epsilon)
        unit = center * r
        gain = short[6:7, :]
        final = to_half(unit * gain + short[7:8, :])
        e = cotangent[at, :].astype(jnp.float32) * lse[at, V_LANE : V_LANE + 1]
        cotangent[at, :] = final
        vgrads[6:7, :] = vgrads[6:7, :] + jnp.sum(e * unit, axis=0, keepdims=True)
        vgrads[7:8, :] = vgrads[7:8, :] + jnp.sum(e, axis=0, keepdims=True)
        eg = e * gain
        d = r * (
            eg - jnp.mean(eg, axis=-1, keepdims=True) - unit * jnp.mean(eg * unit, axis=-1, keepdims=True)
        )
        total[at, :] = d
        half[at, :] = to_half(d)
        vgrads[3:4, :] = vgrads[3:4, :] + jnp.sum(to_half(d).astype(jnp.float32), axis=0, keepdims=True)

    side_loop(length // NORM_ROWS, second_norm)
    pltpu.make_async_copy(cotangent, out_hbm, osem.at[0]).start()

    outs = [gdown.at[:, i * width : (i + 1) * width] for i in range(4)]
    outs += [gup.at[:, i * width : (i + 1) * width] for i in range(4)] + [go, gv, gk, gq]

    held_at = [(4, 0), (4, 1), (9, 0), (9, 1), (5, 0), (5, 1), (10, 0)]

    def grad_of(b):
        return spare.at[b % 2]

    def block(b):
        gathered, half_at = held_at[b % len(held_at)]
        lent = dict(zip(LENT, (grad_of(b), full.at[gathered, :, :, :, half_at])))
        return SumBlock(here, big, OWN_BUFFERS, b, **lent)

    vblock = SumBlock(here, vec, SUM_NAMES, 0)
    turn_b = square(full, 6).at[:, 0:length]

    def leave(b):
        return pltpu.make_async_copy(staged.at[b % 2], outs[b], osem.at[2 + b % 2])

    def pump(t):
        for s in SUM_ORDER:
            b = t - SUM_LAGS[s]
            if 0 <= b < BLOCKS:
                if s == 8 and b > 1:
                    leave(b - 2).wait()
                block(b).stage(s, staged.at[b % 2])
                if s == 8:
                    leave(b).start()
            if b == BLOCKS - 1:
                vblock.stage(s, tile_sum)

    def weight_grad(b, left, right):
        grad = grad_of(b)
        for part in range(2):
            got = to_half(matmul(left[part * width // 2 : (part + 1) * width // 2, :], right[...]))
            grad[2 * part : 2 * part + 2] = got.reshape((2,) + grad.shape[1:])

    def sums_of(values):
        return jnp.sum(values.astype(f32), axis=0, keepdims=True)

    turn_a[...] = jnp.transpose(half[...])
    weight_grad(0, turn_a, act.at[0])
    pump(0)
    for t in range(ready + 12, BLOCKS + max(GATHER_LAGS)):
        gather_pump(t)

    up_grads = up_bias

    def units_back(j):
        d_pre = to_half(matmul(half[...], square(full, 2 * ATTN + j)[...]) * dge[j].astype(f32))
        dge[j] = d_pre
        up_grads[:, aligned(j * width, width)] = sums_of(d_pre)
        add_product(dge.at[j], square(full, ATTN + j))

        @pl.when(j < ATTN - 1)
        def _():
            weight_grad(j + 1, turn_a, act.at[j + 1])

    def add_product(left, weight):
        total[...] = total[...] + matmul_nt(left[...], weight[...])

    stepwise(units_back, [lambda: pump(1), lambda: pump(2), lambda: pump(3), nothing])
    turn_b[...] = jnp.transpose(mid[...])
    loads[BLOCKS].start()
    weight_grad(4, turn_b, dge.at[0])
    pump(4)


    def first_norm_back(i):
        at = aligned(i * NORM_ROWS, NORM_ROWS)
        e = total[at, :]
        unit = nhat[at, :].astype(f32)
        vgrads[4:5, :] = vgrads[4:5, :] + jnp.sum(e * unit, axis=0, keepdims=True)
        vgrads[5:6, :] = vgrads[5:6, :] + jnp.sum(e, axis=0, keepdims=True)
        eg = e * short[4:5, :]
        d = lse[at, R_LANE : R_LANE + 1] * (
            eg - jnp.mean(eg, axis=-1, keepdims=True) - unit * jnp.mean(eg * unit, axis=-1, keepdims=True)
        )
        total[at, :] = d
        d_half = to_half(d)
        half[at, :] = d_half
        vgrads[2:3, :] = vgrads[2:3, :] + jnp.sum(d_half.astype(f32), axis=0, keepdims=True)

    side_loop(length // NORM_ROWS, first_norm_back)
    wo_full = square(full, 3)
    delta = lse

    def context_back(n):
        cols = aligned(n * SIDE, SIDE)
        d_context = to_half(matmul_nt(half[...], wo_full[cols, :]))
        act[3, :, cols] = d_context
        product = d_context.astype(f32) * qkvc[3, :, cols].astype(f32)
        lane = lax.broadcasted_iota(jnp.int32, (length, LANES), 1)
        got = delta[...]
        for i in range(SIDE // HEAD):
            two = product[:, (i // 2) * LANES : (i // 2 + 1) * LANES]
            here = lane // HEAD == i % 2
            head = jnp.sum(jnp.where(here, two, 0.0), axis=-1, keepdims=True)
            got = jnp.where(lane == n * (SIDE // HEAD) + i, head, got)
        delta[...] = got

    side_loop(width // SIDE, context_back)
    delta_turned[...] = jnp.transpose(delta[...])[: delta_turned.shape[0]]
    weight_grad(5, turn_b, dge.at[1])
    pump(5)

    def attention_step(i):
        attend_back_pairs(3 * i, jnp.minimum(3 * i + 3, 8), qkvc, lse_turned, delta_turned, mask, act)

        @pl.when(i < 2)
        def _():
            weight_grad(6 + i, turn_b, dge.at[2 + i])

    stepwise(attention_step, [lambda: pump(6), lambda: pump(7), nothing])
    turn_a[...] = jnp.transpose(qkvc[3])
    weight_grad(8, turn_a, half)
    pump(8)
    loads[BLOCKS].wait()
    turn_b[...] = jnp.transpose(tokens[...])

    def place_vectors():
        vgrads[0:1, :] = sums_of(act[0])
        vgrads[1:2, :] = sums_of(act[2])
        for dp in range(2 * depth):
            for fsdp in range(4):
                at = (dp * 4 + fsdp) * LANES
                vec[0][0, dp // 2, dp % 2, fsdp // 2, fsdp % 2] = to_half(
                    jnp.concatenate(
                        [
                            vgrads[:, dp * LANES : (dp + 1) * LANES],
                            jnp.broadcast_to(up_grads[:, at : at + LANES], (8, LANES)),
                        ],
                        axis=0,
                    )
                )

    def middle_pump():
        pump(9)
        place_vectors()

    stepwise(
        lambda i: weight_grad(9 + i, turn_b, act.at[2 - i]), [middle_pump, lambda: pump(10), lambda: pump(11)]
    )

    def hand_back():
        pltpu.make_async_copy(total, dtok_hbm, osem.at[1]).start()
        pump(14)

    stepwise(
        lambda i: add_product(act.at[2 - i], square(full, 2 - i)), [lambda: pump(12), lambda: pump(13), hand_back]
    )
    for t in range(15, BLOCKS + max(SUM_LAGS)):
        pump(t)
    leave(BLOCKS - 2).wait()
    leave(BLOCKS - 1).wait()
    moved = pltpu.roll(tile_sum[...], (4 - fs) * rows % LANES, 1)
    gshort[...] = moved[:8]
    gup_bias[...] = tile_sum[8:9, :]
    pltpu.make_async_copy(total, dtok_hbm, osem.at[1]).wait()
    pltpu.make_async_copy(cotangent, out_hbm, osem.at[0]).wait()


def layer_call(depth, tokens, segment, cotangent, weights, vectors):
    length, width = tokens.shape
    rows = weights[0].shape[0]
    dims = (depth, 2, 2, 2)
    bf, f32 = jnp.bfloat16, jnp.float32
    part = ((rows, width), f32)
    shapes = [
        ((length, width), bf), ((length, width), f32), part, part, part, part, ((rows, ATTN * width), f32),
        ((rows, ATTN * width), f32), ((8, LANES), f32), ((1, LANES), f32),
    ]
    vmem, hbm = pl.BlockSpec(memory_space=pltpu.VMEM), pl.BlockSpec(memory_space=pl.ANY)
    scratch = [
        pltpu.VMEM((BLOCKS,) + dims + (rows, width), bf),
        pltpu.VMEM(dims + (16, LANES), bf),
        pltpu.VMEM((16, LANES), f32),
        pltpu.VMEM((8, width), f32),
        pltpu.VMEM((1, ATTN * width), f32),
        pltpu.VMEM((4, length, width), bf),
        pltpu.VMEM((length, LANES), f32),
        pltpu.VMEM((width // HEAD, length), f32),
        pltpu.VMEM((length, length), f32),
        pltpu.VMEM((length, width), bf),
        pltpu.VMEM((ATTN, length, width), bf),
        pltpu.VMEM((ATTN, length, width), bf),
        pltpu.VMEM((length, width), bf),
        pltpu.VMEM((length, width), f32),
        pltpu.VMEM((length, width), bf),
        pltpu.VMEM((width, length), bf),
        pltpu.VMEM((width // HEAD, length), f32),
        pltpu.VMEM((length, width), bf),
        pltpu.VMEM((8, width), f32),
        pltpu.VMEM((16, LANES), f32),
        pltpu.VMEM((2,) + dims + (rows, width), bf),
        pltpu.VMEM((2, rows, width), f32),
        pltpu.SemaphoreType.DMA((BLOCKS + 1, len(GatherBlock.SENDS))),
        pltpu.SemaphoreType.DMA((BLOCKS + 1, len(GATHER_GETS))),
        pltpu.SemaphoreType.DMA((BLOCKS + 2,)),
        pltpu.SemaphoreType.DMA((4,)),
    ]
    scratch += sum_scratch(rows, width, BLOCKS, OWN_BUFFERS) + sum_scratch(16, LANES, 1, SUM_NAMES)
    return pl.pallas_call(
        functools.partial(layer_kernel, depth),
        out_shape=tuple(jax.ShapeDtypeStruct(*s) for s in shapes),
        in_specs=[hbm, vmem, hbm] + [hbm] * 6 + [vmem] * 9,
        out_specs=tuple([hbm] * 8 + [vmem] * 2),
        scratch_shapes=scratch,
        compiler_params=pltpu.CompilerParams(
            collective_id=0, has_side_effects=True, vmem_limit_bytes=63 * 2**20
        ),
        name="layer",
    )(tokens, segment, cotangent, *weights, *vectors)


PIECE = 1024


def results_kernel(large, short, *refs):
    sources, targets, vectors = refs[:large], refs[large + 2 : 2 * large + 2], refs[2 * large + 2 : 2 * large + 11]
    rows, up = refs[large : large + 2]
    held, (came, gone) = refs[2 * large + 11 : -2], refs[-2:]
    ins, outs = [], []
    for src, mid, dst in zip(sources, held, targets):
        for start in range(0, src.shape[0], PIECE):
            at = pl.ds(start, min(PIECE, src.shape[0]))
            i = len(ins)
            ins.append(pltpu.make_async_copy(src.at[at], mid.at[at], came.at[i]))
            outs.append(pltpu.make_async_copy(mid.at[at], dst.at[at], gone.at[i]))
    for copy in ins:
        copy.start()
    for i in range(8):
        vectors[i][...] = rows[i : i + 1, 0:short]
    vectors[8][...] = up[...]
    for copy, onward in zip(ins, outs):
        copy.wait()
        onward.start()
    for copy in outs:
        copy.wait()


def results_call(large, rows, up, short):
    vmem, hbm = pl.BlockSpec(memory_space=pltpu.VMEM), pl.BlockSpec(memory_space=pl.ANY)
    shapes = [jax.ShapeDtypeStruct(a.shape, a.dtype) for a in large]
    shapes += [jax.ShapeDtypeStruct((1, short), jnp.float32)] * 8 + [jax.ShapeDtypeStruct(up.shape, jnp.float32)]
    return pl.pallas_call(
        functools.partial(results_kernel, len(large), short),
        out_shape=tuple(shapes),
        in_specs=[hbm] * len(large) + [vmem] * 2,
        out_specs=tuple([hbm] * len(large) + [vmem] * 9),
        scratch_shapes=[pltpu.VMEM(a.shape, a.dtype) for a in large]
        + [pltpu.SemaphoreType.DMA((sum(-(-a.shape[0] // PIECE) for a in large),))] * 2,
        name="results",
    )(*large, rows, up)


def kernel_device(
    tokens, segment, cotangent, query_w, key_w, value_w, attn_out_w, up_w, down_w, query_bias, value_bias,
    attn_out_bias, up_bias, down_bias, norm1_gain, norm1_shift, norm2_gain, norm2_shift,
):
    depth = lax.axis_size(DP) // 2
    weights = (query_w, key_w, value_w, attn_out_w, up_w, jnp.transpose(down_w))
    vectors = (
        query_bias, value_bias, attn_out_bias, down_bias, norm1_gain, norm1_shift, norm2_gain, norm2_shift, up_bias,
    )
    outputs, d_tokens, qw, kw, vw, ow, uw, dw, short_sum, up_sum = layer_call(
        depth, tokens, segment, cotangent, weights, [vector[None] for vector in vectors]
    )
    outputs, d_tokens, qw, kw, vw, ow, uw, dw, *vectors = results_call(
        (outputs, d_tokens, qw, kw, vw, ow, uw, dw), short_sum, up_sum, query_w.shape[0]
    )
    qb, vb, ob, db, g1, s1, g2, s2, ub = [vector.reshape(-1) for vector in vectors]
    return (
        outputs, d_tokens, qw, kw, vw, ow, uw, jnp.transpose(dw), qb, vb, ob, ub, db, g1, s1, g2, s2,
    )


def solution(mesh):
    fits = mesh.shape[FSDP] == 4 and mesh.shape[DP] == 8
    body = kernel_device if fits else plain_device
    in_specs = (
        P(BOTH, None),
        P(BOTH, None),
        P(BOTH, None),
        P(BOTH, None),
        P(BOTH, None),
        P(BOTH, None),
        P(BOTH, None),
        P(BOTH, None),
        P(None, BOTH),
        P(BOTH),
        P(BOTH),
        P(BOTH),
        P(BOTH),
        P(BOTH),
        P(BOTH),
        P(BOTH),
        P(BOTH),
        P(BOTH),
    )
    out_specs = (
        P(BOTH, None),
        P(BOTH, None),
        P(BOTH, None),
        P(BOTH, None),
        P(BOTH, None),
        P(BOTH, None),
        P(BOTH, None),
        P(None, BOTH),
        P(BOTH),
        P(BOTH),
        P(BOTH),
        P(BOTH),
        P(BOTH),
        P(BOTH),
        P(BOTH),
        P(BOTH),
        P(BOTH),
    )
    return jax.shard_map(
        body, mesh=mesh, in_specs=in_specs, out_specs=out_specs, check_vma=False
    )
```

```python
import functools

import jax
import jax.numpy as jnp
from jax import lax
from jax.experimental import pallas as pl
from jax.experimental.pallas import tpu as pltpu
from jax.sharding import PartitionSpec as P

MESH = pl.DeviceIdType.MESH
BLOCKS = 12
DP, FSDP = BOTH = ("dp", "fsdp")


class Place:
    def __init__(self):
        dp, fs = lax.axis_index(DP), lax.axis_index(FSDP)
        z, x, y, c = self.z, self.x, self.y, self.c = dp // 2, dp % 2, fs // 2, fs % 2
        self.fs = fs
        self.near = z + 1 - 2 * (z % 2)
        self.other = 3 - z
        self.low = 2 * (z // 2)
        self.high = 2 - self.low
        self.near_pair, self.far_pair = pl.ds(self.low, 2), pl.ds(self.high, 2)
        self.far_one = z // 2 * -1 + 2
        self.far_two = 3 - z // 2 * 3
        self.inside = (z == 1) | (z == 2)
        self.to_x, self.to_y = device(z, 1 - x, y, c), device(z, x, 1 - y, c)
        self.to_c = device(z, x, y, 1 - c)
        self.to_near, self.to_other = device(self.near, x, y, c), device(self.other, x, y, c)


def device(z, x, y, c):
    return (z * 2 + x, y * 2 + c)


def greet(at):
    bar = pltpu.get_barrier_semaphore()

    def hail(peer):
        pl.semaphore_signal(bar, inc=1, device_id=peer, device_id_type=MESH)

    def meet(*peers):
        for peer in peers:
            hail(peer)
        pl.semaphore_wait(bar, len(peers))

    always = (at.to_c, at.to_x, at.to_y, at.to_near)
    pl.when(at.inside)(lambda: meet(*always, at.to_other))
    pl.when(jnp.logical_not(at.inside))(lambda: meet(*always))


def send(src, dst, ssem, rsem, peer):
    return pltpu.make_async_remote_copy(
        src_ref=src, dst_ref=dst, send_sem=ssem, recv_sem=rsem, device_id=peer, device_id_type=MESH
    )


def numbered(*names):
    return {name: i for i, name in enumerate(names)}


GATHER_GETS = numbered(
    "near", "one", "two", "xn", "yn", "xf", "yf", "da", "db", "df", "xo", "yo",
    "c0", "c1", "c2", "c3", "c4", "c5", "c6", "c7",
)


C_NAMES = list(GATHER_GETS)[-8:]


class GatherBlock:
    def __init__(self, at, full, mine, ss, rs, early=False):
        self.at, self.full, self.mine, self.ss, self.rs, self.early = at, full, mine, ss, rs, early

    def piece(self, name):
        a, full = self.at, self.full
        x, y, c = a.x, a.y, a.c
        both = {"n": a.near_pair, "f": a.far_pair}
        return {
            "own": lambda: full.at[a.z, x, y, c],
            "near": lambda: full.at[a.near, x, y, c],
            "one": lambda: full.at[a.far_one, x, y, c],
            "two": lambda: full.at[a.far_two, x, y, c],
            "on": lambda: full.at[both["n"], x, y, c],
            "of": lambda: full.at[both["f"], x, y, c],
            "xn": lambda: full.at[both["n"], 1 - x, y, c],
            "xf": lambda: full.at[both["f"], 1 - x, y, c],
            "yn": lambda: full.at[both["n"], x, 1 - y, c],
            "yf": lambda: full.at[both["f"], x, 1 - y, c],
            "dn": lambda: full.at[both["n"], 1 - x, 1 - y, c],
            "df": lambda: full.at[both["f"], 1 - x, 1 - y, c],
            "xo": lambda: full.at[a.z, 1 - x, y, c],
            "yo": lambda: full.at[a.z, x, 1 - y, c],
            "x_near": lambda: full.at[a.near, 1 - x, y, c],
            "x_own": lambda: full.at[a.z, 1 - x, y, c],
            "y_near": lambda: full.at[a.near, x, 1 - y, c],
            "d_own": lambda: full.at[a.z, 1 - x, 1 - y, c],
            "d_near": lambda: full.at[a.near, 1 - x, 1 - y, c],
            "c0": lambda: full.at[both["n"], x, y, 1 - c],
            "c1": lambda: full.at[both["f"], x, y, 1 - c],
            "c2": lambda: full.at[both["n"], 1 - x, y, 1 - c],
            "c3": lambda: full.at[both["n"], x, 1 - y, 1 - c],
            "c4": lambda: full.at[both["n"], 1 - x, 1 - y, 1 - c],
            "c5": lambda: full.at[both["f"], 1 - x, y, 1 - c],
            "c6": lambda: full.at[both["f"], x, 1 - y, 1 - c],
            "c7": lambda: full.at[both["f"], 1 - x, 1 - y, 1 - c],
        }[name]()

    SENDS = {
        "own_near": ("own", "near", "to_near"),
        "own_other": ("own", "one", "to_other"),
        "near_other": ("near", "two", "to_other"),
        "one_near": ("one", "one", "to_near"),
        "two_near": ("two", "two", "to_near"),
        "xn": ("on", "xn", "to_x"),
        "yn": ("on", "yn", "to_y"),
        "xo": ("own", "xo", "to_x"),
        "yo": ("own", "yo", "to_y"),
        "xp": ("near", "xn", "to_x"),
        "yp": ("near", "yn", "to_y"),
        "xf": ("of", "xf", "to_x"),
        "yf": ("of", "yf", "to_y"),
        "da": ("x_own", "da", "to_y"),
        "db": ("y_near", "db", "to_x"),
        "d_other": ("dn", "df", "to_other"),
        "d_near": ("df", "df", "to_near"),
        "c0": ("on", "c0", "to_c"),
        "c1": ("of", "c1", "to_c"),
        "c2": ("xn", "c2", "to_c"),
        "c3": ("yn", "c3", "to_c"),
        "c4": ("dn", "c4", "to_c"),
        "c5": ("xf", "c5", "to_c"),
        "c6": ("yf", "c6", "to_c"),
        "c7": ("df", "c7", "to_c"),
    }
    ARRIVES = {"da": "d_own", "db": "d_near"}
    INSIDE = ("own_other", "near_other", "one_near", "two_near", "d_other", "d_near")

    def move(self, name):
        what, called, whom = self.SENDS[name]
        piece = self.piece(what)
        return send(
            piece, piece, self.ss.at[list(self.SENDS).index(name)], self.rs.at[GATHER_GETS[called]], getattr(self.at, whom)
        )

    def go(self, *names):
        for name in names:
            if name in self.INSIDE:
                pl.when(self.at.inside)(lambda: self.move(name).start())
            else:
                self.move(name).start()

    def get(self, name, what=None):
        piece = self.piece(what or self.ARRIVES.get(name, name))
        send(piece, piece, self.ss.at[0], self.rs.at[GATHER_GETS[name]], self.at.to_c).wait_recv()

    def stage(self, s):
        a = self.at
        if s == 0:
            self.full[a.z, a.x, a.y, a.c] = self.mine()
            self.go("own_near", "own_other")
            if self.early:
                self.go("xo", "yo")
        if s == 1:
            self.get("near")
            self.go("near_other")
            if self.early:
                self.go("xp", "yp", "c0")
            else:
                self.go("xn", "yn", "c0")
        if s == 2:
            self.get("one")
            self.go("one_near")
        if s == 3:
            self.get("two")
            self.go("two_near", "xf", "yf", "c1")
        if s == 4:
            if self.early:
                self.get("xo")
                self.go("da")
                self.get("xn", "x_near")
                self.go("c2")
                self.get("yo")
                self.get("yn", "y_near")
            else:
                self.get("xn")
                self.go("da", "c2")
                self.get("yn")
            self.go("db", "c3")
        if s == 5:
            self.get("da")
            self.get("db")
            self.go("d_other", "c4")
        if s == 6:
            self.get("xf")
            self.go("c5")
            self.get("yf")
            self.go("c6")
        if s == 7:
            self.get("df")
            self.go("d_near", "c7")
        if s == 8:
            for i in range(8):
                self.get(C_NAMES[i])
        if s == 9:
            for name in self.SENDS:
                if name not in self.INSIDE + (("xn", "yn") if self.early else ("xo", "yo", "xp", "yp")):
                    self.move(name).wait_send()

            @pl.when(a.inside)
            def _():
                for name in self.INSIDE:
                    self.move(name).wait_send()


GATHER_LAGS = (0, 1, 3, 5, 5, 7, 8, 8, 9, 11)
GATHER_ORDER = (0, 2, 5, 6, 4, 7, 1, 3, 8, 9)


HEAD = 64


norm_epsilon = 1e-12
masked_score = -1000000000.0


def to_half(array):
    return array.astype(jnp.bfloat16)


def matmul(left, right):
    return jnp.dot(left, right, preferred_element_type=jnp.float32)


def matmul_nt(left, right):
    return lax.dot_general(
        left, right, (((1,), (1,)), ((), ())), preferred_element_type=jnp.float32
    )


def contract_rows(left, right):
    return lax.dot_general(
        left, right, (((0,), (0,)), ((), ())), preferred_element_type=jnp.float32
    )


def column_sums(array):
    return jnp.sum(array.astype(jnp.float32), axis=0)


def normalize(values, gain_vec, shift_vec):
    center = values - jnp.mean(values, axis=-1, keepdims=True)
    spread = jnp.mean(center * center, axis=-1, keepdims=True)
    return center * lax.rsqrt(spread + norm_epsilon) * gain_vec + shift_vec


def gelu_exact(values):
    return jax.nn.gelu(values, approximate=False)


def split_heads(block):
    return block.reshape(block.shape[0], -1, HEAD)


def row_scores(queries, key_rows, labels):
    scores = (
        jnp.einsum("qhe,khe->hqk", queries, key_rows, preferred_element_type=jnp.float32) * 0.125
    )
    allowed = labels[:, None] == labels[None, :]
    return jnp.where(allowed[None], scores, masked_score)


def attend_row(pieces):
    queries, key_rows, value_rows, labels = pieces
    scores = row_scores(split_heads(queries), split_heads(key_rows), labels)
    row_max = jnp.max(scores, axis=-1, keepdims=True)
    row_exp = jnp.exp(scores - row_max)
    row_total = jnp.sum(row_exp, axis=-1, keepdims=True)
    probs_half = to_half(row_exp / row_total)
    context = jnp.einsum(
        "hqk,khe->qhe", probs_half, split_heads(value_rows), preferred_element_type=jnp.float32
    )
    return (to_half(context.reshape(queries.shape)), (row_max + jnp.log(row_total))[..., 0])


def attend_back(pieces):
    queries, key_rows, value_rows, labels, log_total, d_context = pieces
    query_heads = split_heads(queries)
    key_heads = split_heads(key_rows)
    context_heads = split_heads(d_context)
    scores = row_scores(query_heads, key_heads, labels)
    attn_probs = jnp.exp(scores - log_total[..., None])
    d_probs = jnp.einsum(
        "qhe,khe->hqk", context_heads, split_heads(value_rows), preferred_element_type=jnp.float32
    )
    row_delta = jnp.sum(attn_probs * d_probs, axis=-1, keepdims=True)
    d_scores = to_half(attn_probs * (d_probs - row_delta))
    d_queries = (
        jnp.einsum("hqk,khe->qhe", d_scores, key_heads, preferred_element_type=jnp.float32) * 0.125
    )
    d_keys = (
        jnp.einsum("hqk,qhe->khe", d_scores, query_heads, preferred_element_type=jnp.float32)
        * 0.125
    )
    d_values = jnp.einsum(
        "hqk,qhe->khe", to_half(attn_probs), context_heads, preferred_element_type=jnp.float32
    )
    return (
        to_half(d_queries.reshape(queries.shape)),
        to_half(d_keys.reshape(queries.shape)),
        to_half(d_values.reshape(queries.shape)),
    )


def plain_device(
    tokens,
    segment,
    cotangent,
    query_w,
    key_w,
    value_w,
    attn_out_w,
    up_w,
    down_w,
    query_bias,
    value_bias,
    attn_out_bias,
    up_bias,
    down_bias,
    norm1_gain,
    norm1_shift,
    norm2_gain,
    norm2_shift,
):
    row_count = segment.shape[0]
    row_length = segment.shape[1]
    model_width = tokens.shape[1]

    def by_rows(array):
        return array.reshape(row_count, row_length, -1)

    attn_set = (
        lax.all_gather(to_half(query_w), BOTH, axis=0, tiled=True),
        lax.all_gather(to_half(key_w), BOTH, axis=0, tiled=True),
        lax.all_gather(to_half(value_w), BOTH, axis=0, tiled=True),
        lax.all_gather(to_half(attn_out_w), BOTH, axis=0, tiled=True),
        lax.all_gather(to_half(query_bias), BOTH, axis=0, tiled=True),
        lax.all_gather(to_half(value_bias), BOTH, axis=0, tiled=True),
        lax.all_gather(to_half(attn_out_bias), BOTH, axis=0, tiled=True),
        lax.all_gather(to_half(norm1_gain), BOTH, axis=0, tiled=True),
        lax.all_gather(to_half(norm1_shift), BOTH, axis=0, tiled=True),
    )
    wq_full, wk_full, wv_full, wo_full, bias_q, bias_v, bias_o, gain_one, shift_one = attn_set
    ffn_set = (
        lax.all_gather(to_half(up_w), BOTH, axis=0, tiled=True),
        lax.all_gather(to_half(down_w), BOTH, axis=1, tiled=True),
        lax.all_gather(to_half(up_bias), BOTH, axis=0, tiled=True),
        lax.all_gather(to_half(down_bias), BOTH, axis=0, tiled=True),
        lax.all_gather(to_half(norm2_gain), BOTH, axis=0, tiled=True),
        lax.all_gather(to_half(norm2_shift), BOTH, axis=0, tiled=True),
    )
    w_up, w_down, bias_up, bias_down, gain_two, shift_two = ffn_set
    queries = to_half(matmul(tokens, wq_full) + bias_q.astype(jnp.float32))
    key_rows = to_half(matmul(tokens, wk_full))
    value_rows = to_half(matmul(tokens, wv_full) + bias_v.astype(jnp.float32))
    context, log_total = lax.map(
        attend_row, (by_rows(queries), by_rows(key_rows), by_rows(value_rows), segment)
    )
    context = context.reshape(-1, model_width)
    attended = matmul(context, wo_full) + bias_o.astype(jnp.float32)
    first_sum = tokens.astype(jnp.float32) + attended
    norm_mid, pull_one = jax.vjp(
        normalize, first_sum, gain_one.astype(jnp.float32), shift_one.astype(jnp.float32)
    )
    mid_half = to_half(norm_mid)
    pre_act = matmul(mid_half, w_up) + bias_up.astype(jnp.float32)
    act_out, pull_act = jax.vjp(gelu_exact, pre_act)
    act_half = to_half(act_out)
    ffn_out = matmul(act_half, w_down) + bias_down.astype(jnp.float32)
    second_sum = mid_half.astype(jnp.float32) + ffn_out
    final, pull_two = jax.vjp(
        normalize, second_sum, gain_two.astype(jnp.float32), shift_two.astype(jnp.float32)
    )
    outputs = to_half(final)
    valid = (segment.reshape(-1) >= 0).astype(jnp.float32)[:, None]
    d_out = cotangent.astype(jnp.float32) * valid
    d_second, d_gain_two, d_shift_two = pull_two(d_out)
    up_back, down_back = (
        lax.all_gather(to_half(up_w), BOTH, axis=0, tiled=True),
        lax.all_gather(to_half(down_w), BOTH, axis=1, tiled=True),
    )
    d_ffn = to_half(d_second)
    d_down_turned = contract_rows(d_ffn, act_half)
    d_down_bias = column_sums(d_ffn)
    (d_pre,) = pull_act(matmul_nt(d_ffn, down_back))
    d_pre_half = to_half(d_pre)
    d_up_w = contract_rows(mid_half, d_pre_half)
    d_up_bias = column_sums(d_pre_half)
    d_mid = d_second + matmul_nt(d_pre_half, up_back)
    d_first, d_gain_one, d_shift_one = pull_one(d_mid)
    wq_back, wk_back, wv_back, wo_back = (
        lax.all_gather(to_half(query_w), BOTH, axis=0, tiled=True),
        lax.all_gather(to_half(key_w), BOTH, axis=0, tiled=True),
        lax.all_gather(to_half(value_w), BOTH, axis=0, tiled=True),
        lax.all_gather(to_half(attn_out_w), BOTH, axis=0, tiled=True),
    )
    d_att = to_half(d_first)
    d_attn_out_w = contract_rows(context, d_att)
    d_attn_out_bias = column_sums(d_att)
    d_context = to_half(matmul_nt(d_att, wo_back))
    d_queries, d_keys, d_values = lax.map(
        attend_back,
        (
            by_rows(queries),
            by_rows(key_rows),
            by_rows(value_rows),
            segment,
            log_total,
            by_rows(d_context),
        ),
    )
    d_queries = d_queries.reshape(-1, model_width)
    d_keys = d_keys.reshape(-1, model_width)
    d_values = d_values.reshape(-1, model_width)
    d_query_w = contract_rows(tokens, d_queries)
    d_key_w = contract_rows(tokens, d_keys)
    d_value_w = contract_rows(tokens, d_values)
    d_query_bias = column_sums(d_queries)
    d_value_bias = column_sums(d_values)
    d_tokens = (
        d_first
        + matmul_nt(d_queries, wq_back)
        + matmul_nt(d_keys, wk_back)
        + matmul_nt(d_values, wv_back)
    )
    members = (
        d_query_w,
        d_key_w,
        d_value_w,
        d_attn_out_w,
        d_up_w,
        d_down_turned,
        d_query_bias,
        d_value_bias,
        d_attn_out_bias,
        d_up_bias,
        d_down_bias,
        d_gain_one,
        d_shift_one,
        d_gain_two,
        d_shift_two,
    )
    block_sums = (
        lax.psum_scatter(
            members[0].astype(jnp.bfloat16), DP, scatter_dimension=0, tiled=True
        ).astype(jnp.float32),
        lax.psum_scatter(
            members[1].astype(jnp.bfloat16), DP, scatter_dimension=0, tiled=True
        ).astype(jnp.float32),
        lax.psum_scatter(
            members[2].astype(jnp.bfloat16), DP, scatter_dimension=0, tiled=True
        ).astype(jnp.float32),
        lax.psum_scatter(
            members[3].astype(jnp.bfloat16), DP, scatter_dimension=0, tiled=True
        ).astype(jnp.float32),
        lax.psum_scatter(
            members[4].astype(jnp.bfloat16), DP, scatter_dimension=0, tiled=True
        ).astype(jnp.float32),
        lax.psum_scatter(
            members[5].astype(jnp.bfloat16), DP, scatter_dimension=0, tiled=True
        ).astype(jnp.float32),
        lax.psum_scatter(
            members[6].astype(jnp.bfloat16), DP, scatter_dimension=0, tiled=True
        ).astype(jnp.float32),
        lax.psum_scatter(
            members[7].astype(jnp.bfloat16), DP, scatter_dimension=0, tiled=True
        ).astype(jnp.float32),
        lax.psum_scatter(
            members[8].astype(jnp.bfloat16), DP, scatter_dimension=0, tiled=True
        ).astype(jnp.float32),
        lax.psum_scatter(
            members[9].astype(jnp.bfloat16), DP, scatter_dimension=0, tiled=True
        ).astype(jnp.float32),
        lax.psum_scatter(
            members[10].astype(jnp.bfloat16), DP, scatter_dimension=0, tiled=True
        ).astype(jnp.float32),
        lax.psum_scatter(
            members[11].astype(jnp.bfloat16), DP, scatter_dimension=0, tiled=True
        ).astype(jnp.float32),
        lax.psum_scatter(
            members[12].astype(jnp.bfloat16), DP, scatter_dimension=0, tiled=True
        ).astype(jnp.float32),
        lax.psum_scatter(
            members[13].astype(jnp.bfloat16), DP, scatter_dimension=0, tiled=True
        ).astype(jnp.float32),
        lax.psum_scatter(
            members[14].astype(jnp.bfloat16), DP, scatter_dimension=0, tiled=True
        ).astype(jnp.float32),
    )
    every_shard = (
        lax.psum_scatter(
            block_sums[0].astype(jnp.bfloat16), FSDP, scatter_dimension=0, tiled=True
        ).astype(jnp.float32),
        lax.psum_scatter(
            block_sums[1].astype(jnp.bfloat16), FSDP, scatter_dimension=0, tiled=True
        ).astype(jnp.float32),
        lax.psum_scatter(
            block_sums[2].astype(jnp.bfloat16), FSDP, scatter_dimension=0, tiled=True
        ).astype(jnp.float32),
        lax.psum_scatter(
            block_sums[3].astype(jnp.bfloat16), FSDP, scatter_dimension=0, tiled=True
        ).astype(jnp.float32),
        lax.psum_scatter(
            block_sums[4].astype(jnp.bfloat16), FSDP, scatter_dimension=0, tiled=True
        ).astype(jnp.float32),
        lax.psum_scatter(
            block_sums[5].astype(jnp.bfloat16), FSDP, scatter_dimension=0, tiled=True
        ).astype(jnp.float32),
        lax.psum_scatter(
            block_sums[6].astype(jnp.bfloat16), FSDP, scatter_dimension=0, tiled=True
        ).astype(jnp.float32),
        lax.psum_scatter(
            block_sums[7].astype(jnp.bfloat16), FSDP, scatter_dimension=0, tiled=True
        ).astype(jnp.float32),
        lax.psum_scatter(
            block_sums[8].astype(jnp.bfloat16), FSDP, scatter_dimension=0, tiled=True
        ).astype(jnp.float32),
        lax.psum_scatter(
            block_sums[9].astype(jnp.bfloat16), FSDP, scatter_dimension=0, tiled=True
        ).astype(jnp.float32),
        lax.psum_scatter(
            block_sums[10].astype(jnp.bfloat16), FSDP, scatter_dimension=0, tiled=True
        ).astype(jnp.float32),
        lax.psum_scatter(
            block_sums[11].astype(jnp.bfloat16), FSDP, scatter_dimension=0, tiled=True
        ).astype(jnp.float32),
        lax.psum_scatter(
            block_sums[12].astype(jnp.bfloat16), FSDP, scatter_dimension=0, tiled=True
        ).astype(jnp.float32),
        lax.psum_scatter(
            block_sums[13].astype(jnp.bfloat16), FSDP, scatter_dimension=0, tiled=True
        ).astype(jnp.float32),
        lax.psum_scatter(
            block_sums[14].astype(jnp.bfloat16), FSDP, scatter_dimension=0, tiled=True
        ).astype(jnp.float32),
    )
    (
        shard_qw,
        shard_kw,
        shard_vw,
        shard_ow,
        shard_uw,
        shard_turned,
        shard_qb,
        shard_vb,
        shard_ob,
        shard_ub,
        shard_db,
        shard_g1,
        shard_s1,
        shard_g2,
        shard_s2,
    ) = every_shard
    shard_dw = jnp.transpose(shard_turned)
    return (
        outputs,
        d_tokens,
        shard_qw,
        shard_kw,
        shard_vw,
        shard_ow,
        shard_uw,
        shard_dw,
        shard_qb,
        shard_vb,
        shard_ob,
        shard_ub,
        shard_db,
        shard_g1,
        shard_s1,
        shard_g2,
        shard_s2,
    )


ATTN = 4
NORM_ROWS = 256
LANES = 128
SIDE = 1024
V_LANE, R_LANE = 32, 64


def aligned(start, size, step=None):
    return pl.ds(pl.multiple_of(start, step or size), size)


def side_loop(count, body):
    def step(i, carry):
        body(i)
        return carry

    lax.fori_loop(0, count, step, 0)


def square(full, b):
    size = full.shape[-1]
    return full.at[b].reshape(size, size)


def spread_vectors(tiles, short_ref, up_ref, depth):
    for dp in range(2 * depth):
        total = jnp.zeros((16, LANES), jnp.float32)
        for fs in range(4):
            total = total + tiles[dp // 2, dp % 2, fs // 2, fs % 2].astype(jnp.float32)
        short_ref[:, dp * LANES : (dp + 1) * LANES] = total[:8]
        for fs in range(4):
            at = (dp * 4 + fs) * LANES
            up_ref[:, at : at + LANES] = total[8 + fs : 9 + fs]


def stepwise(body, after):
    def step(i):
        body(i)
        for k, follow in enumerate(after):
            pl.when(i == k)(follow)

    side_loop(len(after), step)


def nothing():
    pass


def attend_pairs(first, last, qkvc, lse, mask):
    length = mask.shape[0]

    def pair(p):
        lanes = aligned(p * LANES, LANES)
        q, k, v = qkvc[0, :, lanes], qkvc[1, :, lanes], qkvc[2, :, lanes]
        lane = lax.broadcasted_iota(jnp.int32, (length, LANES), 1)
        lower = lane < HEAD
        total = jnp.zeros((length, LANES), jnp.float32)
        logs = lse[...]
        for h in range(2):
            here = lower if h == 0 else jnp.logical_not(lower)
            key = jnp.where(here, k, jnp.zeros_like(k))
            scores = matmul_nt(q, key) + mask[...]
            row_max = jnp.max(scores, axis=-1, keepdims=True)
            row_exp = jnp.exp(scores - row_max)
            row_total = jnp.sum(row_exp, axis=-1, keepdims=True)
            part = matmul(to_half(row_exp), v) / row_total
            total = jnp.where(here, part, total)
            logs = jnp.where(lane == 2 * p + h, row_max + jnp.log(row_total), logs)
        qkvc[3, :, lanes] = to_half(total)
        lse[...] = logs

    def step(i, carry):
        pair(i)
        return carry

    lax.fori_loop(first, last, step, 0)


SUM_SENDS = numbered("c", "df", "dg", "da", "db", "xn", "yn", "xf", "yf", "f", "m", "n")
SUM_LAGS = (0, 1, 2, 3, 4, 3, 5, 6, 7)
SUM_ORDER = (6, 3, 1, 2, 4, 5, 0, 7, 8)
SUM_BUFFERS = {
    "grad": (2, (4, 2, 2, 2)),
    "held": (7, (4, 2, 2)),
    "c": (2, (4, 2, 2)),
    "df": (7, (2,)),
    "dg": (2, (2,)),
    "da": (4, ()),
    "db": (4, ()),
    "xn": (5, (2,)),
    "yn": (4, (2,)),
    "xf": (5, (2,)),
    "yf": (5, (2,)),
    "f": (5, (2,)),
    "m": (4, (2,)),
    "n": (4, ()),
}


def sum_scratch(rows, cols, blocks, names):
    bufs = [SUM_BUFFERS[name] for name in names]
    bufs = [pltpu.VMEM((min(slots, blocks),) + parts + (rows, cols), jnp.bfloat16) for slots, parts in bufs]
    return bufs + [pltpu.SemaphoreType.DMA((blocks, len(SUM_SENDS)))] * 2


class SumBlock:
    def __init__(self, at, refs, names, b, **others):
        self.at = at
        *bufs, ss, rs = refs
        self.ss, self.rs = ss.at[b], rs.at[b]
        self.buf = {n: ref.at[b % ref.shape[0]] for n, ref in zip(names, bufs)} | others

    def move(self, name):
        a, held = self.at, self.buf["held"]
        x, y = a.x, a.y
        every, both = pl.ds(0, 4), pl.ds(0, 2)
        src, to = {
            "c": lambda: (self.buf["grad"].at[every, both, both, 1 - a.c], a.to_c),
            "df": lambda: (held.at[a.far_pair, 1 - x, 1 - y], a.to_near),
            "dg": lambda: (held.at[a.far_pair, 1 - x, 1 - y], a.to_other),
            "da": lambda: (held.at[a.z, 1 - x, 1 - y], a.to_y),
            "db": lambda: (held.at[a.near, 1 - x, 1 - y], a.to_x),
            "xn": lambda: (held.at[a.near_pair, 1 - x, y], a.to_x),
            "yn": lambda: (held.at[a.near_pair, x, 1 - y], a.to_y),
            "xf": lambda: (held.at[a.far_pair, 1 - x, y], a.to_x),
            "yf": lambda: (held.at[a.far_pair, x, 1 - y], a.to_y),
            "f": lambda: (held.at[a.far_pair, x, y], a.to_near),
            "m": lambda: (held.at[a.far_pair, x, y], a.to_other),
            "n": lambda: (held.at[a.near, x, y], a.to_near),
        }[name]()
        i = SUM_SENDS[name]
        return send(src, self.buf[name], self.ss.at[i], self.rs.at[i], to)

    def start(self, name):
        self.move(name).start()

    def got(self, name):
        self.move(name).wait_recv()
        return self.buf[name]

    def stage(self, s, out=None):
        a, held, grad = self.at, self.buf["held"], self.buf["grad"]
        x, y, c = a.x, a.y, a.c
        inside = a.inside
        outside = jnp.logical_not(inside)

        def add(first, xx, yy, *others, count=2):
            for i in range(count):
                total = held[first + i, xx, yy].astype(jnp.float32)
                for other in others:
                    total = total + (other[i] if count == 2 else other[...]).astype(jnp.float32)
                held[first + i, xx, yy] = total.astype(jnp.bfloat16)

        if s == 0:
            self.start("c")
        if s == 1:
            self.move("c").wait()
            pair = self.buf["c"]

            def join(first, xx, yy):
                for i in range(2):
                    held[first + i, xx, yy] = grad[first + i, xx, yy, c] + pair[first + i, xx, yy]

            join(a.high, 1 - x, 1 - y)
            pl.when(outside)(lambda: self.start("df"))
            join(a.high, 1 - x, y)
            self.start("xf")
            join(a.high, x, 1 - y)
            self.start("yf")
            join(a.low, 1 - x, 1 - y)
            join(a.low, 1 - x, y)
            join(a.low, x, 1 - y)
            join(a.high, x, y)
            join(a.low, x, y)
        if s == 2:

            @pl.when(inside)
            def _():
                add(a.high, 1 - x, 1 - y, self.got("df"))
                self.start("dg")

        if s == 3:

            @pl.when(inside)
            def _():
                add(a.low, 1 - x, 1 - y, self.got("dg"))

            self.start("da")
            self.start("db")
        if s == 4:
            add(a.z, 1 - x, y, self.got("da"), count=1)
            self.start("xn")
            add(a.near, x, 1 - y, self.got("db"), count=1)
            self.start("yn")
        if s == 5:
            add(a.high, x, y, self.got("xf"), self.got("yf"))
            pl.when(outside)(lambda: self.start("f"))
        if s == 6:

            @pl.when(inside)
            def _():
                add(a.high, x, y, self.got("f"))
                self.start("m")

        if s == 7:
            add(a.low, x, y, self.got("xn"), self.got("yn"))

            @pl.when(inside)
            def _():
                add(a.low, x, y, self.got("m"))

            self.start("n")
        if s == 8:
            out[...] = held[a.z, x, y].astype(jnp.float32) + self.got("n")[...].astype(jnp.float32)
            for name in ("da", "db", "xn", "yn", "xf", "yf", "n"):
                self.move(name).wait_send()

            @pl.when(inside)
            def _():
                self.move("dg").wait_send()
                self.move("m").wait_send()

            @pl.when(outside)
            def _():
                self.move("df").wait_send()
                self.move("f").wait_send()


def attend_back_pairs(first, last, qkvc, lse, delta, mask, grads):
    length = mask.shape[0]

    def pair(p, carry):
        lanes = aligned(p * LANES, LANES)
        q, k, v, d_context = qkvc[0, :, lanes], qkvc[1, :, lanes], qkvc[2, :, lanes], grads[3, :, lanes]
        lower = lax.broadcasted_iota(jnp.int32, (length, LANES), 1) < HEAD
        sums = [jnp.zeros((length, LANES), jnp.float32) for _ in range(3)]
        for h in range(2):
            here = lower if h == 0 else jnp.logical_not(lower)
            row = pl.ds(2 * p + h, 1)
            key = jnp.where(here, k, jnp.zeros_like(k))
            value = jnp.where(here, v, jnp.zeros_like(v))
            probs = jnp.exp(matmul_nt(key, q) + mask[...] - lse[row, :])
            d_scores = to_half(probs * (matmul_nt(value, d_context) - delta[row, :]))
            parts = (
                contract_rows(d_scores, k) * 0.125,
                matmul(d_scores, q),
                matmul(to_half(probs), d_context),
            )
            sums = [jnp.where(here, part, total) for part, total in zip(parts, sums)]
        for i in range(3):
            grads[i, :, lanes] = to_half(sums[i])
        return carry

    lax.fori_loop(first, last, pair, 0)


SUM_NAMES = tuple(SUM_BUFFERS)
LENT = SUM_NAMES[:2]
OWN_BUFFERS = SUM_NAMES[2:]


def layer_kernel(depth, *refs):
    tokens_hbm, segment, cotangent_hbm, wq, wk, wv, wo, up_w, down_w, *vectors = refs[:18]
    out_hbm, dtok_hbm, gq, gk, gv, go, gup, gdown, gshort, gup_bias = refs[18:28]
    (
        full, tiles, mine_vec, short, up_bias, qkvc, lse, lse_turned, mask, mid, act, dge, nhat, total, half,
        turn_a, delta_turned, cotangent, vgrads, tile_sum, spare, staged, ss, rs, isem, osem, *rest,
    ) = refs[28:]
    count = len(OWN_BUFFERS) + 2
    big, vec = rest[:count], rest[count:]
    length, width = mid.shape
    tokens = mid
    here = Place()
    fs = here.fs
    rows = wq.shape[0]
    f32 = jnp.float32

    shards = [wq, wk, wv, wo]
    for wide in (up_w, down_w):
        shards += [wide.at[:, i * width : (i + 1) * width] for i in range(ATTN)]
    loads = [
        pltpu.make_async_copy(src, total.at[i * rows : (i + 1) * rows], isem.at[i]) for i, src in enumerate(shards)
    ]
    loads.append(pltpu.make_async_copy(tokens_hbm, tokens, isem.at[BLOCKS]))
    loads.append(pltpu.make_async_copy(cotangent_hbm, cotangent, isem.at[BLOCKS + 1]))
    for load in loads:
        load.start()
    greet(here)

    def own(b):
        loads[b].wait()
        return to_half(total[b * rows : (b + 1) * rows, :])

    def gather_block(b):
        return GatherBlock(here, full.at[b], lambda: own(b), ss.at[b], rs.at[b], True)

    def own_vectors():
        mine_vec[...] = jnp.zeros_like(mine_vec)
        for i in range(8):
            mine_vec[i : i + 1, 0:rows] = vectors[i][...]
        placed = pltpu.roll(mine_vec[...], fs * rows, 1)
        row_at = lax.broadcasted_iota(jnp.int32, (16, LANES), 0)
        mine_vec[...] = jnp.where(row_at == 8 + fs, jnp.broadcast_to(vectors[8][...], (16, LANES)), placed)
        return to_half(mine_vec[...])

    own_tiles = GatherBlock(here, tiles, own_vectors, ss.at[BLOCKS], rs.at[BLOCKS])

    def gather_pump(t):
        for s in GATHER_ORDER:
            b = t - GATHER_LAGS[s]
            if 0 <= b < BLOCKS:
                gather_block(b).stage(s)
            if b == 0:
                own_tiles.stage(s)

    gather_pump(0)
    gather_pump(1)
    labels = segment[...].astype(jnp.float32)
    turned = jnp.transpose(jnp.broadcast_to(labels, (LANES, length)))
    mask[...] = jnp.where(turned[:, :1] == labels, 0.0, masked_score)
    lse[...] = jnp.where(turned >= 0.0, 1.0, 0.0)
    ready = GATHER_LAGS[8]
    for t in range(2, ready + 1):
        gather_pump(t)
    spread_vectors(tiles, short, up_bias, depth)
    loads[BLOCKS].wait()

    def project(i):
        biased = jnp.where(i == 1, 0.0, 1.0)
        scale = jnp.where(i == 0, 0.125, 1.0)
        bias = short[pl.ds(i // 2, 1), :] * biased
        qkvc[i] = to_half(to_half(matmul(tokens[...], square(full, i)[...]) + bias).astype(f32) * scale)

    stepwise(project, [lambda: gather_pump(ready + 1), lambda: gather_pump(ready + 2), nothing])
    stepwise(
        lambda i: attend_pairs(i * 4, i * 4 + 4, qkvc, lse, mask),
        [lambda: gather_pump(ready + 3), nothing],
    )
    lse_turned[...] = jnp.transpose(lse[...])[: lse_turned.shape[0]]
    gather_pump(ready + 4)

    wo_full = square(full, 3)

    def attended(n):
        cols = aligned(n * SIDE, SIDE)
        total[:, cols] = (
            matmul(qkvc[3], wo_full[:, cols]) + short[2:3, cols] + tokens[:, cols].astype(jnp.float32)
        )

    side_loop(width // SIDE, attended)

    lane_at = lax.broadcasted_iota(jnp.int32, (NORM_ROWS, LANES), 1)

    def first_norm(i):
        at = aligned(i * NORM_ROWS, NORM_ROWS)
        values = total[at, :]
        center = values - jnp.mean(values, axis=-1, keepdims=True)
        spread = jnp.mean(center * center, axis=-1, keepdims=True)
        r = lax.rsqrt(spread + norm_epsilon)
        unit = center * r
        nhat[at, :] = to_half(unit)
        lse[at, :] = jnp.where(lane_at >= R_LANE, r, lse[at, :])
        mid[at, :] = to_half(unit * short[4:5, :] + short[5:6, :])

    side_loop(length // NORM_ROWS, first_norm)

    def activate(j):
        weight = square(full, ATTN + j)
        for part in range(2):
            cols = slice(part * width // 2, (part + 1) * width // 2)
            pre = matmul(mid[...], weight[:, cols]) + up_bias[:, aligned(j * width + part * width // 2, width // 2)]
            cdf = 0.5 * (1.0 + lax.erf(pre * 0.7071067811865476))
            act[j, :, cols] = to_half(pre * cdf)
            pdf = jnp.exp(-0.5 * pre * pre) * 0.3989422804014327
            dge[j, :, cols] = to_half(cdf + pre * pdf)

    def contract(j):
        total[...] = total[...] + matmul_nt(act[j], square(full, 2 * ATTN + j)[...])

    gather_pump(ready + 5)
    stepwise(activate, [lambda: gather_pump(ready + 6), lambda: gather_pump(ready + 7), lambda: gather_pump(ready + 8), nothing])
    total[...] = mid[...].astype(f32) + short[3:4, :]
    stepwise(contract, [lambda: gather_pump(ready + 9), lambda: gather_pump(ready + 10), lambda: gather_pump(ready + 11), nothing])

    loads[BLOCKS + 1].wait()
    vgrads[...] = jnp.zeros_like(vgrads)

    def second_norm(i):
        at = aligned(i * NORM_ROWS, NORM_ROWS)
        values = total[at, :]
        center = values - jnp.mean(values, axis=-1, keepdims=True)
        spread = jnp.mean(center * center, axis=-1, keepdims=True)
        r = lax.rsqrt(spread + norm_epsilon)
        unit = center * r
        gain = short[6:7, :]
        final = to_half(unit * gain + short[7:8, :])
        e = cotangent[at, :].astype(jnp.float32) * lse[at, V_LANE : V_LANE + 1]
        cotangent[at, :] = final
        vgrads[6:7, :] = vgrads[6:7, :] + jnp.sum(e * unit, axis=0, keepdims=True)
        vgrads[7:8, :] = vgrads[7:8, :] + jnp.sum(e, axis=0, keepdims=True)
        eg = e * gain
        d = r * (
            eg - jnp.mean(eg, axis=-1, keepdims=True) - unit * jnp.mean(eg * unit, axis=-1, keepdims=True)
        )
        total[at, :] = d
        half[at, :] = to_half(d)
        vgrads[3:4, :] = vgrads[3:4, :] + jnp.sum(to_half(d).astype(jnp.float32), axis=0, keepdims=True)

    side_loop(length // NORM_ROWS, second_norm)
    pltpu.make_async_copy(cotangent, out_hbm, osem.at[0]).start()

    outs = [gdown.at[:, i * width : (i + 1) * width] for i in range(4)]
    outs += [gup.at[:, i * width : (i + 1) * width] for i in range(4)] + [go, gv, gk, gq]

    held_at = [(4, 0), (4, 1), (9, 0), (9, 1), (5, 0), (5, 1), (10, 0)]

    def grad_of(b):
        return spare.at[b % 2]

    def block(b):
        gathered, half_at = held_at[b % len(held_at)]
        lent = dict(zip(LENT, (grad_of(b), full.at[gathered, :, :, :, half_at])))
        return SumBlock(here, big, OWN_BUFFERS, b, **lent)

    vblock = SumBlock(here, vec, SUM_NAMES, 0)
    turn_b = square(full, 6).at[:, 0:length]

    def leave(b):
        return pltpu.make_async_copy(staged.at[b % 2], outs[b], osem.at[2 + b % 2])

    def pump(t):
        for s in SUM_ORDER:
            b = t - SUM_LAGS[s]
            if 0 <= b < BLOCKS:
                if s == 8 and b > 1:
                    leave(b - 2).wait()
                block(b).stage(s, staged.at[b % 2])
                if s == 8:
                    leave(b).start()
            if b == BLOCKS - 1:
                vblock.stage(s, tile_sum)

    def weight_grad(b, left, right):
        grad = grad_of(b)
        for part in range(2):
            got = to_half(matmul(left[part * width // 2 : (part + 1) * width // 2, :], right[...]))
            grad[2 * part : 2 * part + 2] = got.reshape((2,) + grad.shape[1:])

    def sums_of(values):
        return jnp.sum(values.astype(f32), axis=0, keepdims=True)

    turn_a[...] = jnp.transpose(half[...])
    weight_grad(0, turn_a, act.at[0])
    pump(0)
    for t in range(ready + 12, BLOCKS + max(GATHER_LAGS)):
        gather_pump(t)

    up_grads = up_bias

    def units_back(j):
        d_pre = to_half(matmul(half[...], square(full, 2 * ATTN + j)[...]) * dge[j].astype(f32))
        dge[j] = d_pre
        up_grads[:, aligned(j * width, width)] = sums_of(d_pre)
        add_product(dge.at[j], square(full, ATTN + j))

        @pl.when(j < ATTN - 1)
        def _():
            weight_grad(j + 1, turn_a, act.at[j + 1])

    def add_product(left, weight):
        total[...] = total[...] + matmul_nt(left[...], weight[...])

    stepwise(units_back, [lambda: pump(1), lambda: pump(2), lambda: pump(3), nothing])
    turn_b[...] = jnp.transpose(mid[...])
    loads[BLOCKS].start()
    weight_grad(4, turn_b, dge.at[0])
    pump(4)


    def first_norm_back(i):
        at = aligned(i * NORM_ROWS, NORM_ROWS)
        e = total[at, :]
        unit = nhat[at, :].astype(f32)
        vgrads[4:5, :] = vgrads[4:5, :] + jnp.sum(e * unit, axis=0, keepdims=True)
        vgrads[5:6, :] = vgrads[5:6, :] + jnp.sum(e, axis=0, keepdims=True)
        eg = e * short[4:5, :]
        d = lse[at, R_LANE : R_LANE + 1] * (
            eg - jnp.mean(eg, axis=-1, keepdims=True) - unit * jnp.mean(eg * unit, axis=-1, keepdims=True)
        )
        total[at, :] = d
        d_half = to_half(d)
        half[at, :] = d_half
        vgrads[2:3, :] = vgrads[2:3, :] + jnp.sum(d_half.astype(f32), axis=0, keepdims=True)

    side_loop(length // NORM_ROWS, first_norm_back)
    wo_full = square(full, 3)
    delta = lse

    def context_back(n):
        cols = aligned(n * SIDE, SIDE)
        d_context = to_half(matmul_nt(half[...], wo_full[cols, :]))
        act[3, :, cols] = d_context
        product = d_context.astype(f32) * qkvc[3, :, cols].astype(f32)
        lane = lax.broadcasted_iota(jnp.int32, (length, LANES), 1)
        got = delta[...]
        for i in range(SIDE // HEAD):
            two = product[:, (i // 2) * LANES : (i // 2 + 1) * LANES]
            here = lane // HEAD == i % 2
            head = jnp.sum(jnp.where(here, two, 0.0), axis=-1, keepdims=True)
            got = jnp.where(lane == n * (SIDE // HEAD) + i, head, got)
        delta[...] = got

    side_loop(width // SIDE, context_back)
    delta_turned[...] = jnp.transpose(delta[...])[: delta_turned.shape[0]]
    weight_grad(5, turn_b, dge.at[1])
    pump(5)

    def attention_step(i):
        attend_back_pairs(3 * i, jnp.minimum(3 * i + 3, 8), qkvc, lse_turned, delta_turned, mask, act)

        @pl.when(i < 2)
        def _():
            weight_grad(6 + i, turn_b, dge.at[2 + i])

    stepwise(attention_step, [lambda: pump(6), lambda: pump(7), nothing])
    turn_a[...] = jnp.transpose(qkvc[3])
    weight_grad(8, turn_a, half)
    pump(8)
    loads[BLOCKS].wait()
    turn_b[...] = jnp.transpose(tokens[...])

    def place_vectors():
        vgrads[0:1, :] = sums_of(act[0])
        vgrads[1:2, :] = sums_of(act[2])
        for dp in range(2 * depth):
            for fsdp in range(4):
                at = (dp * 4 + fsdp) * LANES
                vec[0][0, dp // 2, dp % 2, fsdp // 2, fsdp % 2] = to_half(
                    jnp.concatenate(
                        [
                            vgrads[:, dp * LANES : (dp + 1) * LANES],
                            jnp.broadcast_to(up_grads[:, at : at + LANES], (8, LANES)),
                        ],
                        axis=0,
                    )
                )

    def middle_pump():
        pump(9)
        place_vectors()

    stepwise(
        lambda i: weight_grad(9 + i, turn_b, act.at[2 - i]), [middle_pump, lambda: pump(10), lambda: pump(11)]
    )

    def hand_back():
        pltpu.make_async_copy(total, dtok_hbm, osem.at[1]).start()
        pump(14)

    stepwise(
        lambda i: add_product(act.at[2 - i], square(full, 2 - i)), [lambda: pump(12), lambda: pump(13), hand_back]
    )
    for t in range(15, BLOCKS + max(SUM_LAGS)):
        pump(t)
    leave(BLOCKS - 2).wait()
    leave(BLOCKS - 1).wait()
    moved = pltpu.roll(tile_sum[...], (4 - fs) * rows % LANES, 1)
    gshort[...] = moved[:8]
    gup_bias[...] = tile_sum[8:9, :]
    pltpu.make_async_copy(total, dtok_hbm, osem.at[1]).wait()
    pltpu.make_async_copy(cotangent, out_hbm, osem.at[0]).wait()


def layer_call(depth, tokens, segment, cotangent, weights, vectors):
    length, width = tokens.shape
    rows = weights[0].shape[0]
    dims = (depth, 2, 2, 2)
    bf, f32 = jnp.bfloat16, jnp.float32
    part = ((rows, width), f32)
    shapes = [
        ((length, width), bf), ((length, width), f32), part, part, part, part, ((rows, ATTN * width), f32),
        ((rows, ATTN * width), f32), ((8, LANES), f32), ((1, LANES), f32),
    ]
    vmem, hbm = pl.BlockSpec(memory_space=pltpu.VMEM), pl.BlockSpec(memory_space=pl.ANY)
    scratch = [
        pltpu.VMEM((BLOCKS,) + dims + (rows, width), bf),
        pltpu.VMEM(dims + (16, LANES), bf),
        pltpu.VMEM((16, LANES), f32),
        pltpu.VMEM((8, width), f32),
        pltpu.VMEM((1, ATTN * width), f32),
        pltpu.VMEM((4, length, width), bf),
        pltpu.VMEM((length, LANES), f32),
        pltpu.VMEM((width // HEAD, length), f32),
        pltpu.VMEM((length, length), f32),
        pltpu.VMEM((length, width), bf),
        pltpu.VMEM((ATTN, length, width), bf),
        pltpu.VMEM((ATTN, length, width), bf),
        pltpu.VMEM((length, width), bf),
        pltpu.VMEM((length, width), f32),
        pltpu.VMEM((length, width), bf),
        pltpu.VMEM((width, length), bf),
        pltpu.VMEM((width // HEAD, length), f32),
        pltpu.VMEM((length, width), bf),
        pltpu.VMEM((8, width), f32),
        pltpu.VMEM((16, LANES), f32),
        pltpu.VMEM((2,) + dims + (rows, width), bf),
        pltpu.VMEM((2, rows, width), f32),
        pltpu.SemaphoreType.DMA((BLOCKS + 1, len(GatherBlock.SENDS))),
        pltpu.SemaphoreType.DMA((BLOCKS + 1, len(GATHER_GETS))),
        pltpu.SemaphoreType.DMA((BLOCKS + 2,)),
        pltpu.SemaphoreType.DMA((4,)),
    ]
    scratch += sum_scratch(rows, width, BLOCKS, OWN_BUFFERS) + sum_scratch(16, LANES, 1, SUM_NAMES)
    return pl.pallas_call(
        functools.partial(layer_kernel, depth),
        out_shape=tuple(jax.ShapeDtypeStruct(*s) for s in shapes),
        in_specs=[hbm, vmem, hbm] + [hbm] * 6 + [vmem] * 9,
        out_specs=tuple([hbm] * 8 + [vmem] * 2),
        scratch_shapes=scratch,
        compiler_params=pltpu.CompilerParams(
            collective_id=0, has_side_effects=True, vmem_limit_bytes=63 * 2**20
        ),
        name="layer",
    )(tokens, segment, cotangent, *weights, *vectors)


PIECE = 1024


def results_kernel(large, short, *refs):
    sources, targets, vectors = refs[:large], refs[large + 2 : 2 * large + 2], refs[2 * large + 2 : 2 * large + 11]
    rows, up = refs[large : large + 2]
    held, (came, gone) = refs[2 * large + 11 : -2], refs[-2:]
    ins, outs = [], []
    for src, mid, dst in zip(sources, held, targets):
        for start in range(0, src.shape[0], PIECE):
            at = pl.ds(start, min(PIECE, src.shape[0]))
            i = len(ins)
            ins.append(pltpu.make_async_copy(src.at[at], mid.at[at], came.at[i]))
            outs.append(pltpu.make_async_copy(mid.at[at], dst.at[at], gone.at[i]))
    for copy in ins:
        copy.start()
    for i in range(8):
        vectors[i][...] = rows[i : i + 1, 0:short]
    vectors[8][...] = up[...]
    for copy, onward in zip(ins, outs):
        copy.wait()
        onward.start()
    for copy in outs:
        copy.wait()


def results_call(large, rows, up, short):
    vmem, hbm = pl.BlockSpec(memory_space=pltpu.VMEM), pl.BlockSpec(memory_space=pl.ANY)
    shapes = [jax.ShapeDtypeStruct(a.shape, a.dtype) for a in large]
    shapes += [jax.ShapeDtypeStruct((1, short), jnp.float32)] * 8 + [jax.ShapeDtypeStruct(up.shape, jnp.float32)]
    return pl.pallas_call(
        functools.partial(results_kernel, len(large), short),
        out_shape=tuple(shapes),
        in_specs=[hbm] * len(large) + [vmem] * 2,
        out_specs=tuple([hbm] * len(large) + [vmem] * 9),
        scratch_shapes=[pltpu.VMEM(a.shape, a.dtype) for a in large]
        + [pltpu.SemaphoreType.DMA((sum(-(-a.shape[0] // PIECE) for a in large),))] * 2,
        name="results",
    )(*large, rows, up)


def kernel_device(
    tokens, segment, cotangent, query_w, key_w, value_w, attn_out_w, up_w, down_w, query_bias, value_bias,
    attn_out_bias, up_bias, down_bias, norm1_gain, norm1_shift, norm2_gain, norm2_shift,
):
    depth = lax.axis_size(DP) // 2
    weights = (query_w, key_w, value_w, attn_out_w, up_w, jnp.transpose(down_w))
    vectors = (
        query_bias, value_bias, attn_out_bias, down_bias, norm1_gain, norm1_shift, norm2_gain, norm2_shift, up_bias,
    )
    outputs, d_tokens, qw, kw, vw, ow, uw, dw, short_sum, up_sum = layer_call(
        depth, tokens, segment, cotangent, weights, [vector[None] for vector in vectors]
    )
    outputs, d_tokens, qw, kw, vw, ow, uw, dw, *vectors = results_call(
        (outputs, d_tokens, qw, kw, vw, ow, uw, dw), short_sum, up_sum, query_w.shape[0]
    )
    qb, vb, ob, db, g1, s1, g2, s2, ub = [vector.reshape(-1) for vector in vectors]
    return (
        outputs, d_tokens, qw, kw, vw, ow, uw, jnp.transpose(dw), qb, vb, ob, ub, db, g1, s1, g2, s2,
    )


def solution(mesh):
    fits = mesh.shape[FSDP] == 4 and mesh.shape[DP] == 8
    body = kernel_device if fits else plain_device
    in_specs = (
        P(BOTH, None),
        P(BOTH, None),
        P(BOTH, None),
        P(BOTH, None),
        P(BOTH, None),
        P(BOTH, None),
        P(BOTH, None),
        P(BOTH, None),
        P(None, BOTH),
        P(BOTH),
        P(BOTH),
        P(BOTH),
        P(BOTH),
        P(BOTH),
        P(BOTH),
        P(BOTH),
        P(BOTH),
        P(BOTH),
    )
    out_specs = (
        P(BOTH, None),
        P(BOTH, None),
        P(BOTH, None),
        P(BOTH, None),
        P(BOTH, None),
        P(BOTH, None),
        P(BOTH, None),
        P(None, BOTH),
        P(BOTH),
        P(BOTH),
        P(BOTH),
        P(BOTH),
        P(BOTH),
        P(BOTH),
        P(BOTH),
        P(BOTH),
        P(BOTH),
    )
    return jax.shard_map(
        body, mesh=mesh, in_specs=in_specs, out_specs=out_specs, check_vma=False
    )
```
